32 devices in a mesh: rep: 4 (over z), exp: 8 (over y, x, core).
Axes of the slice: x: 2, y: 2, z: 4, core: 2. Of those that a mesh axis runs over, the one named last changes fastest.
Arguments:
- tokens: bfloat16 [512, 4096], P(('rep', 'exp')), may hold values from -6 to 6
- routed_experts: int32 [512, 8], P(('rep', 'exp')), may hold values from 0 to 15, all different within a row; in each aligned block of 16 rows (0 to 15, 16 to 31, ...) at most 12 rows name the same one
- route_weights: float32 [512, 8], P(('rep', 'exp')), may hold values from 0.02 to 0.5
- gate_weight: bfloat16 [16, 1536, 4096], P('exp', 'rep'), may hold values from -0.09375 to 0.09375
- up_weight: bfloat16 [16, 1536, 4096], P('exp', 'rep'), may hold values from -0.09375 to 0.09375
- down_weight: bfloat16 [16, 1536, 4096], P('exp', 'rep'), may hold values from -0.15625 to 0.15625
Outputs:
- layer_output: bfloat16 [512, 4096], P(('rep', 'exp'))
The draws below stay inside these ranges and needn't reach their ends.
Inputs may be any that keep to these rules, and one draw needn't show every extreme that they name: `routed_experts`: each token names 8 different experts. Among the 16 tokens of one device (aligned blocks of rows), no expert is named more than 12 times, a bound that some block reaches.
All inputs are finite; a program needn't handle non-finite values.
Results may differ from the reference program's by a relative error of at most 0.01.
Values may be sent and summed in bfloat16 or wider, within the bound.
No kernel may reach another device: no remote copies, remote signals or barrier semaphores. Data moves between devices by JAX's collectives and lax.ppermute only.
A program may use at most 128 MiB of HBM per device.

```python
import math
import jax
import jax.numpy as jnp
import numpy as np
from jax import lax

D = 4096
FF = 1536
TOP = 8
TOK_DEV = 16
EXPERTS = 16
SHARD_FF = 384
CAP = 12
TOKENS = 512
N_REP = 4
N_EXP = 8


def steps_of(stream_key, dims, cuts, least, top_value):
    def one(position, shards_of):
        heights = jax.random.uniform(jax.random.fold_in(jax.random.fold_in(stream_key, 6), position), (shards_of,), jnp.float32, least / len(cuts), top_value / len(cuts))
        return jnp.repeat(jnp.exp(heights), dims[position] // shards_of).reshape((-1,) + (1,) * (len(dims) - position - 1))

    level = one(*cuts[0])
    for cut in cuts[1:]:
        level = level * one(*cut)
    return level


def assign_block(own_key, own, number, rows, number_of, top, most, skew):
    ranking = jax.random.permutation(own_key, number_of)
    heavy_load, ordinary = shares(number_of, rows * top, most, skew, True), shares(number_of, rows * top, most, skew, False)
    places = jnp.arange(number_of)

    def named(sizes, rotation):
        used = int((sizes > 0).sum())
        fixed = max(1, used // 4)
        passed = fixed + (places - fixed + rotation * (used - fixed)) % max(1, number_of - fixed)
        return jnp.zeros((number_of,), jnp.int32).at[ranking[jnp.where(places < fixed, places, passed)]].set(jnp.asarray(sizes, jnp.int32))

    sizes = jnp.where(number % 4 == 0, named(heavy_load, number // 4), named(ordinary, number - number // 4 - 1))
    mixed = jax.random.permutation(jax.random.fold_in(own, 3), number_of)
    giver, sink = mixed[0:number_of // 2 * 2:2], mixed[1:number_of // 2 * 2:2]
    slack = jnp.minimum(sizes[giver] - 1, most - sizes[sink]) // 2
    slack = jnp.where((giver == ranking[0]) | (sink == ranking[0]) | (sizes[sink] == 0), 0, jnp.maximum(slack, 0))
    passed = jax.random.randint(jax.random.fold_in(own, 4), (number_of // 2,), 0, 1 << 20) % (slack + 1)
    sizes = sizes.at[giver].add(-passed).at[sink].add(passed)
    items = jnp.searchsorted(jnp.cumsum(sizes), jnp.arange(rows * top), side="right").astype(jnp.int32)
    grid = items.reshape(top, rows).T
    grid = grid[jax.random.permutation(jax.random.fold_in(own, 1), rows)]
    rotation = jax.random.randint(jax.random.fold_in(own, 2), (rows, 1), 0, top)
    return jnp.take_along_axis(grid, (jnp.arange(top)[None, :] + rotation) % top, axis=1)


def shares(count, total, most, lean, full):
    loads = [(1 << 20) // math.isqrt(standing ** lean) + 1 for standing in range(1, count + 1)]
    largest = most if full else min(most, max(-(-total // count), total * loads[0] // sum(loads)))
    least = 1 if total - largest >= count - 1 else 0
    counts, rest = [largest] + [least] * (count - 1), total - largest - least * (count - 1)
    while rest > 0:
        candidates = [i for i in range(1, count) if counts[i] < largest] or [i for i in range(1, count) if counts[i] < most]
        whole, remaining = sum([loads[i] for i in candidates]), rest
        for i in candidates:
            extra = min(most - counts[i], max(1, remaining * loads[i] // whole), rest)
            counts[i] = counts[i] + extra
            rest = rest - extra
    return np.array(counts)


def normal_values(key, shape, deviation, most, cuts=(), kind=jnp.bfloat16):
    array = jax.random.normal(key, shape, jnp.float32) * deviation
    if len(cuts) > 0:
        array = steps_of(key, shape, cuts, -0.22, 0.18) * array
    return jnp.clip(array, min=-most, max=most).astype(kind)


def setup_inputs(seed: int = 0) -> dict:
    key_of = jax.random.split(jax.random.key(seed), 7)
    tokens = normal_values(key_of[0], (TOKENS, D), 1.0, 6.0, ((0, 32),))
    routed_experts_keys = jax.random.split(jax.random.fold_in(key_of[1], 1), TOKENS // TOK_DEV)
    routed_experts_turns = jax.random.permutation(jax.random.fold_in(key_of[1], 3), TOKENS // TOK_DEV)
    routed_experts = jax.vmap(lambda own, number: assign_block(jax.random.fold_in(key_of[1], 2), own, number, TOK_DEV, EXPERTS, TOP, CAP, 2))(routed_experts_keys, routed_experts_turns).reshape((TOKENS, TOP))
    route_weights = jnp.clip(jnp.exp(math.log(0.5) - 3.218876 * jax.random.uniform(key_of[2], (TOKENS, TOP), jnp.float32) ** steps_of(key_of[2], (TOKENS, TOP), ((0, 32),), -0.2, 0.2)), 0.02, 0.5)
    gate_weight = normal_values(key_of[3], (EXPERTS, FF, D), D ** -0.5, 0.09375, ((0, 8), (1, 4)))
    up_weight = normal_values(key_of[4], (EXPERTS, FF, D), D ** -0.5, 0.09375, ((0, 8), (1, 4)))
    down_weight = normal_values(key_of[5], (EXPERTS, FF, D), FF ** -0.5, 0.15625, ((0, 8), (1, 4)))
    return {"tokens": tokens, "routed_experts": routed_experts, "route_weights": route_weights, "gate_weight": gate_weight, "up_weight": up_weight, "down_weight": down_weight}


def reference(tokens, routed_experts, route_weights, gate_weight, up_weight, down_weight):
    flat_experts = routed_experts.reshape(-1)
    flat_weights = route_weights.reshape(-1)
    slot_limit = CAP * N_REP * N_EXP

    def one_expert(accumulated, expert):
        chosen = flat_experts == expert
        expert_load = jnp.sum(chosen.astype(jnp.int32))
        indices = jnp.nonzero(chosen, size=slot_limit, fill_value=0)[0].astype(jnp.int32)
        filled = jnp.arange(slot_limit, dtype=jnp.int32) < expert_load
        token_index = (indices // TOP).astype(jnp.int32)
        weight = jnp.where(filled, flat_weights[indices], jnp.float32(0.0))
        token_rows = tokens[token_index]
        gate_expert = gate_weight[expert]
        up_expert = up_weight[expert]
        down_expert = down_weight[expert]
        summed = jnp.zeros((slot_limit, D), jnp.float32)
        for hidden_group in range(N_REP):
            first_unit = hidden_group * SHARD_FF
            last_unit = first_unit + SHARD_FF
            gate_value = jnp.dot(token_rows, gate_expert[first_unit:last_unit].T, preferred_element_type=jnp.float32)
            up_value = jnp.dot(token_rows, up_expert[first_unit:last_unit].T, preferred_element_type=jnp.float32)
            hidden = (jax.nn.silu(gate_value) * up_value).astype(jnp.bfloat16)
            group_part = jnp.dot(hidden, down_expert[first_unit:last_unit], preferred_element_type=jnp.float32)
            group_part = lax.optimization_barrier(group_part.astype(jnp.bfloat16))
            summed = summed + group_part.astype(jnp.float32)
        accumulated = accumulated.at[token_index].add(summed * weight[:, None])
        return accumulated, None

    accumulated, _ = lax.scan(one_expert, jnp.zeros((TOKENS, D), jnp.float32), jnp.arange(EXPERTS, dtype=jnp.int32))
    return accumulated.astype(jnp.bfloat16)
```

```python
import jax
import jax.numpy as jnp
from jax import lax
from jax.sharding import PartitionSpec as P


def slot_table(experts, expert_count, capacity):
    blocks = experts.shape[0]
    flattened = experts.reshape(blocks, -1)
    onehot = (
        flattened[:, :, None] == jnp.arange(expert_count, dtype=jnp.int32)[None, None, :]
    ).astype(jnp.int32)
    before = jnp.cumsum(onehot, axis=1) - onehot
    position = jnp.sum(before * onehot, axis=2)
    return flattened * capacity + position


def token_picks(slots, top_count, slot_count):
    blocks = slots.shape[0]
    grouped = slots.reshape(blocks, 1, -1, top_count)
    return jnp.any(grouped == jnp.arange(slot_count, dtype=jnp.int32)[None, :, None, None], axis=3)


def routing_column(route_weights, routed_experts):
    as_float = routed_experts.astype(jnp.float32)
    weights_all, experts_all = (
        lax.all_gather(route_weights, "rep", axis=0, tiled=True),
        lax.all_gather(as_float, "rep", axis=0, tiled=True),
    )
    return (weights_all, experts_all.astype(jnp.int32))


def on_device_slots(tokens, routed_experts, route_weights, gate_weight, up_weight, down_weight):
    replicas = lax.axis_size("rep")
    owners = lax.axis_size("exp")
    token_rows, model_width = tokens.shape
    top_count = routed_experts.shape[1]
    local_experts = gate_weight.shape[0]
    expert_count = local_experts * owners
    capacity = max(2, 3 * token_rows * top_count // (2 * expert_count))
    slot_count = expert_count * capacity
    own_slots = slot_table(routed_experts[None], expert_count, capacity)
    column = None
    column_slots = None
    selected = token_picks(own_slots, top_count, slot_count)[0].astype(jnp.bfloat16)
    buffer = jnp.dot(selected, tokens, preferred_element_type=jnp.float32).astype(jnp.bfloat16)
    buffer = buffer.reshape(owners, local_experts, capacity, model_width)
    arrived = lax.all_to_all(buffer, "exp", split_axis=0, concat_axis=2, tiled=True)
    rows_now = lax.all_gather(arrived, "rep", axis=2, tiled=True)[0]
    gate_value = jnp.einsum(
        "emd,efd->emf", rows_now, gate_weight, preferred_element_type=jnp.float32
    )
    up_value = jnp.einsum("emd,efd->emf", rows_now, up_weight, preferred_element_type=jnp.float32)
    hidden = (jax.nn.silu(gate_value) * up_value).astype(jnp.bfloat16)
    outcome = jnp.einsum("emf,efd->emd", hidden, down_weight, preferred_element_type=jnp.float32)
    outcome = lax.optimization_barrier(outcome.astype(jnp.bfloat16))
    outcomes = outcome[None]
    outcomes = outcomes.reshape(local_experts, replicas, owners, capacity, model_width)
    column = routing_column(route_weights, routed_experts)
    column_slots = slot_table(
        column[1].reshape(replicas, token_rows, top_count), expert_count, capacity
    )
    returned = lax.all_to_all(outcomes, "exp", split_axis=2, concat_axis=0, tiled=True)
    returned = returned.reshape(expert_count, replicas, capacity, model_width)
    expert_index = column_slots // capacity
    place_index = column_slots % capacity
    replica_index = jnp.broadcast_to(
        jnp.arange(replicas, dtype=jnp.int32)[:, None], column_slots.shape
    )
    picked = returned[expert_index, replica_index, place_index].astype(jnp.float32)
    column_weights = column[0].reshape(replicas, token_rows, top_count)
    weighted = jnp.sum(
        picked.reshape(replicas, token_rows, top_count, model_width)
        * column_weights[:, :, :, None],
        axis=2,
    )
    summed = lax.psum_scatter(weighted, "rep", scatter_dimension=0, tiled=True)
    return summed.reshape(token_rows, model_width).astype(jnp.bfloat16)


def swap_exp(value, bit):
    owners = lax.axis_size("exp")
    return lax.ppermute(value, "exp", [(i, i ^ bit) for i in range(owners)])


def turn_rep(value, shift):
    replicas = lax.axis_size("rep")
    return lax.ppermute(value, "rep", [(i, (i - shift) % replicas) for i in range(replicas)])


def add(left, right):
    return (left.astype(jnp.float32) + right.astype(jnp.float32)).astype(jnp.bfloat16)


def on_device_dense(tokens, routed_experts, route_weights, gate_weight, up_weight, down_weight):
    replicas = lax.axis_size("rep")
    token_rows, model_width = tokens.shape
    local_experts, shard_units, _ = gate_weight.shape
    half = replicas // 2
    high = route_weights.astype(jnp.bfloat16)
    low = (route_weights - high.astype(jnp.float32)).astype(jnp.bfloat16)
    extra = jnp.concatenate([routed_experts.astype(jnp.bfloat16), high, low], axis=1)
    extra = jnp.pad(extra, ((0, 0), (0, 128 - extra.shape[1])))
    packed = jnp.concatenate([tokens, extra], axis=1)

    blocks = [packed] + [turn_rep(packed, s) for s in range(1, replicas)]
    first = jnp.concatenate(blocks[:half], axis=0)
    second = jnp.concatenate(blocks[half:], axis=0)
    first = jnp.concatenate([first, swap_exp(first, 2)], axis=0)
    second = jnp.concatenate([second, swap_exp(second, 4)], axis=0)
    plane = jnp.concatenate([first, swap_exp(first, 4), second, swap_exp(second, 2)], axis=0)
    rows = jnp.concatenate([plane, swap_exp(plane, 1)], axis=0)

    own_first = lax.axis_index("exp") * local_experts
    top = routed_experts.shape[1]
    names = rows[:, model_width : model_width + top].astype(jnp.int32)
    scale = rows[:, model_width + top : model_width + 2 * top].astype(jnp.float32) + rows[
        :, model_width + 2 * top : model_width + 3 * top
    ].astype(jnp.float32)
    local = own_first + jnp.arange(local_experts, dtype=jnp.int32)
    weight = jnp.sum(
        jnp.where(names[:, None, :] == local[None, :, None], scale[:, None, :], 0.0), axis=2
    )
    activations = rows[:, :model_width]
    gates = gate_weight.reshape(local_experts * shard_units, model_width)
    ups = up_weight.reshape(local_experts * shard_units, model_width)
    downs = down_weight.reshape(local_experts * shard_units, model_width)
    gate_value = jnp.einsum("md,fd->mf", activations, gates, preferred_element_type=jnp.float32)
    up_value = jnp.einsum("md,fd->mf", activations, ups, preferred_element_type=jnp.float32)
    unit_weight = jnp.repeat(weight, shard_units, axis=1)
    hidden = (jax.nn.silu(gate_value) * up_value * unit_weight).astype(jnp.bfloat16)
    partial = jnp.dot(hidden, downs, preferred_element_type=jnp.float32).astype(jnp.bfloat16)

    size = partial.shape[0] // 2
    plane = add(partial[:size], swap_exp(partial[size:], 1))
    size = size // 2
    first, second = plane[:size], plane[size:]
    size = size // 2
    first, second = (
        add(first[:size], swap_exp(first[size:], 4)),
        add(second[:size], swap_exp(second[size:], 2)),
    )
    size = size // 2
    first, second = (
        add(first[:size], swap_exp(first[size:], 2)),
        add(second[:size], swap_exp(second[size:], 4)),
    )
    column = jnp.concatenate([first, second], axis=0).reshape(replicas, token_rows, model_width)
    total = column[0].astype(jnp.float32)
    for s in range(1, replicas):
        total = total + turn_rep(column[s], -s).astype(jnp.float32)
    return total.astype(jnp.bfloat16)


def solution(mesh):
    placed = (
        P(("rep", "exp"), None),
        P(("rep", "exp"), None),
        P(("rep", "exp"), None),
        P("exp", "rep", None),
        P("exp", "rep", None),
        P("exp", "rep", None),
    )
    plane = mesh.shape["exp"] == 8
    return jax.shard_map(
        on_device_dense if plane else on_device_slots,
        mesh=mesh,
        in_specs=placed,
        out_specs=P(("rep", "exp"), None),
        check_vma=False,
    )
```

```python
import functools

import jax
import jax.numpy as jnp
from jax import lax
from jax.experimental import pallas as pl
from jax.experimental.pallas import tpu as pltpu
from jax.sharding import PartitionSpec as P


def slot_table(experts, expert_count, capacity):
    blocks = experts.shape[0]
    flattened = experts.reshape(blocks, -1)
    onehot = (
        flattened[:, :, None] == jnp.arange(expert_count, dtype=jnp.int32)[None, None, :]
    ).astype(jnp.int32)
    before = jnp.cumsum(onehot, axis=1) - onehot
    position = jnp.sum(before * onehot, axis=2)
    return flattened * capacity + position


def token_picks(slots, top_count, slot_count):
    blocks = slots.shape[0]
    grouped = slots.reshape(blocks, 1, -1, top_count)
    return jnp.any(grouped == jnp.arange(slot_count, dtype=jnp.int32)[None, :, None, None], axis=3)


def routing_column(route_weights, routed_experts):
    as_float = routed_experts.astype(jnp.float32)
    weights_all, experts_all = (
        lax.all_gather(route_weights, "rep", axis=0, tiled=True),
        lax.all_gather(as_float, "rep", axis=0, tiled=True),
    )
    return (weights_all, experts_all.astype(jnp.int32))


def on_device_slots(tokens, routed_experts, route_weights, gate_weight, up_weight, down_weight):
    replicas = lax.axis_size("rep")
    owners = lax.axis_size("exp")
    token_rows, model_width = tokens.shape
    top_count = routed_experts.shape[1]
    local_experts = gate_weight.shape[0]
    expert_count = local_experts * owners
    capacity = max(2, 3 * token_rows * top_count // (2 * expert_count))
    slot_count = expert_count * capacity
    own_slots = slot_table(routed_experts[None], expert_count, capacity)
    column = None
    column_slots = None
    selected = token_picks(own_slots, top_count, slot_count)[0].astype(jnp.bfloat16)
    buffer = jnp.dot(selected, tokens, preferred_element_type=jnp.float32).astype(jnp.bfloat16)
    buffer = buffer.reshape(owners, local_experts, capacity, model_width)
    arrived = lax.all_to_all(buffer, "exp", split_axis=0, concat_axis=2, tiled=True)
    rows_now = lax.all_gather(arrived, "rep", axis=2, tiled=True)[0]
    gate_value = jnp.einsum(
        "emd,efd->emf", rows_now, gate_weight, preferred_element_type=jnp.float32
    )
    up_value = jnp.einsum("emd,efd->emf", rows_now, up_weight, preferred_element_type=jnp.float32)
    hidden = (jax.nn.silu(gate_value) * up_value).astype(jnp.bfloat16)
    outcome = jnp.einsum("emf,efd->emd", hidden, down_weight, preferred_element_type=jnp.float32)
    outcome = lax.optimization_barrier(outcome.astype(jnp.bfloat16))
    outcomes = outcome[None]
    outcomes = outcomes.reshape(local_experts, replicas, owners, capacity, model_width)
    column = routing_column(route_weights, routed_experts)
    column_slots = slot_table(
        column[1].reshape(replicas, token_rows, top_count), expert_count, capacity
    )
    returned = lax.all_to_all(outcomes, "exp", split_axis=2, concat_axis=0, tiled=True)
    returned = returned.reshape(expert_count, replicas, capacity, model_width)
    expert_index = column_slots // capacity
    place_index = column_slots % capacity
    replica_index = jnp.broadcast_to(
        jnp.arange(replicas, dtype=jnp.int32)[:, None], column_slots.shape
    )
    picked = returned[expert_index, replica_index, place_index].astype(jnp.float32)
    column_weights = column[0].reshape(replicas, token_rows, top_count)
    weighted = jnp.sum(
        picked.reshape(replicas, token_rows, top_count, model_width)
        * column_weights[:, :, :, None],
        axis=2,
    )
    summed = lax.psum_scatter(weighted, "rep", scatter_dimension=0, tiled=True)
    return summed.reshape(token_rows, model_width).astype(jnp.bfloat16)


def expert_kernel(pieces_in, pieces_out, local_experts, shard_units, model_width, top, block, *refs):
    own_ref, refs = refs[0], refs[1:]
    ins, refs = refs[: len(pieces_in)], refs[len(pieces_in) :]
    (gate_hbm, up_hbm, down_hbm), refs = refs[:3], refs[3:]
    outs, refs = refs[: len(pieces_out)], refs[len(pieces_out) :]
    rows, gates, ups, downs, hidden, result, row_sem, gate_sem, up_sem, down_sem, out_sem = refs
    units = local_experts * shard_units
    unit_block = gates.shape[1]
    unit_blocks = units // unit_block
    column_blocks = model_width // block

    row_copies, start = [], 0
    for place, count in enumerate(pieces_in):
        row_copies.append(
            pltpu.make_async_copy(ins[place], rows.at[pl.ds(start, count)], row_sem.at[place])
        )
        start += count

    def weight_copies(step):
        span = pl.ds(step * unit_block, unit_block)
        return (
            pltpu.make_async_copy(gate_hbm.at[span], gates.at[step], gate_sem.at[step]),
            pltpu.make_async_copy(up_hbm.at[span], ups.at[step], up_sem.at[step]),
        )

    for copy in row_copies:
        copy.start()
    for step in range(unit_blocks):
        for copy in weight_copies(step):
            copy.start()
    down_copy = pltpu.make_async_copy(down_hbm, downs, down_sem)
    down_copy.start()
    for copy in row_copies:
        copy.wait()

    extra = rows[:, model_width:].astype(jnp.float32)
    width = extra.shape[1]
    scale = pltpu.roll(extra, width - top, 1) + pltpu.roll(extra, width - 2 * top, 1)
    lane = lax.broadcasted_iota(jnp.int32, extra.shape, 1)
    weights = []
    for expert in range(local_experts):
        name = (own_ref[0] + expert).astype(jnp.float32)
        chosen = jnp.logical_and(lane < top, extra == name)
        weights.append(jnp.sum(jnp.where(chosen, scale, 0.0), axis=1, keepdims=True))

    def unit_step(step, carry):
        for copy in weight_copies(step):
            copy.wait()
        values = rows[:, :model_width]
        contract = (((1,), (1,)), ((), ()))
        gate = lax.dot_general(values, gates[step], contract, preferred_element_type=jnp.float32)
        up = lax.dot_general(values, ups[step], contract, preferred_element_type=jnp.float32)
        unit = step * unit_block + lax.broadcasted_iota(jnp.int32, gate.shape, 1)
        weight = weights[0]
        for expert in range(1, local_experts):
            weight = jnp.where(unit >= expert * shard_units, weights[expert], weight)
        active = gate / (1.0 + jnp.exp(-gate)) * up * weight
        hidden[step] = active.astype(jnp.bfloat16)
        return carry

    lax.fori_loop(0, unit_blocks, unit_step, 0)
    down_copy.wait()
    active = jnp.concatenate([hidden[step] for step in range(unit_blocks)], axis=1)

    def out_copies(step):
        span = pl.ds(pl.multiple_of(step * block, block), block)
        copies, begin = [], 0
        for place, count in enumerate(pieces_out):
            copies.append(
                pltpu.make_async_copy(
                    result.at[pl.ds(begin, count), span], outs[place].at[:, span], out_sem.at[step, place]
                )
            )
            begin += count
        return copies

    def column_step(step, carry):
        span = pl.ds(pl.multiple_of(step * block, block), block)
        value = jnp.dot(active, downs[:, span], preferred_element_type=jnp.float32)
        result[:, span] = value.astype(jnp.bfloat16)
        for copy in out_copies(step):
            copy.start()
        return carry

    def finish_step(step, carry):
        for copy in out_copies(step):
            copy.wait()
        return carry

    lax.fori_loop(0, column_blocks, column_step, 0)
    lax.fori_loop(0, column_blocks, finish_step, 0)


def experts_of(pieces, out_rows, gate_weight, up_weight, down_weight, top):
    local_experts, shard_units, model_width = gate_weight.shape
    units = local_experts * shard_units
    unit_block = 256 if units % 256 == 0 else 128
    block = 512
    pieces_in = [piece.shape[0] for piece in pieces]
    total = sum(pieces_in)
    packed = pieces[0].shape[1]
    own = jnp.full((1,), lax.axis_index("exp") * local_experts, jnp.int32)
    anywhere = pl.BlockSpec(memory_space=pl.ANY)
    kernel = functools.partial(
        expert_kernel, pieces_in, out_rows, local_experts, shard_units, model_width, top, block
    )
    return pl.pallas_call(
        kernel,
        out_shape=[jax.ShapeDtypeStruct((count, model_width), jnp.bfloat16) for count in out_rows],
        in_specs=[pl.BlockSpec(memory_space=pltpu.SMEM)] + [anywhere] * (len(pieces) + 3),
        out_specs=[anywhere] * len(out_rows),
        scratch_shapes=[
            pltpu.VMEM((total, packed), jnp.bfloat16),
            pltpu.VMEM((units // unit_block, unit_block, model_width), jnp.bfloat16),
            pltpu.VMEM((units // unit_block, unit_block, model_width), jnp.bfloat16),
            pltpu.VMEM((units, model_width), jnp.bfloat16),
            pltpu.VMEM((units // unit_block, total, unit_block), jnp.bfloat16),
            pltpu.VMEM((total, model_width), jnp.bfloat16),
            pltpu.SemaphoreType.DMA((len(pieces),)),
            pltpu.SemaphoreType.DMA((units // unit_block,)),
            pltpu.SemaphoreType.DMA((units // unit_block,)),
            pltpu.SemaphoreType.DMA,
            pltpu.SemaphoreType.DMA((model_width // block, len(out_rows))),
        ],
        compiler_params=pltpu.CompilerParams(vmem_limit_bytes=48 * 1024 * 1024),
        cost_estimate=pl.CostEstimate(
            flops=6 * total * units * model_width,
            bytes_accessed=6 * units * model_width + 4 * total * model_width,
            transcendentals=total * units,
        ),
        name="experts",
    )(
        own,
        *pieces,
        gate_weight.reshape(units, model_width),
        up_weight.reshape(units, model_width),
        down_weight.reshape(units, model_width),
    )


def with_routing(tokens, routed_experts, route_weights):
    high = route_weights.astype(jnp.bfloat16)
    low = (route_weights - high.astype(jnp.float32)).astype(jnp.bfloat16)
    extra = jnp.concatenate([routed_experts.astype(jnp.bfloat16), high, low], axis=1)
    extra = jnp.pad(extra, ((0, 0), (0, 128 - extra.shape[1])))
    return jnp.concatenate([tokens, extra], axis=1)


def on_device_dense(tokens, routed_experts, route_weights, gate_weight, up_weight, down_weight):
    top = routed_experts.shape[1]
    packed = with_routing(tokens, routed_experts, route_weights)
    rows = lax.all_gather(packed, ("rep", "exp"), axis=0, tiled=True)
    partial = experts_of([rows], [rows.shape[0]], gate_weight, up_weight, down_weight, top)[0]
    return lax.psum_scatter(partial, ("rep", "exp"), scatter_dimension=0, tiled=True)


def solution(mesh):
    placed = (
        P(("rep", "exp"), None),
        P(("rep", "exp"), None),
        P(("rep", "exp"), None),
        P("exp", "rep", None),
        P("exp", "rep", None),
        P("exp", "rep", None),
    )
    plane = mesh.shape["exp"] == 8 and mesh.shape["rep"] == 4
    return jax.shard_map(
        on_device_dense if plane else on_device_slots,
        mesh=mesh,
        in_specs=placed,
        out_specs=P(("rep", "exp"), None),
        check_vma=False,
    )
```

```python
import functools

import jax
import jax.numpy as jnp
from jax import lax
from jax.experimental import pallas as pl
from jax.experimental.pallas import tpu as pltpu
from jax.sharding import PartitionSpec as P


def slot_table(experts, expert_count, capacity):
    blocks = experts.shape[0]
    flattened = experts.reshape(blocks, -1)
    onehot = (
        flattened[:, :, None] == jnp.arange(expert_count, dtype=jnp.int32)[None, None, :]
    ).astype(jnp.int32)
    before = jnp.cumsum(onehot, axis=1) - onehot
    position = jnp.sum(before * onehot, axis=2)
    return flattened * capacity + position


def token_picks(slots, top_count, slot_count):
    blocks = slots.shape[0]
    grouped = slots.reshape(blocks, 1, -1, top_count)
    return jnp.any(grouped == jnp.arange(slot_count, dtype=jnp.int32)[None, :, None, None], axis=3)


def routing_column(route_weights, routed_experts):
    as_float = routed_experts.astype(jnp.float32)
    weights_all, experts_all = (
        lax.all_gather(route_weights, "rep", axis=0, tiled=True),
        lax.all_gather(as_float, "rep", axis=0, tiled=True),
    )
    return (weights_all, experts_all.astype(jnp.int32))


def on_device_slots(tokens, routed_experts, route_weights, gate_weight, up_weight, down_weight):
    replicas = lax.axis_size("rep")
    owners = lax.axis_size("exp")
    token_rows, model_width = tokens.shape
    top_count = routed_experts.shape[1]
    local_experts = gate_weight.shape[0]
    expert_count = local_experts * owners
    capacity = max(2, 3 * token_rows * top_count // (2 * expert_count))
    slot_count = expert_count * capacity
    own_slots = slot_table(routed_experts[None], expert_count, capacity)
    column = None
    column_slots = None
    selected = token_picks(own_slots, top_count, slot_count)[0].astype(jnp.bfloat16)
    buffer = jnp.dot(selected, tokens, preferred_element_type=jnp.float32).astype(jnp.bfloat16)
    buffer = buffer.reshape(owners, local_experts, capacity, model_width)
    arrived = lax.all_to_all(buffer, "exp", split_axis=0, concat_axis=2, tiled=True)
    rows_now = lax.all_gather(arrived, "rep", axis=2, tiled=True)[0]
    gate_value = jnp.einsum(
        "emd,efd->emf", rows_now, gate_weight, preferred_element_type=jnp.float32
    )
    up_value = jnp.einsum("emd,efd->emf", rows_now, up_weight, preferred_element_type=jnp.float32)
    hidden = (jax.nn.silu(gate_value) * up_value).astype(jnp.bfloat16)
    outcome = jnp.einsum("emf,efd->emd", hidden, down_weight, preferred_element_type=jnp.float32)
    outcome = lax.optimization_barrier(outcome.astype(jnp.bfloat16))
    outcomes = outcome[None]
    outcomes = outcomes.reshape(local_experts, replicas, owners, capacity, model_width)
    column = routing_column(route_weights, routed_experts)
    column_slots = slot_table(
        column[1].reshape(replicas, token_rows, top_count), expert_count, capacity
    )
    returned = lax.all_to_all(outcomes, "exp", split_axis=2, concat_axis=0, tiled=True)
    returned = returned.reshape(expert_count, replicas, capacity, model_width)
    expert_index = column_slots // capacity
    place_index = column_slots % capacity
    replica_index = jnp.broadcast_to(
        jnp.arange(replicas, dtype=jnp.int32)[:, None], column_slots.shape
    )
    picked = returned[expert_index, replica_index, place_index].astype(jnp.float32)
    column_weights = column[0].reshape(replicas, token_rows, top_count)
    weighted = jnp.sum(
        picked.reshape(replicas, token_rows, top_count, model_width)
        * column_weights[:, :, :, None],
        axis=2,
    )
    summed = lax.psum_scatter(weighted, "rep", scatter_dimension=0, tiled=True)
    return summed.reshape(token_rows, model_width).astype(jnp.bfloat16)


def expert_kernel(pieces_in, pieces_out, local_experts, shard_units, model_width, top, block, *refs):
    own_ref, refs = refs[0], refs[1:]
    ins, refs = refs[: len(pieces_in)], refs[len(pieces_in) :]
    (gate_hbm, up_hbm, down_hbm), refs = refs[:3], refs[3:]
    outs, refs = refs[: len(pieces_out)], refs[len(pieces_out) :]
    rows, gates, ups, downs, hidden, result, row_sem, gate_sem, up_sem, down_sem, out_sem = refs
    units = local_experts * shard_units
    unit_block = gates.shape[1]
    unit_blocks = units // unit_block
    column_blocks = model_width // block

    row_copies, start = [], 0
    for place, count in enumerate(pieces_in):
        row_copies.append(
            pltpu.make_async_copy(ins[place], rows.at[pl.ds(start, count)], row_sem.at[place])
        )
        start += count

    def weight_copies(step):
        span = pl.ds(step * unit_block, unit_block)
        return (
            pltpu.make_async_copy(gate_hbm.at[span], gates.at[step], gate_sem.at[step]),
            pltpu.make_async_copy(up_hbm.at[span], ups.at[step], up_sem.at[step]),
        )

    for copy in row_copies:
        copy.start()
    for copy in weight_copies(0):
        copy.start()
    for copy in row_copies:
        copy.wait()
    for step in range(1, unit_blocks):
        for copy in weight_copies(step):
            copy.start()
    down_copy = pltpu.make_async_copy(down_hbm, downs, down_sem)
    down_copy.start()

    extra = rows[:, model_width:].astype(jnp.float32)
    width = extra.shape[1]
    scale = pltpu.roll(extra, width - top, 1) + pltpu.roll(extra, width - 2 * top, 1)
    lane = lax.broadcasted_iota(jnp.int32, extra.shape, 1)
    weights = []
    for expert in range(local_experts):
        name = (own_ref[0] + expert).astype(jnp.float32)
        chosen = jnp.logical_and(lane < top, extra == name)
        weights.append(jnp.sum(jnp.where(chosen, scale, 0.0), axis=1, keepdims=True))

    def unit_step(step, carry):
        for copy in weight_copies(step):
            copy.wait()
        values = rows[:, :model_width]
        contract = (((1,), (1,)), ((), ()))
        gate = lax.dot_general(values, gates[step], contract, preferred_element_type=jnp.float32)
        up = lax.dot_general(values, ups[step], contract, preferred_element_type=jnp.float32)
        unit = step * unit_block + lax.broadcasted_iota(jnp.int32, gate.shape, 1)
        weight = weights[0]
        for expert in range(1, local_experts):
            weight = jnp.where(unit >= expert * shard_units, weights[expert], weight)
        active = gate / (1.0 + jnp.exp(-gate)) * up * weight
        hidden[step] = active.astype(jnp.bfloat16)
        return carry

    lax.fori_loop(0, unit_blocks, unit_step, 0)
    down_copy.wait()
    active = jnp.concatenate([hidden[step] for step in range(unit_blocks)], axis=1)

    def out_copies(step):
        span = pl.ds(pl.multiple_of(step * block, block), block)
        copies, begin = [], 0
        for place, count in enumerate(pieces_out):
            copies.append(
                pltpu.make_async_copy(
                    result.at[pl.ds(begin, count), span], outs[place].at[:, span], out_sem.at[step, place]
                )
            )
            begin += count
        return copies

    def column_step(step, carry):
        span = pl.ds(pl.multiple_of(step * block, block), block)
        value = jnp.dot(active, downs[:, span], preferred_element_type=jnp.float32)
        result[:, span] = value.astype(jnp.bfloat16)
        for copy in out_copies(step):
            copy.start()
        return carry

    def finish_step(step, carry):
        for copy in out_copies(step):
            copy.wait()
        return carry

    lax.fori_loop(0, column_blocks, column_step, 0)
    lax.fori_loop(0, column_blocks, finish_step, 0)


def experts_of(pieces, out_rows, gate_weight, up_weight, down_weight, top):
    local_experts, shard_units, model_width = gate_weight.shape
    units = local_experts * shard_units
    unit_block = 256 if units % 256 == 0 else 128
    block = 512
    pieces_in = [piece.shape[0] for piece in pieces]
    total = sum(pieces_in)
    packed = pieces[0].shape[1]
    own = jnp.full((1,), lax.axis_index("exp") * local_experts, jnp.int32)
    anywhere = pl.BlockSpec(memory_space=pl.ANY)
    kernel = functools.partial(
        expert_kernel, pieces_in, out_rows, local_experts, shard_units, model_width, top, block
    )
    return pl.pallas_call(
        kernel,
        out_shape=[jax.ShapeDtypeStruct((count, model_width), jnp.bfloat16) for count in out_rows],
        in_specs=[pl.BlockSpec(memory_space=pltpu.SMEM)] + [anywhere] * (len(pieces) + 3),
        out_specs=[anywhere] * len(out_rows),
        scratch_shapes=[
            pltpu.VMEM((total, packed), jnp.bfloat16),
            pltpu.VMEM((units // unit_block, unit_block, model_width), jnp.bfloat16),
            pltpu.VMEM((units // unit_block, unit_block, model_width), jnp.bfloat16),
            pltpu.VMEM((units, model_width), jnp.bfloat16),
            pltpu.VMEM((units // unit_block, total, unit_block), jnp.bfloat16),
            pltpu.VMEM((total, model_width), jnp.bfloat16),
            pltpu.SemaphoreType.DMA((len(pieces),)),
            pltpu.SemaphoreType.DMA((units // unit_block,)),
            pltpu.SemaphoreType.DMA((units // unit_block,)),
            pltpu.SemaphoreType.DMA,
            pltpu.SemaphoreType.DMA((model_width // block, len(out_rows))),
        ],
        compiler_params=pltpu.CompilerParams(vmem_limit_bytes=48 * 1024 * 1024),
        cost_estimate=pl.CostEstimate(
            flops=6 * total * units * model_width,
            bytes_accessed=6 * units * model_width + 4 * total * model_width,
            transcendentals=total * units,
        ),
        name="experts",
    )(
        own,
        *pieces,
        gate_weight.reshape(units, model_width),
        up_weight.reshape(units, model_width),
        down_weight.reshape(units, model_width),
    )


def swap_exp(value, bit):
    owners = lax.axis_size("exp")
    return lax.ppermute(value, "exp", [(i, i ^ bit) for i in range(owners)])


def turn_rep(value, shift):
    replicas = lax.axis_size("rep")
    return lax.ppermute(value, "rep", [(i, (i - shift) % replicas) for i in range(replicas)])


def add(left, right):
    return (left.astype(jnp.float32) + right.astype(jnp.float32)).astype(jnp.bfloat16)


def with_routing(tokens, routed_experts, route_weights):
    high = route_weights.astype(jnp.bfloat16)
    low = (route_weights - high.astype(jnp.float32)).astype(jnp.bfloat16)
    extra = jnp.concatenate([routed_experts.astype(jnp.bfloat16), high, low], axis=1)
    extra = jnp.pad(extra, ((0, 0), (0, 128 - extra.shape[1])))
    return jnp.concatenate([tokens, extra], axis=1)


def on_device_dense(tokens, routed_experts, route_weights, gate_weight, up_weight, down_weight):
    replicas = lax.axis_size("rep")
    token_rows = tokens.shape[0]
    half = replicas // 2
    top = routed_experts.shape[1]
    packed = with_routing(tokens, routed_experts, route_weights)
    blocks = [packed] + [turn_rep(packed, s) for s in range(1, replicas)]
    first = jnp.concatenate(blocks[:half], axis=0)
    second = jnp.concatenate(blocks[half:], axis=0)
    first = jnp.concatenate([first, swap_exp(first, 2)], axis=0)
    second = jnp.concatenate([second, swap_exp(second, 4)], axis=0)
    planes = [first, swap_exp(first, 4), second, swap_exp(second, 2)]
    planes = planes + [swap_exp(plane, 1) for plane in planes]

    cuts = [plane.shape[0] for plane in planes]
    parts = experts_of(planes, cuts, gate_weight, up_weight, down_weight, top)
    returned = [swap_exp(part, 1) for part in parts[4:]]
    first_away, second_away = add(parts[1], returned[1]), add(parts[3], returned[3])
    first_back, second_back = swap_exp(first_away, 4), swap_exp(second_away, 2)
    first = add(add(parts[0], returned[0]), first_back)
    second = add(add(parts[2], returned[2]), second_back)
    size = first.shape[0] // 2
    first_back, second_back = swap_exp(first[size:], 2), swap_exp(second[size:], 4)
    first, second = add(first[:size], first_back), add(second[:size], second_back)
    column = [*jnp.split(first, half, axis=0), *jnp.split(second, replicas - half, axis=0)]
    arrived = [turn_rep(column[s], -s) for s in range(1, replicas)]
    total = column[0].astype(jnp.float32)
    for part in arrived:
        total = total + part.astype(jnp.float32)
    return total.astype(jnp.bfloat16)


def solution(mesh):
    placed = (
        P(("rep", "exp"), None),
        P(("rep", "exp"), None),
        P(("rep", "exp"), None),
        P("exp", "rep", None),
        P("exp", "rep", None),
        P("exp", "rep", None),
    )
    plane = mesh.shape["exp"] == 8 and mesh.shape["rep"] == 4
    return jax.shard_map(
        on_device_dense if plane else on_device_slots,
        mesh=mesh,
        in_specs=placed,
        out_specs=P(("rep", "exp"), None),
        check_vma=False,
    )
```

```python
import functools

import jax
import jax.numpy as jnp
from jax import lax
from jax.experimental import pallas as pl
from jax.experimental.pallas import tpu as pltpu
from jax.sharding import PartitionSpec as P


def slot_table(experts, expert_count, capacity):
    blocks = experts.shape[0]
    flattened = experts.reshape(blocks, -1)
    onehot = (
        flattened[:, :, None] == jnp.arange(expert_count, dtype=jnp.int32)[None, None, :]
    ).astype(jnp.int32)
    before = jnp.cumsum(onehot, axis=1) - onehot
    position = jnp.sum(before * onehot, axis=2)
    return flattened * capacity + position


def token_picks(slots, top_count, slot_count):
    blocks = slots.shape[0]
    grouped = slots.reshape(blocks, 1, -1, top_count)
    return jnp.any(grouped == jnp.arange(slot_count, dtype=jnp.int32)[None, :, None, None], axis=3)


def routing_column(route_weights, routed_experts):
    as_float = routed_experts.astype(jnp.float32)
    weights_all, experts_all = (
        lax.all_gather(route_weights, "rep", axis=0, tiled=True),
        lax.all_gather(as_float, "rep", axis=0, tiled=True),
    )
    return (weights_all, experts_all.astype(jnp.int32))


def on_device_slots(tokens, routed_experts, route_weights, gate_weight, up_weight, down_weight):
    replicas = lax.axis_size("rep")
    owners = lax.axis_size("exp")
    token_rows, model_width = tokens.shape
    top_count = routed_experts.shape[1]
    local_experts = gate_weight.shape[0]
    expert_count = local_experts * owners
    capacity = max(2, 3 * token_rows * top_count // (2 * expert_count))
    slot_count = expert_count * capacity
    own_slots = slot_table(routed_experts[None], expert_count, capacity)
    column = None
    column_slots = None
    selected = token_picks(own_slots, top_count, slot_count)[0].astype(jnp.bfloat16)
    buffer = jnp.dot(selected, tokens, preferred_element_type=jnp.float32).astype(jnp.bfloat16)
    buffer = buffer.reshape(owners, local_experts, capacity, model_width)
    arrived = lax.all_to_all(buffer, "exp", split_axis=0, concat_axis=2, tiled=True)
    rows_now = lax.all_gather(arrived, "rep", axis=2, tiled=True)[0]
    gate_value = jnp.einsum(
        "emd,efd->emf", rows_now, gate_weight, preferred_element_type=jnp.float32
    )
    up_value = jnp.einsum("emd,efd->emf", rows_now, up_weight, preferred_element_type=jnp.float32)
    hidden = (jax.nn.silu(gate_value) * up_value).astype(jnp.bfloat16)
    outcome = jnp.einsum("emf,efd->emd", hidden, down_weight, preferred_element_type=jnp.float32)
    outcome = lax.optimization_barrier(outcome.astype(jnp.bfloat16))
    outcomes = outcome[None]
    outcomes = outcomes.reshape(local_experts, replicas, owners, capacity, model_width)
    column = routing_column(route_weights, routed_experts)
    column_slots = slot_table(
        column[1].reshape(replicas, token_rows, top_count), expert_count, capacity
    )
    returned = lax.all_to_all(outcomes, "exp", split_axis=2, concat_axis=0, tiled=True)
    returned = returned.reshape(expert_count, replicas, capacity, model_width)
    expert_index = column_slots // capacity
    place_index = column_slots % capacity
    replica_index = jnp.broadcast_to(
        jnp.arange(replicas, dtype=jnp.int32)[:, None], column_slots.shape
    )
    picked = returned[expert_index, replica_index, place_index].astype(jnp.float32)
    column_weights = column[0].reshape(replicas, token_rows, top_count)
    weighted = jnp.sum(
        picked.reshape(replicas, token_rows, top_count, model_width)
        * column_weights[:, :, :, None],
        axis=2,
    )
    summed = lax.psum_scatter(weighted, "rep", scatter_dimension=0, tiled=True)
    return summed.reshape(token_rows, model_width).astype(jnp.bfloat16)


def expert_kernel(pieces_in, pieces_out, local_experts, shard_units, model_width, top, block, *refs):
    own_ref, refs = refs[0], refs[1:]
    ins, refs = refs[: len(pieces_in)], refs[len(pieces_in) :]
    (gate_hbm, up_hbm, down_hbm), refs = refs[:3], refs[3:]
    outs, refs = refs[: len(pieces_out)], refs[len(pieces_out) :]
    rows, gates, ups, downs, hidden, result, row_sem, gate_sem, up_sem, down_sem, out_sem = refs
    units = local_experts * shard_units
    unit_block = gates.shape[1]
    unit_blocks = units // unit_block
    column_blocks = model_width // block

    row_copies, start = [], 0
    for place, count in enumerate(pieces_in):
        row_copies.append(
            pltpu.make_async_copy(ins[place], rows.at[pl.ds(start, count)], row_sem.at[place])
        )
        start += count

    def weight_copies(step):
        span = pl.ds(step * unit_block, unit_block)
        return (
            pltpu.make_async_copy(gate_hbm.at[span], gates.at[step], gate_sem.at[step]),
            pltpu.make_async_copy(up_hbm.at[span], ups.at[step], up_sem.at[step]),
        )

    for copy in row_copies:
        copy.start()
    for copy in weight_copies(0):
        copy.start()
    for copy in row_copies:
        copy.wait()
    for step in range(1, unit_blocks):
        for copy in weight_copies(step):
            copy.start()
    down_copy = pltpu.make_async_copy(down_hbm, downs, down_sem)
    down_copy.start()

    extra = rows[:, model_width:].astype(jnp.float32)
    width = extra.shape[1]
    scale = pltpu.roll(extra, width - top, 1) + pltpu.roll(extra, width - 2 * top, 1)
    lane = lax.broadcasted_iota(jnp.int32, extra.shape, 1)
    weights = []
    for expert in range(local_experts):
        name = (own_ref[0] + expert).astype(jnp.float32)
        chosen = jnp.logical_and(lane < top, extra == name)
        weights.append(jnp.sum(jnp.where(chosen, scale, 0.0), axis=1, keepdims=True))

    def unit_step(step, carry):
        for copy in weight_copies(step):
            copy.wait()
        values = rows[:, :model_width]
        contract = (((1,), (1,)), ((), ()))
        gate = lax.dot_general(values, gates[step], contract, preferred_element_type=jnp.float32)
        up = lax.dot_general(values, ups[step], contract, preferred_element_type=jnp.float32)
        unit = step * unit_block + lax.broadcasted_iota(jnp.int32, gate.shape, 1)
        weight = weights[0]
        for expert in range(1, local_experts):
            weight = jnp.where(unit >= expert * shard_units, weights[expert], weight)
        active = gate / (1.0 + jnp.exp(-gate)) * up * weight
        hidden[step] = active.astype(jnp.bfloat16)
        return carry

    lax.fori_loop(0, unit_blocks, unit_step, 0)
    down_copy.wait()
    active = jnp.concatenate([hidden[step] for step in range(unit_blocks)], axis=1)

    def out_copies(step):
        span = pl.ds(pl.multiple_of(step * block, block), block)
        copies = []
        for place, segments in enumerate(pieces_out):
            filled = 0
            for begin, count in segments:
                copies.append(
                    pltpu.make_async_copy(
                        result.at[pl.ds(begin, count), span],
                        outs[place].at[pl.ds(filled, count), span],
                        out_sem.at[step, len(copies)],
                    )
                )
                filled += count
        return copies

    def column_step(step, carry):
        span = pl.ds(pl.multiple_of(step * block, block), block)
        value = jnp.dot(active, downs[:, span], preferred_element_type=jnp.float32)
        result[:, span] = value.astype(jnp.bfloat16)
        for copy in out_copies(step):
            copy.start()
        return carry

    def finish_step(step, carry):
        for copy in out_copies(step):
            copy.wait()
        return carry

    lax.fori_loop(0, column_blocks, column_step, 0)
    lax.fori_loop(0, column_blocks, finish_step, 0)


def experts_of(pieces, pieces_out, gate_weight, up_weight, down_weight, top):
    local_experts, shard_units, model_width = gate_weight.shape
    units = local_experts * shard_units
    unit_block = 256 if units % 256 == 0 else 128
    block = 512
    pieces_in = [piece.shape[0] for piece in pieces]
    total = sum(pieces_in)
    packed = pieces[0].shape[1]
    own = jnp.full((1,), lax.axis_index("exp") * local_experts, jnp.int32)
    anywhere = pl.BlockSpec(memory_space=pl.ANY)
    kernel = functools.partial(
        expert_kernel, pieces_in, pieces_out, local_experts, shard_units, model_width, top, block
    )
    out_rows = [sum(count for _, count in segments) for segments in pieces_out]
    return pl.pallas_call(
        kernel,
        out_shape=[jax.ShapeDtypeStruct((count, model_width), jnp.bfloat16) for count in out_rows],
        in_specs=[pl.BlockSpec(memory_space=pltpu.SMEM)] + [anywhere] * (len(pieces) + 3),
        out_specs=[anywhere] * len(out_rows),
        scratch_shapes=[
            pltpu.VMEM((total, packed), jnp.bfloat16),
            pltpu.VMEM((units // unit_block, unit_block, model_width), jnp.bfloat16),
            pltpu.VMEM((units // unit_block, unit_block, model_width), jnp.bfloat16),
            pltpu.VMEM((units, model_width), jnp.bfloat16),
            pltpu.VMEM((units // unit_block, total, unit_block), jnp.bfloat16),
            pltpu.VMEM((total, model_width), jnp.bfloat16),
            pltpu.SemaphoreType.DMA((len(pieces),)),
            pltpu.SemaphoreType.DMA((units // unit_block,)),
            pltpu.SemaphoreType.DMA((units // unit_block,)),
            pltpu.SemaphoreType.DMA,
            pltpu.SemaphoreType.DMA((model_width // block, sum(len(segments) for segments in pieces_out))),
        ],
        compiler_params=pltpu.CompilerParams(vmem_limit_bytes=48 * 1024 * 1024),
        cost_estimate=pl.CostEstimate(
            flops=6 * total * units * model_width,
            bytes_accessed=6 * units * model_width + 4 * total * model_width,
            transcendentals=total * units,
        ),
        name="experts",
    )(
        own,
        *pieces,
        gate_weight.reshape(units, model_width),
        up_weight.reshape(units, model_width),
        down_weight.reshape(units, model_width),
    )


def pack_kernel(tokens_ref, experts_ref, weights_ref, packed_ref):
    model_width = tokens_ref.shape[1]
    packed_ref[:, :model_width] = tokens_ref[...]
    weights = weights_ref[...]
    high = weights.astype(jnp.bfloat16).astype(jnp.float32)
    listed = jnp.concatenate([experts_ref[...].astype(jnp.float32), high, weights - high], axis=0)
    width = packed_ref.shape[1] - model_width
    place = lax.broadcasted_iota(jnp.int32, (listed.shape[0], width), 0)
    lane = lax.broadcasted_iota(jnp.int32, (listed.shape[0], width), 1)
    chosen = jnp.where(place == lane, 1.0, 0.0).astype(jnp.bfloat16)
    extra = lax.dot_general(
        listed.astype(jnp.bfloat16),
        chosen,
        (((0,), (0,)), ((), ())),
        preferred_element_type=jnp.float32,
    )
    packed_ref[:, model_width:] = extra.astype(jnp.bfloat16)


def with_routing(tokens, routed_experts, route_weights):
    rows, width = tokens.shape
    return pl.pallas_call(
        pack_kernel,
        out_shape=jax.ShapeDtypeStruct((rows, width + 128), jnp.bfloat16),
        in_specs=[pl.BlockSpec(memory_space=pltpu.VMEM)] * 3,
        out_specs=pl.BlockSpec(memory_space=pltpu.VMEM),
        name="pack",
    )(tokens, routed_experts.T, route_weights.T)


def swap_exp(value, bit):
    owners = lax.axis_size("exp")
    return lax.ppermute(value, "exp", [(i, i ^ bit) for i in range(owners)])


def turn_rep(value, shift):
    replicas = lax.axis_size("rep")
    return lax.ppermute(value, "rep", [(i, (i - shift) % replicas) for i in range(replicas)])


def added(*terms):
    total = terms[0].astype(jnp.float32)
    for term in terms[1:]:
        total = total + term.astype(jnp.float32)
    return total


def rounded(*terms):
    return added(*terms).astype(jnp.bfloat16)


def gathered(one, two):
    rows = one.shape[0]
    pair = jnp.concatenate([one, two], axis=0)
    from_x, from_y = swap_exp(pair, 2), swap_exp(pair, 4)
    far_one, far_two = swap_exp(from_x[:rows], 4), swap_exp(from_y[rows:], 2)
    pieces = [pair, from_x, from_y, far_one, far_two]
    return pieces + [swap_exp(piece, 1) for piece in pieces]


def segments_of(rows):
    own, x_one, x_two, y_one, y_two, far_one, far_two = 0, 2, 3, 4, 5, 6, 7
    other = 8
    cuts = [
        [x_two, far_two],
        [y_one, far_one],
        [own, own + 1],
        [x_one],
        [y_two],
    ]
    cuts.append([other + place for cut in cuts for place in cut])
    return [[(place * rows, rows) for place in cut] for cut in cuts]


def reduced(parts, rows):
    to_x, to_y, own, x_one, y_two, other = parts
    back = swap_exp(other, 1)
    to_x = rounded(to_x, back[: 2 * rows])
    to_y = rounded(to_y, back[2 * rows : 4 * rows])
    from_x, from_y = swap_exp(to_x, 2), swap_exp(to_y, 4)
    x_one = rounded(x_one, back[6 * rows : 7 * rows], from_y[rows:])
    y_two = rounded(y_two, back[7 * rows :], from_x[rows:])
    last_x, last_y = swap_exp(x_one, 2), swap_exp(y_two, 4)
    one = added(own[:rows], back[4 * rows : 5 * rows], from_y[:rows], last_x)
    two = added(own[rows:], back[5 * rows : 6 * rows], from_x[:rows], last_y)
    return one, two


def on_device_dense(tokens, routed_experts, route_weights, gate_weight, up_weight, down_weight):
    top = routed_experts.shape[1]
    rows = tokens.shape[0]
    packed = with_routing(tokens, routed_experts, route_weights)
    turned = {s: turn_rep(packed, s) for s in (2, 1, 3)}
    near = gathered(packed, turned[2])
    far = gathered(turned[1], turned[3])
    segments = segments_of(rows)
    near_sums = reduced(experts_of(near, segments, gate_weight, up_weight, down_weight, top), rows)
    far_sums = reduced(experts_of(far, segments, gate_weight, up_weight, down_weight, top), rows)
    arrived = [
        turn_rep(near_sums[1].astype(jnp.bfloat16), -2),
        turn_rep(far_sums[0].astype(jnp.bfloat16), -1),
        turn_rep(far_sums[1].astype(jnp.bfloat16), -3),
    ]
    return rounded(near_sums[0], *arrived)


def solution(mesh):
    placed = (
        P(("rep", "exp"), None),
        P(("rep", "exp"), None),
        P(("rep", "exp"), None),
        P("exp", "rep", None),
        P("exp", "rep", None),
        P("exp", "rep", None),
    )
    plane = mesh.shape["exp"] == 8 and mesh.shape["rep"] == 4
    return jax.shard_map(
        on_device_dense if plane else on_device_slots,
        mesh=mesh,
        in_specs=placed,
        out_specs=P(("rep", "exp"), None),
        check_vma=False,
    )
```

```python
import functools

import jax
import jax.numpy as jnp
from jax import lax
from jax.experimental import pallas as pl
from jax.experimental.pallas import tpu as pltpu
from jax.sharding import PartitionSpec as P


def slot_table(experts, expert_count, capacity):
    blocks = experts.shape[0]
    flattened = experts.reshape(blocks, -1)
    onehot = (
        flattened[:, :, None] == jnp.arange(expert_count, dtype=jnp.int32)[None, None, :]
    ).astype(jnp.int32)
    before = jnp.cumsum(onehot, axis=1) - onehot
    position = jnp.sum(before * onehot, axis=2)
    return flattened * capacity + position


def token_picks(slots, top_count, slot_count):
    blocks = slots.shape[0]
    grouped = slots.reshape(blocks, 1, -1, top_count)
    return jnp.any(grouped == jnp.arange(slot_count, dtype=jnp.int32)[None, :, None, None], axis=3)


def routing_column(route_weights, routed_experts):
    as_float = routed_experts.astype(jnp.float32)
    weights_all, experts_all = (
        lax.all_gather(route_weights, "rep", axis=0, tiled=True),
        lax.all_gather(as_float, "rep", axis=0, tiled=True),
    )
    return (weights_all, experts_all.astype(jnp.int32))


def on_device_slots(tokens, routed_experts, route_weights, gate_weight, up_weight, down_weight):
    replicas = lax.axis_size("rep")
    owners = lax.axis_size("exp")
    token_rows, model_width = tokens.shape
    top_count = routed_experts.shape[1]
    local_experts = gate_weight.shape[0]
    expert_count = local_experts * owners
    capacity = max(2, 3 * token_rows * top_count // (2 * expert_count))
    slot_count = expert_count * capacity
    own_slots = slot_table(routed_experts[None], expert_count, capacity)
    column = None
    column_slots = None
    selected = token_picks(own_slots, top_count, slot_count)[0].astype(jnp.bfloat16)
    buffer = jnp.dot(selected, tokens, preferred_element_type=jnp.float32).astype(jnp.bfloat16)
    buffer = buffer.reshape(owners, local_experts, capacity, model_width)
    arrived = lax.all_to_all(buffer, "exp", split_axis=0, concat_axis=2, tiled=True)
    rows_now = lax.all_gather(arrived, "rep", axis=2, tiled=True)[0]
    gate_value = jnp.einsum(
        "emd,efd->emf", rows_now, gate_weight, preferred_element_type=jnp.float32
    )
    up_value = jnp.einsum("emd,efd->emf", rows_now, up_weight, preferred_element_type=jnp.float32)
    hidden = (jax.nn.silu(gate_value) * up_value).astype(jnp.bfloat16)
    outcome = jnp.einsum("emf,efd->emd", hidden, down_weight, preferred_element_type=jnp.float32)
    outcome = lax.optimization_barrier(outcome.astype(jnp.bfloat16))
    outcomes = outcome[None]
    outcomes = outcomes.reshape(local_experts, replicas, owners, capacity, model_width)
    column = routing_column(route_weights, routed_experts)
    column_slots = slot_table(
        column[1].reshape(replicas, token_rows, top_count), expert_count, capacity
    )
    returned = lax.all_to_all(outcomes, "exp", split_axis=2, concat_axis=0, tiled=True)
    returned = returned.reshape(expert_count, replicas, capacity, model_width)
    expert_index = column_slots // capacity
    place_index = column_slots % capacity
    replica_index = jnp.broadcast_to(
        jnp.arange(replicas, dtype=jnp.int32)[:, None], column_slots.shape
    )
    picked = returned[expert_index, replica_index, place_index].astype(jnp.float32)
    column_weights = column[0].reshape(replicas, token_rows, top_count)
    weighted = jnp.sum(
        picked.reshape(replicas, token_rows, top_count, model_width)
        * column_weights[:, :, :, None],
        axis=2,
    )
    summed = lax.psum_scatter(weighted, "rep", scatter_dimension=0, tiled=True)
    return summed.reshape(token_rows, model_width).astype(jnp.bfloat16)


def expert_kernel(pieces_in, pieces_out, local_experts, shard_units, model_width, top, block, *refs):
    own_ref, refs = refs[0], refs[1:]
    ins, refs = refs[: len(pieces_in)], refs[len(pieces_in) :]
    (gate_ref, up_ref, down_ref), refs = refs[:3], refs[3:]
    outs, refs = refs[: len(pieces_out)], refs[len(pieces_out) :]
    rows, turned, hidden, result, row_sem, out_sem = refs
    units = local_experts * shard_units
    unit_block = shard_units
    unit_blocks = local_experts
    column_blocks = model_width // block
    total = rows.shape[0]

    row_copies, start = [], 0
    for place, count in enumerate(pieces_in):
        row_copies.append(
            pltpu.make_async_copy(ins[place], rows.at[pl.ds(start, count)], row_sem.at[place])
        )
        start += count

    for copy in row_copies:
        copy.start()
    for copy in row_copies:
        copy.wait()

    turned[...] = rows[...].T
    extra = turned[model_width:, :].astype(jnp.float32)
    scale = extra[top : 2 * top] + extra[2 * top : 3 * top]
    weights = []
    for expert in range(local_experts):
        name = (own_ref[0] + expert).astype(jnp.float32)
        weights.append(jnp.sum(jnp.where(extra[:top] == name, scale, 0.0), axis=0, keepdims=True))

    values = turned[:model_width, :]
    for expert in range(local_experts):
        span = pl.ds(expert * shard_units, shard_units)
        gate = jnp.dot(gate_ref[span, :], values, preferred_element_type=jnp.float32)
        up = jnp.dot(up_ref[span, :], values, preferred_element_type=jnp.float32)
        active = gate / (1.0 + jnp.exp(-gate)) * up * weights[expert]
        hidden[:, span] = active.astype(jnp.bfloat16).T

    def out_copies(step):
        span = pl.ds(pl.multiple_of(step * block, block), block)
        copies = []
        for place, segments in enumerate(pieces_out):
            filled = 0
            for begin, count in segments:
                copies.append(
                    pltpu.make_async_copy(
                        result.at[pl.ds(begin, count), span],
                        outs[place].at[pl.ds(filled, count), span],
                        out_sem.at[step, len(copies)],
                    )
                )
                filled += count
        return copies

    def column_step(step, carry):
        span = pl.ds(pl.multiple_of(step * block, block), block)
        value = jnp.dot(hidden[...], down_ref[:, span], preferred_element_type=jnp.float32)
        result[:, span] = value.astype(jnp.bfloat16)
        for copy in out_copies(step):
            copy.start()
        return carry

    def finish_step(step, carry):
        for copy in out_copies(step):
            copy.wait()
        return carry

    lax.fori_loop(0, column_blocks, column_step, 0)
    lax.fori_loop(0, column_blocks, finish_step, 0)


def experts_of(pieces, pieces_out, gate_weight, up_weight, down_weight, top):
    local_experts, shard_units, model_width = gate_weight.shape
    units = local_experts * shard_units
    block = 512
    pieces_in = [piece.shape[0] for piece in pieces]
    total = sum(pieces_in)
    packed = pieces[0].shape[1]
    own = jnp.full((1,), lax.axis_index("exp") * local_experts, jnp.int32)
    anywhere = pl.BlockSpec(memory_space=pl.ANY)
    kernel = functools.partial(
        expert_kernel, pieces_in, pieces_out, local_experts, shard_units, model_width, top, block
    )
    out_rows = [sum(count for _, count in segments) for segments in pieces_out]
    return pl.pallas_call(
        kernel,
        out_shape=[jax.ShapeDtypeStruct((count, model_width), jnp.bfloat16) for count in out_rows],
        in_specs=[pl.BlockSpec(memory_space=pltpu.SMEM)]
        + [anywhere] * len(pieces)
        + [pl.BlockSpec(memory_space=pltpu.VMEM)] * 3,
        out_specs=[anywhere] * len(out_rows),
        scratch_shapes=[
            pltpu.VMEM((total, packed), jnp.bfloat16),
            pltpu.VMEM((packed, total), jnp.bfloat16),
            pltpu.VMEM((total, units), jnp.bfloat16),
            pltpu.VMEM((total, model_width), jnp.bfloat16),
            pltpu.SemaphoreType.DMA((len(pieces),)),
            pltpu.SemaphoreType.DMA((model_width // block, sum(len(segments) for segments in pieces_out))),
        ],
        compiler_params=pltpu.CompilerParams(vmem_limit_bytes=12 * 1024 * 1024),
        cost_estimate=pl.CostEstimate(
            flops=6 * total * units * model_width,
            bytes_accessed=6 * units * model_width + 4 * total * model_width,
            transcendentals=total * units,
        ),
        name="experts",
    )(
        own,
        *pieces,
        gate_weight.reshape(units, model_width),
        up_weight.reshape(units, model_width),
        down_weight.reshape(units, model_width),
    )


def pack_kernel(tokens_ref, experts_ref, weights_ref, packed_ref):
    model_width = tokens_ref.shape[1]
    packed_ref[:, :model_width] = tokens_ref[...]
    weights = weights_ref[...]
    high = weights.astype(jnp.bfloat16).astype(jnp.float32)
    listed = jnp.concatenate([experts_ref[...].astype(jnp.float32), high, weights - high], axis=0)
    width = packed_ref.shape[1] - model_width
    place = lax.broadcasted_iota(jnp.int32, (listed.shape[0], width), 0)
    lane = lax.broadcasted_iota(jnp.int32, (listed.shape[0], width), 1)
    chosen = jnp.where(place == lane, 1.0, 0.0).astype(jnp.bfloat16)
    extra = lax.dot_general(
        listed.astype(jnp.bfloat16),
        chosen,
        (((0,), (0,)), ((), ())),
        preferred_element_type=jnp.float32,
    )
    packed_ref[:, model_width:] = extra.astype(jnp.bfloat16)


def with_routing(tokens, routed_experts, route_weights):
    rows, width = tokens.shape
    return pl.pallas_call(
        pack_kernel,
        out_shape=jax.ShapeDtypeStruct((rows, width + 128), jnp.bfloat16),
        in_specs=[pl.BlockSpec(memory_space=pltpu.VMEM)] * 3,
        out_specs=pl.BlockSpec(memory_space=pltpu.VMEM),
        compiler_params=pltpu.CompilerParams(vmem_limit_bytes=2 * 1024 * 1024),
        name="pack",
    )(tokens, routed_experts.T, route_weights.T)


def swap_exp(value, bit):
    owners = lax.axis_size("exp")
    return lax.ppermute(value, "exp", [(i, i ^ bit) for i in range(owners)])


def turn_rep(value, shift):
    replicas = lax.axis_size("rep")
    return lax.ppermute(value, "rep", [(i, (i - shift) % replicas) for i in range(replicas)])


def added(*terms):
    total = terms[0].astype(jnp.float32)
    for term in terms[1:]:
        total = total + term.astype(jnp.float32)
    return total


def rounded(*terms):
    return added(*terms).astype(jnp.bfloat16)


def gathered(one, two):
    rows = one.shape[0]
    pair = jnp.concatenate([one, two], axis=0)
    from_x, from_y = swap_exp(pair, 2), swap_exp(pair, 4)
    far_one, far_two = swap_exp(from_x[:rows], 4), swap_exp(from_y[rows:], 2)
    pieces = [pair, from_x, from_y, far_one, far_two]
    return pieces + [swap_exp(piece, 1) for piece in pieces]


def segments_of(rows):
    own, x_one, x_two, y_one, y_two, far_one, far_two = 0, 2, 3, 4, 5, 6, 7
    other = 8
    cuts = [
        [x_two, far_two],
        [y_one, far_one],
        [own, own + 1],
        [x_one],
        [y_two],
    ]
    cuts.append([other + place for cut in cuts for place in cut])
    return [[(place * rows, rows) for place in cut] for cut in cuts]


def reduced(parts, rows):
    to_x, to_y, own, x_one, y_two, other = parts
    back = swap_exp(other, 1)
    to_x = rounded(to_x, back[: 2 * rows])
    to_y = rounded(to_y, back[2 * rows : 4 * rows])
    from_x, from_y = swap_exp(to_x, 2), swap_exp(to_y, 4)
    x_one = rounded(x_one, back[6 * rows : 7 * rows], from_y[rows:])
    y_two = rounded(y_two, back[7 * rows :], from_x[rows:])
    last_x, last_y = swap_exp(x_one, 2), swap_exp(y_two, 4)
    one = added(own[:rows], back[4 * rows : 5 * rows], from_y[:rows], last_x)
    two = added(own[rows:], back[5 * rows : 6 * rows], from_x[:rows], last_y)
    return one, two


def on_device_dense(tokens, routed_experts, route_weights, gate_weight, up_weight, down_weight):
    top = routed_experts.shape[1]
    rows = tokens.shape[0]
    packed = with_routing(tokens, routed_experts, route_weights)
    turned = {s: turn_rep(packed, s) for s in (2, 1, 3)}
    near = gathered(packed, turned[2])
    far = gathered(turned[1], turned[3])
    segments = segments_of(rows)
    near_sums = reduced(experts_of(near, segments, gate_weight, up_weight, down_weight, top), rows)
    far_sums = reduced(experts_of(far, segments, gate_weight, up_weight, down_weight, top), rows)
    arrived = [
        turn_rep(near_sums[1].astype(jnp.bfloat16), -2),
        turn_rep(far_sums[0].astype(jnp.bfloat16), -1),
        turn_rep(far_sums[1].astype(jnp.bfloat16), -3),
    ]
    return rounded(near_sums[0], *arrived)


def solution(mesh):
    placed = (
        P(("rep", "exp"), None),
        P(("rep", "exp"), None),
        P(("rep", "exp"), None),
        P("exp", "rep", None),
        P("exp", "rep", None),
        P("exp", "rep", None),
    )
    plane = mesh.shape["exp"] == 8 and mesh.shape["rep"] == 4
    return jax.shard_map(
        on_device_dense if plane else on_device_slots,
        mesh=mesh,
        in_specs=placed,
        out_specs=P(("rep", "exp"), None),
        check_vma=False,
    )
```

```python
import functools

import jax
import jax.numpy as jnp
from jax import lax
from jax.experimental import pallas as pl
from jax.experimental.pallas import tpu as pltpu
from jax.sharding import PartitionSpec as P


def slot_table(experts, expert_count, capacity):
    blocks = experts.shape[0]
    flattened = experts.reshape(blocks, -1)
    onehot = (
        flattened[:, :, None] == jnp.arange(expert_count, dtype=jnp.int32)[None, None, :]
    ).astype(jnp.int32)
    before = jnp.cumsum(onehot, axis=1) - onehot
    position = jnp.sum(before * onehot, axis=2)
    return flattened * capacity + position


def token_picks(slots, top_count, slot_count):
    blocks = slots.shape[0]
    grouped = slots.reshape(blocks, 1, -1, top_count)
    return jnp.any(grouped == jnp.arange(slot_count, dtype=jnp.int32)[None, :, None, None], axis=3)


def routing_column(route_weights, routed_experts):
    as_float = routed_experts.astype(jnp.float32)
    weights_all, experts_all = (
        lax.all_gather(route_weights, "rep", axis=0, tiled=True),
        lax.all_gather(as_float, "rep", axis=0, tiled=True),
    )
    return (weights_all, experts_all.astype(jnp.int32))


def on_device_slots(tokens, routed_experts, route_weights, gate_weight, up_weight, down_weight):
    replicas = lax.axis_size("rep")
    owners = lax.axis_size("exp")
    token_rows, model_width = tokens.shape
    top_count = routed_experts.shape[1]
    local_experts = gate_weight.shape[0]
    expert_count = local_experts * owners
    capacity = max(2, 3 * token_rows * top_count // (2 * expert_count))
    slot_count = expert_count * capacity
    own_slots = slot_table(routed_experts[None], expert_count, capacity)
    column = None
    column_slots = None
    selected = token_picks(own_slots, top_count, slot_count)[0].astype(jnp.bfloat16)
    buffer = jnp.dot(selected, tokens, preferred_element_type=jnp.float32).astype(jnp.bfloat16)
    buffer = buffer.reshape(owners, local_experts, capacity, model_width)
    arrived = lax.all_to_all(buffer, "exp", split_axis=0, concat_axis=2, tiled=True)
    rows_now = lax.all_gather(arrived, "rep", axis=2, tiled=True)[0]
    gate_value = jnp.einsum(
        "emd,efd->emf", rows_now, gate_weight, preferred_element_type=jnp.float32
    )
    up_value = jnp.einsum("emd,efd->emf", rows_now, up_weight, preferred_element_type=jnp.float32)
    hidden = (jax.nn.silu(gate_value) * up_value).astype(jnp.bfloat16)
    outcome = jnp.einsum("emf,efd->emd", hidden, down_weight, preferred_element_type=jnp.float32)
    outcome = lax.optimization_barrier(outcome.astype(jnp.bfloat16))
    outcomes = outcome[None]
    outcomes = outcomes.reshape(local_experts, replicas, owners, capacity, model_width)
    column = routing_column(route_weights, routed_experts)
    column_slots = slot_table(
        column[1].reshape(replicas, token_rows, top_count), expert_count, capacity
    )
    returned = lax.all_to_all(outcomes, "exp", split_axis=2, concat_axis=0, tiled=True)
    returned = returned.reshape(expert_count, replicas, capacity, model_width)
    expert_index = column_slots // capacity
    place_index = column_slots % capacity
    replica_index = jnp.broadcast_to(
        jnp.arange(replicas, dtype=jnp.int32)[:, None], column_slots.shape
    )
    picked = returned[expert_index, replica_index, place_index].astype(jnp.float32)
    column_weights = column[0].reshape(replicas, token_rows, top_count)
    weighted = jnp.sum(
        picked.reshape(replicas, token_rows, top_count, model_width)
        * column_weights[:, :, :, None],
        axis=2,
    )
    summed = lax.psum_scatter(weighted, "rep", scatter_dimension=0, tiled=True)
    return summed.reshape(token_rows, model_width).astype(jnp.bfloat16)


def fetch_kernel(turn, source_ref, result_ref):
    rows, width = source_ref.shape
    block = 512

    def fetch_block(step, carry):
        span = pl.ds(pl.multiple_of(step * block, block), block)
        if turn:
            for part in range(0, rows, 128):
                result_ref[span, part : part + 128] = source_ref[part : part + 128, span].T
        else:
            result_ref[:, span] = source_ref[:, span]
        return carry

    lax.fori_loop(0, width // block, fetch_block, 0)


def fetched(weight, turn):
    rows, width = weight.shape
    return pl.pallas_call(
        functools.partial(fetch_kernel, turn),
        out_shape=jax.ShapeDtypeStruct((width, rows) if turn else (rows, width), jnp.bfloat16),
        in_specs=[pl.BlockSpec(memory_space=pltpu.VMEM)],
        out_specs=pl.BlockSpec(memory_space=pltpu.VMEM),
        compiler_params=pltpu.CompilerParams(vmem_limit_bytes=4 * 1024 * 1024),
        cost_estimate=pl.CostEstimate(
            flops=0, bytes_accessed=4 * rows * width, transcendentals=0
        ),
        name="fetch_turned" if turn else "fetch",
    )(weight)


def expert_kernel(pieces_in, pieces_out, local_experts, shard_units, model_width, top, *refs):
    own_ref, refs = refs[0], refs[1:]
    ins, refs = refs[: len(pieces_in)], refs[len(pieces_in) :]
    (gate_ref, up_ref, down_ref), refs = refs[:3], refs[3:]
    outs, refs = refs[: len(pieces_out)], refs[len(pieces_out) :]
    rows, hidden = refs
    units = local_experts * shard_units
    unit_block = 256 if units % 256 == 0 else 128
    block = 512

    start = 0
    for place, count in enumerate(pieces_in):
        rows[start : start + count, :] = ins[place][...]
        start += count

    extra = rows[:, model_width:].astype(jnp.float32)
    width = extra.shape[1]
    scale = pltpu.roll(extra, width - top, 1) + pltpu.roll(extra, width - 2 * top, 1)
    lane = lax.broadcasted_iota(jnp.int32, extra.shape, 1)
    weights = []
    for expert in range(local_experts):
        name = (own_ref[0] + expert).astype(jnp.float32)
        chosen = jnp.logical_and(lane < top, extra == name)
        weights.append(jnp.sum(jnp.where(chosen, scale, 0.0), axis=1, keepdims=True))

    for begin in range(0, units, unit_block):
        span = slice(begin, begin + unit_block)
        values = rows[:, :model_width]
        gate = jnp.dot(values, gate_ref[:, span], preferred_element_type=jnp.float32)
        up = jnp.dot(values, up_ref[:, span], preferred_element_type=jnp.float32)
        unit = begin + lax.broadcasted_iota(jnp.int32, gate.shape, 1)
        weight = weights[begin // shard_units]
        for expert in range(begin // shard_units + 1, (begin + unit_block - 1) // shard_units + 1):
            weight = jnp.where(unit >= expert * shard_units, weights[expert], weight)
        active = gate / (1.0 + jnp.exp(-gate)) * up * weight
        hidden[:, span] = active.astype(jnp.bfloat16)

    for begin in range(0, model_width, block):
        span = slice(begin, begin + block)
        value = jnp.dot(hidden[...], down_ref[:, span], preferred_element_type=jnp.float32)
        value = value.astype(jnp.bfloat16)
        for place, segments in enumerate(pieces_out):
            filled = 0
            for first, count in segments:
                outs[place][filled : filled + count, span] = value[first : first + count]
                filled += count


def experts_of(pieces, pieces_out, gates, ups, downs, shard_units, top):
    units, model_width = downs.shape
    local_experts = units // shard_units
    pieces_in = [piece.shape[0] for piece in pieces]
    total = sum(pieces_in)
    packed = pieces[0].shape[1]
    own = jnp.full((1,), lax.axis_index("exp") * local_experts, jnp.int32)
    resident = pl.BlockSpec(memory_space=pltpu.VMEM)
    kernel = functools.partial(
        expert_kernel, pieces_in, pieces_out, local_experts, shard_units, model_width, top
    )
    out_rows = [sum(count for _, count in segments) for segments in pieces_out]
    return pl.pallas_call(
        kernel,
        out_shape=[jax.ShapeDtypeStruct((count, model_width), jnp.bfloat16) for count in out_rows],
        in_specs=[pl.BlockSpec(memory_space=pltpu.SMEM)] + [resident] * (len(pieces) + 3),
        out_specs=[resident] * len(out_rows),
        scratch_shapes=[
            pltpu.VMEM((total, packed), jnp.bfloat16),
            pltpu.VMEM((total, units), jnp.bfloat16),
        ],
        compiler_params=pltpu.CompilerParams(vmem_limit_bytes=12 * 1024 * 1024),
        cost_estimate=pl.CostEstimate(
            flops=6 * total * units * model_width,
            bytes_accessed=4 * total * model_width,
            transcendentals=total * units,
        ),
        name="experts",
    )(own, *pieces, gates, ups, downs)


def pack_kernel(tokens_ref, experts_ref, weights_ref, packed_ref):
    model_width = tokens_ref.shape[1]
    packed_ref[:, :model_width] = tokens_ref[...]
    weights = weights_ref[...]
    high = weights.astype(jnp.bfloat16).astype(jnp.float32)
    listed = jnp.concatenate([experts_ref[...].astype(jnp.float32), high, weights - high], axis=0)
    width = packed_ref.shape[1] - model_width
    place = lax.broadcasted_iota(jnp.int32, (listed.shape[0], width), 0)
    lane = lax.broadcasted_iota(jnp.int32, (listed.shape[0], width), 1)
    chosen = jnp.where(place == lane, 1.0, 0.0).astype(jnp.bfloat16)
    extra = lax.dot_general(
        listed.astype(jnp.bfloat16),
        chosen,
        (((0,), (0,)), ((), ())),
        preferred_element_type=jnp.float32,
    )
    packed_ref[:, model_width:] = extra.astype(jnp.bfloat16)


def with_routing(tokens, routed_experts, route_weights):
    rows, width = tokens.shape
    return pl.pallas_call(
        pack_kernel,
        out_shape=jax.ShapeDtypeStruct((rows, width + 128), jnp.bfloat16),
        in_specs=[pl.BlockSpec(memory_space=pltpu.VMEM)] * 3,
        out_specs=pl.BlockSpec(memory_space=pltpu.VMEM),
        name="pack",
    )(tokens, routed_experts.T, route_weights.T)


def swap_exp(value, bit):
    owners = lax.axis_size("exp")
    return lax.ppermute(value, "exp", [(i, i ^ bit) for i in range(owners)])


def turn_rep(value, shift):
    replicas = lax.axis_size("rep")
    return lax.ppermute(value, "rep", [(i, (i - shift) % replicas) for i in range(replicas)])


def added(*terms):
    total = terms[0].astype(jnp.float32)
    for term in terms[1:]:
        total = total + term.astype(jnp.float32)
    return total


def rounded(*terms):
    return added(*terms).astype(jnp.bfloat16)


def segments_of(rows):
    own, x_one, x_two, y_one, y_two, far_one, far_two = 0, 2, 3, 4, 5, 6, 7
    other = 8
    cuts = [
        [x_two, far_two],
        [y_one, far_one],
        [own, own + 1],
        [x_one],
        [y_two],
    ]
    cuts.append([other + place for cut in cuts for place in cut])
    return [[(place * rows, rows) for place in cut] for cut in cuts]


def cores_added(parts, rows):
    to_x, to_y, own, x_one, y_two, other = parts
    back = swap_exp(other, 1)
    to_x = rounded(to_x, back[: 2 * rows])
    to_y = rounded(to_y, back[2 * rows : 4 * rows])
    return to_x, to_y, own, x_one, y_two, back


def plane_halved(parts, arrived, rows):
    to_x, to_y, own, x_one, y_two, back = parts
    from_x, from_y = arrived
    x_one = rounded(x_one, back[6 * rows : 7 * rows], from_y[rows:])
    y_two = rounded(y_two, back[7 * rows :], from_x[rows:])
    last_x, last_y = swap_exp(x_one, 2), swap_exp(y_two, 4)
    one = added(own[:rows], back[4 * rows : 5 * rows], from_y[:rows], last_x)
    two = added(own[rows:], back[5 * rows : 6 * rows], from_x[:rows], last_y)
    return one, two


def ordered(*values):
    return lax.optimization_barrier(values)


def on_device_dense(tokens, routed_experts, route_weights, gate_weight, up_weight, down_weight):
    local_experts, shard_units, model_width = gate_weight.shape
    units = local_experts * shard_units
    top = routed_experts.shape[1]
    rows = tokens.shape[0]
    gate_weight = gate_weight.reshape(units, model_width)
    up_weight = up_weight.reshape(units, model_width)
    down_weight = down_weight.reshape(units, model_width)
    packed = with_routing(tokens, routed_experts, route_weights)
    turned = {s: turn_rep(packed, s) for s in (2, 1, 3)}

    gates = fetched(gate_weight, True)
    near_z, gates, up_weight = ordered(turned[2], gates, up_weight)
    ups = fetched(up_weight, True)
    near = jnp.concatenate([packed, near_z], axis=0)
    near_x, near_y = swap_exp(near, 2), swap_exp(near, 4)
    far = jnp.concatenate([turned[1], turned[3]], axis=0)
    near_x, near_y, far, ups, down_weight = ordered(near_x, near_y, far, ups, down_weight)
    downs = fetched(down_weight, False)
    near_far = [swap_exp(near_x[:rows], 4), swap_exp(near_y[rows:], 2)]
    far_x, far_y = swap_exp(far, 2), swap_exp(far, 4)
    *near_far, downs = ordered(*near_far, downs)
    near = [near, near_x, near_y, *near_far]
    near = near + [swap_exp(piece, 1) for piece in near]

    far_one, far_two = far_x[:rows], far_y[rows:]
    *near, far_one, far_two = ordered(*near, far_one, far_two)
    far = [far, far_x, far_y]
    far_far = [swap_exp(far_one, 4), swap_exp(far_two, 2)]
    far_other = [swap_exp(piece, 1) for piece in far]
    segments = segments_of(rows)
    parts = experts_of(near, segments, gates, ups, downs, shard_units, top)
    *parts, far_one, far_two, other_one, other_x, other_y = ordered(*parts, *far_far, *far_other)
    far = far + [far_one, far_two, other_one, other_x, other_y]
    far = far + [swap_exp(far_one, 1), swap_exp(far_two, 1)]

    near_parts = cores_added(parts, rows)
    arrived = [swap_exp(near_parts[0], 2), swap_exp(near_parts[1], 4)]
    to_x, to_y, *far = ordered(near_parts[0], near_parts[1], *far)
    near_parts = (to_x, to_y, *near_parts[2:])
    parts = experts_of(far, segments, gates, ups, downs, shard_units, top)
    *parts, near_x, near_y = ordered(*parts, *arrived)
    far_parts = cores_added(parts, rows)
    near_sums = plane_halved(near_parts, (near_x, near_y), rows)
    arrived = [swap_exp(far_parts[0], 2), swap_exp(far_parts[1], 4)]
    far_sums = plane_halved(far_parts, arrived, rows)
    arrived = [
        turn_rep(near_sums[1].astype(jnp.bfloat16), -2),
        turn_rep(far_sums[0].astype(jnp.bfloat16), -1),
        turn_rep(far_sums[1].astype(jnp.bfloat16), -3),
    ]
    return rounded(near_sums[0], *arrived)


def solution(mesh):
    placed = (
        P(("rep", "exp"), None),
        P(("rep", "exp"), None),
        P(("rep", "exp"), None),
        P("exp", "rep", None),
        P("exp", "rep", None),
        P("exp", "rep", None),
    )
    plane = mesh.shape["exp"] == 8 and mesh.shape["rep"] == 4
    return jax.shard_map(
        on_device_dense if plane else on_device_slots,
        mesh=mesh,
        in_specs=placed,
        out_specs=P(("rep", "exp"), None),
        check_vma=False,
    )
```

```python
import functools

import jax
import jax.numpy as jnp
from jax import lax
from jax.experimental import pallas as pl
from jax.experimental.pallas import tpu as pltpu
from jax.sharding import PartitionSpec as P


def slot_table(experts, expert_count, capacity):
    blocks = experts.shape[0]
    flattened = experts.reshape(blocks, -1)
    onehot = (
        flattened[:, :, None] == jnp.arange(expert_count, dtype=jnp.int32)[None, None, :]
    ).astype(jnp.int32)
    before = jnp.cumsum(onehot, axis=1) - onehot
    position = jnp.sum(before * onehot, axis=2)
    return flattened * capacity + position


def token_picks(slots, top_count, slot_count):
    blocks = slots.shape[0]
    grouped = slots.reshape(blocks, 1, -1, top_count)
    return jnp.any(grouped == jnp.arange(slot_count, dtype=jnp.int32)[None, :, None, None], axis=3)


def routing_column(route_weights, routed_experts):
    as_float = routed_experts.astype(jnp.float32)
    weights_all, experts_all = (
        lax.all_gather(route_weights, "rep", axis=0, tiled=True),
        lax.all_gather(as_float, "rep", axis=0, tiled=True),
    )
    return (weights_all, experts_all.astype(jnp.int32))


def on_device_slots(tokens, routed_experts, route_weights, gate_weight, up_weight, down_weight):
    replicas = lax.axis_size("rep")
    owners = lax.axis_size("exp")
    token_rows, model_width = tokens.shape
    top_count = routed_experts.shape[1]
    local_experts = gate_weight.shape[0]
    expert_count = local_experts * owners
    capacity = max(2, 3 * token_rows * top_count // (2 * expert_count))
    slot_count = expert_count * capacity
    own_slots = slot_table(routed_experts[None], expert_count, capacity)
    column = None
    column_slots = None
    selected = token_picks(own_slots, top_count, slot_count)[0].astype(jnp.bfloat16)
    buffer = jnp.dot(selected, tokens, preferred_element_type=jnp.float32).astype(jnp.bfloat16)
    buffer = buffer.reshape(owners, local_experts, capacity, model_width)
    arrived = lax.all_to_all(buffer, "exp", split_axis=0, concat_axis=2, tiled=True)
    rows_now = lax.all_gather(arrived, "rep", axis=2, tiled=True)[0]
    gate_value = jnp.einsum(
        "emd,efd->emf", rows_now, gate_weight, preferred_element_type=jnp.float32
    )
    up_value = jnp.einsum("emd,efd->emf", rows_now, up_weight, preferred_element_type=jnp.float32)
    hidden = (jax.nn.silu(gate_value) * up_value).astype(jnp.bfloat16)
    outcome = jnp.einsum("emf,efd->emd", hidden, down_weight, preferred_element_type=jnp.float32)
    outcome = lax.optimization_barrier(outcome.astype(jnp.bfloat16))
    outcomes = outcome[None]
    outcomes = outcomes.reshape(local_experts, replicas, owners, capacity, model_width)
    column = routing_column(route_weights, routed_experts)
    column_slots = slot_table(
        column[1].reshape(replicas, token_rows, top_count), expert_count, capacity
    )
    returned = lax.all_to_all(outcomes, "exp", split_axis=2, concat_axis=0, tiled=True)
    returned = returned.reshape(expert_count, replicas, capacity, model_width)
    expert_index = column_slots // capacity
    place_index = column_slots % capacity
    replica_index = jnp.broadcast_to(
        jnp.arange(replicas, dtype=jnp.int32)[:, None], column_slots.shape
    )
    picked = returned[expert_index, replica_index, place_index].astype(jnp.float32)
    column_weights = column[0].reshape(replicas, token_rows, top_count)
    weighted = jnp.sum(
        picked.reshape(replicas, token_rows, top_count, model_width)
        * column_weights[:, :, :, None],
        axis=2,
    )
    summed = lax.psum_scatter(weighted, "rep", scatter_dimension=0, tiled=True)
    return summed.reshape(token_rows, model_width).astype(jnp.bfloat16)


def fetch_kernel(turn, source_ref, result_ref):
    rows, width = source_ref.shape
    block = 512

    def fetch_block(step, carry):
        span = pl.ds(pl.multiple_of(step * block, block), block)
        if turn:
            for part in range(0, rows, 128):
                result_ref[span, part : part + 128] = source_ref[part : part + 128, span].T
        else:
            result_ref[:, span] = source_ref[:, span]
        return carry

    lax.fori_loop(0, width // block, fetch_block, 0)


def fetched(weight, turn):
    rows, width = weight.shape
    return pl.pallas_call(
        functools.partial(fetch_kernel, turn),
        out_shape=jax.ShapeDtypeStruct((width, rows) if turn else (rows, width), jnp.bfloat16),
        in_specs=[pl.BlockSpec(memory_space=pltpu.VMEM)],
        out_specs=pl.BlockSpec(memory_space=pltpu.VMEM),
        compiler_params=pltpu.CompilerParams(vmem_limit_bytes=4 * 1024 * 1024),
        cost_estimate=pl.CostEstimate(
            flops=0, bytes_accessed=4 * rows * width, transcendentals=0
        ),
        name="fetch_turned" if turn else "fetch",
    )(weight)


def gather_kernel(*refs):
    *pieces, whole_ref = refs
    start = 0
    for piece_ref in pieces:
        count = piece_ref.shape[0]
        whole_ref[start : start + count, :] = piece_ref[...]
        start += count


def gathered(*pieces):
    rows = sum(piece.shape[0] for piece in pieces)
    resident = pl.BlockSpec(memory_space=pltpu.VMEM)
    return pl.pallas_call(
        gather_kernel,
        out_shape=jax.ShapeDtypeStruct((rows, pieces[0].shape[1]), jnp.bfloat16),
        in_specs=[resident] * len(pieces),
        out_specs=resident,
        compiler_params=pltpu.CompilerParams(vmem_limit_bytes=2 * 1024 * 1024),
        name="gather",
    )(*pieces)


def expert_kernel(pieces_in, pieces_out, local_experts, shard_units, model_width, top, *refs):
    own_ref, refs = refs[0], refs[1:]
    ins, refs = refs[: len(pieces_in)], refs[len(pieces_in) :]
    (gate_ref, up_ref, down_ref), refs = refs[:3], refs[3:]
    outs, refs = refs[: len(pieces_out)], refs[len(pieces_out) :]
    rows, hidden = refs
    units = local_experts * shard_units
    unit_block = 256 if units % 256 == 0 else 128
    block = 512

    start = 0
    for place, count in enumerate(pieces_in):
        rows[start : start + count, :] = ins[place][...]
        start += count

    extra = rows[:, model_width:].astype(jnp.float32)
    width = extra.shape[1]
    scale = pltpu.roll(extra, width - top, 1) + pltpu.roll(extra, width - 2 * top, 1)
    lane = lax.broadcasted_iota(jnp.int32, extra.shape, 1)
    weights = []
    for expert in range(local_experts):
        name = (own_ref[0] + expert).astype(jnp.float32)
        chosen = jnp.logical_and(lane < top, extra == name)
        weights.append(jnp.sum(jnp.where(chosen, scale, 0.0), axis=1, keepdims=True))

    for begin in range(0, units, unit_block):
        span = slice(begin, begin + unit_block)
        values = rows[:, :model_width]
        gate = jnp.dot(values, gate_ref[:, span], preferred_element_type=jnp.float32)
        up = jnp.dot(values, up_ref[:, span], preferred_element_type=jnp.float32)
        unit = begin + lax.broadcasted_iota(jnp.int32, gate.shape, 1)
        weight = weights[begin // shard_units]
        for expert in range(begin // shard_units + 1, (begin + unit_block - 1) // shard_units + 1):
            weight = jnp.where(unit >= expert * shard_units, weights[expert], weight)
        active = gate / (1.0 + jnp.exp(-gate)) * up * weight
        hidden[:, span] = active.astype(jnp.bfloat16)

    for begin in range(0, model_width, block):
        span = slice(begin, begin + block)
        value = jnp.dot(hidden[...], down_ref[:, span], preferred_element_type=jnp.float32)
        value = value.astype(jnp.bfloat16)
        for place, segments in enumerate(pieces_out):
            filled = 0
            for first, count in segments:
                outs[place][filled : filled + count, span] = value[first : first + count]
                filled += count


def experts_of(own, pieces, pieces_out, gates, ups, downs, shard_units, top):
    units, model_width = downs.shape
    local_experts = units // shard_units
    pieces_in = [piece.shape[0] for piece in pieces]
    total = sum(pieces_in)
    packed = pieces[0].shape[1]
    resident = pl.BlockSpec(memory_space=pltpu.VMEM)
    kernel = functools.partial(
        expert_kernel, pieces_in, pieces_out, local_experts, shard_units, model_width, top
    )
    out_rows = [sum(count for _, count in segments) for segments in pieces_out]
    return pl.pallas_call(
        kernel,
        out_shape=[jax.ShapeDtypeStruct((count, model_width), jnp.bfloat16) for count in out_rows],
        in_specs=[pl.BlockSpec(memory_space=pltpu.SMEM)] + [resident] * (len(pieces) + 3),
        out_specs=[resident] * len(out_rows),
        scratch_shapes=[
            pltpu.VMEM((total, packed), jnp.bfloat16),
            pltpu.VMEM((total, units), jnp.bfloat16),
        ],
        compiler_params=pltpu.CompilerParams(vmem_limit_bytes=12 * 1024 * 1024),
        cost_estimate=pl.CostEstimate(
            flops=total * model_width, bytes_accessed=total * model_width, transcendentals=0
        ),
        name="experts",
    )(own, *pieces, gates, ups, downs)


def pack_kernel(tokens_ref, experts_ref, weights_ref, packed_ref):
    model_width = tokens_ref.shape[1]
    packed_ref[:, :model_width] = tokens_ref[...]
    weights = weights_ref[...]
    high = weights.astype(jnp.bfloat16).astype(jnp.float32)
    listed = jnp.concatenate([experts_ref[...].astype(jnp.float32), high, weights - high], axis=0)
    width = packed_ref.shape[1] - model_width
    place = lax.broadcasted_iota(jnp.int32, (listed.shape[0], width), 0)
    lane = lax.broadcasted_iota(jnp.int32, (listed.shape[0], width), 1)
    chosen = jnp.where(place == lane, 1.0, 0.0).astype(jnp.bfloat16)
    extra = lax.dot_general(
        listed.astype(jnp.bfloat16),
        chosen,
        (((0,), (0,)), ((), ())),
        preferred_element_type=jnp.float32,
    )
    packed_ref[:, model_width:] = extra.astype(jnp.bfloat16)


def with_routing(tokens, routed_experts, route_weights):
    rows, width = tokens.shape
    return pl.pallas_call(
        pack_kernel,
        out_shape=jax.ShapeDtypeStruct((rows, width + 128), jnp.bfloat16),
        in_specs=[pl.BlockSpec(memory_space=pltpu.VMEM)] * 3,
        out_specs=pl.BlockSpec(memory_space=pltpu.VMEM),
        name="pack",
    )(tokens, routed_experts.T, route_weights.T)


def swap_exp(value, bits):
    owners = lax.axis_size("exp")
    return lax.ppermute(value, "exp", [(i, i ^ bits) for i in range(owners)])


def turn_rep(value, shift):
    replicas = lax.axis_size("rep")
    return lax.ppermute(value, "rep", [(i, (i - shift) % replicas) for i in range(replicas)])


def added(*terms):
    total = terms[0].astype(jnp.float32)
    for term in terms[1:]:
        total = total + term.astype(jnp.float32)
    return total


def rounded(*terms):
    return added(*terms).astype(jnp.bfloat16)


def ordered(*values):
    return lax.optimization_barrier(values)


def segments_of(places, rows):
    other = 8
    cuts = [*places, [other + place for cut in places for place in cut]]
    return [[(place * rows, rows) for place in cut] for cut in cuts]


def cores_added(parts, rows):
    to_x, to_y, to_far, own, other = parts
    back = swap_exp(other, 1)
    sent = [
        rounded(part, back[2 * i * rows : 2 * (i + 1) * rows])
        for i, part in enumerate((to_x, to_y, to_far))
    ]
    return sent, (own, back[6 * rows :])


def crossed(sent):
    return [swap_exp(part, bits) for part, bits in zip(sent, (2, 4, 6))]


def plane_added(kept, arrived, rows):
    return (
        added(*(part[:rows] for part in (*kept, *arrived))),
        added(*(part[rows:] for part in (*kept, *arrived))),
    )


def on_device_dense(tokens, routed_experts, route_weights, gate_weight, up_weight, down_weight):
    local_experts, shard_units, model_width = gate_weight.shape
    units = local_experts * shard_units
    top = routed_experts.shape[1]
    rows = tokens.shape[0]
    gate_weight = gate_weight.reshape(units, model_width)
    up_weight = up_weight.reshape(units, model_width)
    down_weight = down_weight.reshape(units, model_width)
    own = jnp.full((1,), lax.axis_index("exp") * local_experts, jnp.int32)
    tokens, own = ordered(tokens, own)
    packed = with_routing(tokens, routed_experts, route_weights)
    two = turn_rep(packed, 2)
    near_own = [swap_exp(packed, bits) for bits in (2, 4, 6)]
    far_one = turn_rep(packed, 1)
    gates = fetched(gate_weight, True)
    gates, up_weight, again, *near_own, two = ordered(gates, up_weight, packed, *near_own, two)
    near_two = [swap_exp(two, bits) for bits in (2, 4, 6)]
    far_two = turn_rep(again, 3)
    first = gathered(packed, *near_own)
    first_other = swap_exp(first, 1)
    ups = fetched(up_weight, True)
    far_one, far_two, ups, down_weight = ordered(far_one, far_two, ups, down_weight)
    far = gathered(far_one, far_two)
    far_away = [swap_exp(far, bits) for bits in (2, 4, 6)]
    second = gathered(two, *near_two)
    downs = fetched(down_weight, False)
    second, downs = ordered(second, downs)
    near = [first, second, first_other, swap_exp(second, 1)]

    segments = segments_of(([1, 5], [2, 6], [3, 7], [0, 4]), rows)
    parts = experts_of(own, near, segments, gates, ups, downs, shard_units, top)
    *parts, far_x, far_y, far_far = ordered(*parts, *far_away)
    far = [far, far_x, far_y, far_far]
    far = far + [swap_exp(piece, 1) for piece in far]
    sent, near_kept = cores_added(parts, rows)
    near_arrived = crossed(sent)
    *sent, far[0], far[1], far[2], far[3] = ordered(*sent, *far[:4])
    segments = segments_of(([2, 3], [4, 5], [6, 7], [0, 1]), rows)
    parts = experts_of(own, far, segments, gates, ups, downs, shard_units, top)
    *parts, near_x, near_y, near_far = ordered(*parts, *near_arrived)
    sent, far_kept = cores_added(parts, rows)
    far_arrived = crossed(sent)
    near_sums = plane_added(near_kept, (near_x, near_y, near_far), rows)
    far_sums = plane_added(far_kept, far_arrived, rows)
    arrived = [
        turn_rep(near_sums[1].astype(jnp.bfloat16), -2),
        turn_rep(far_sums[0].astype(jnp.bfloat16), -1),
        turn_rep(far_sums[1].astype(jnp.bfloat16), -3),
    ]
    return rounded(near_sums[0], *arrived)


def solution(mesh):
    placed = (
        P(("rep", "exp"), None),
        P(("rep", "exp"), None),
        P(("rep", "exp"), None),
        P("exp", "rep", None),
        P("exp", "rep", None),
        P("exp", "rep", None),
    )
    plane = mesh.shape["exp"] == 8 and mesh.shape["rep"] == 4
    return jax.shard_map(
        on_device_dense if plane else on_device_slots,
        mesh=mesh,
        in_specs=placed,
        out_specs=P(("rep", "exp"), None),
        check_vma=False,
    )
```

```python
import functools

import jax
import jax.numpy as jnp
from jax import lax
from jax.experimental import pallas as pl
from jax.experimental.pallas import tpu as pltpu
from jax.sharding import PartitionSpec as P


def slot_table(experts, expert_count, capacity):
    blocks = experts.shape[0]
    flattened = experts.reshape(blocks, -1)
    onehot = (
        flattened[:, :, None] == jnp.arange(expert_count, dtype=jnp.int32)[None, None, :]
    ).astype(jnp.int32)
    before = jnp.cumsum(onehot, axis=1) - onehot
    position = jnp.sum(before * onehot, axis=2)
    return flattened * capacity + position


def token_picks(slots, top_count, slot_count):
    blocks = slots.shape[0]
    grouped = slots.reshape(blocks, 1, -1, top_count)
    return jnp.any(grouped == jnp.arange(slot_count, dtype=jnp.int32)[None, :, None, None], axis=3)


def routing_column(route_weights, routed_experts):
    as_float = routed_experts.astype(jnp.float32)
    weights_all, experts_all = (
        lax.all_gather(route_weights, "rep", axis=0, tiled=True),
        lax.all_gather(as_float, "rep", axis=0, tiled=True),
    )
    return (weights_all, experts_all.astype(jnp.int32))


def on_device_slots(tokens, routed_experts, route_weights, gate_weight, up_weight, down_weight):
    replicas = lax.axis_size("rep")
    owners = lax.axis_size("exp")
    token_rows, model_width = tokens.shape
    top_count = routed_experts.shape[1]
    local_experts = gate_weight.shape[0]
    expert_count = local_experts * owners
    capacity = max(2, 3 * token_rows * top_count // (2 * expert_count))
    slot_count = expert_count * capacity
    own_slots = slot_table(routed_experts[None], expert_count, capacity)
    column = None
    column_slots = None
    selected = token_picks(own_slots, top_count, slot_count)[0].astype(jnp.bfloat16)
    buffer = jnp.dot(selected, tokens, preferred_element_type=jnp.float32).astype(jnp.bfloat16)
    buffer = buffer.reshape(owners, local_experts, capacity, model_width)
    arrived = lax.all_to_all(buffer, "exp", split_axis=0, concat_axis=2, tiled=True)
    rows_now = lax.all_gather(arrived, "rep", axis=2, tiled=True)[0]
    gate_value = jnp.einsum(
        "emd,efd->emf", rows_now, gate_weight, preferred_element_type=jnp.float32
    )
    up_value = jnp.einsum("emd,efd->emf", rows_now, up_weight, preferred_element_type=jnp.float32)
    hidden = (jax.nn.silu(gate_value) * up_value).astype(jnp.bfloat16)
    outcome = jnp.einsum("emf,efd->emd", hidden, down_weight, preferred_element_type=jnp.float32)
    outcome = lax.optimization_barrier(outcome.astype(jnp.bfloat16))
    outcomes = outcome[None]
    outcomes = outcomes.reshape(local_experts, replicas, owners, capacity, model_width)
    column = routing_column(route_weights, routed_experts)
    column_slots = slot_table(
        column[1].reshape(replicas, token_rows, top_count), expert_count, capacity
    )
    returned = lax.all_to_all(outcomes, "exp", split_axis=2, concat_axis=0, tiled=True)
    returned = returned.reshape(expert_count, replicas, capacity, model_width)
    expert_index = column_slots // capacity
    place_index = column_slots % capacity
    replica_index = jnp.broadcast_to(
        jnp.arange(replicas, dtype=jnp.int32)[:, None], column_slots.shape
    )
    picked = returned[expert_index, replica_index, place_index].astype(jnp.float32)
    column_weights = column[0].reshape(replicas, token_rows, top_count)
    weighted = jnp.sum(
        picked.reshape(replicas, token_rows, top_count, model_width)
        * column_weights[:, :, :, None],
        axis=2,
    )
    summed = lax.psum_scatter(weighted, "rep", scatter_dimension=0, tiled=True)
    return summed.reshape(token_rows, model_width).astype(jnp.bfloat16)


def fetch_kernel(turn, source_ref, result_ref):
    rows, width = source_ref.shape
    block = 512

    def fetch_block(step, carry):
        span = pl.ds(pl.multiple_of(step * block, block), block)
        if turn:
            for part in range(0, rows, 128):
                result_ref[span, part : part + 128] = source_ref[part : part + 128, span].T
        else:
            result_ref[:, span] = source_ref[:, span]
        return carry

    lax.fori_loop(0, width // block, fetch_block, 0)


def fetched(weight, turn):
    rows, width = weight.shape
    return pl.pallas_call(
        functools.partial(fetch_kernel, turn),
        out_shape=jax.ShapeDtypeStruct((width, rows) if turn else (rows, width), jnp.bfloat16),
        in_specs=[pl.BlockSpec(memory_space=pltpu.VMEM)],
        out_specs=pl.BlockSpec(memory_space=pltpu.VMEM),
        compiler_params=pltpu.CompilerParams(vmem_limit_bytes=4 * 1024 * 1024),
        cost_estimate=pl.CostEstimate(
            flops=0, bytes_accessed=4 * rows * width, transcendentals=0
        ),
        name="fetch_turned" if turn else "fetch",
    )(weight)


def gather_kernel(*refs):
    *pieces, whole_ref = refs
    start = 0
    for piece_ref in pieces:
        count = piece_ref.shape[0]
        whole_ref[start : start + count, :] = piece_ref[...]
        start += count


def gathered(*pieces):
    rows = sum(piece.shape[0] for piece in pieces)
    resident = pl.BlockSpec(memory_space=pltpu.VMEM)
    return pl.pallas_call(
        gather_kernel,
        out_shape=jax.ShapeDtypeStruct((rows, pieces[0].shape[1]), jnp.bfloat16),
        in_specs=[resident] * len(pieces),
        out_specs=resident,
        compiler_params=pltpu.CompilerParams(vmem_limit_bytes=2 * 1024 * 1024),
        name="gather",
    )(*pieces)


def expert_kernel(pieces_in, pieces_out, local_experts, shard_units, model_width, top, *refs):
    own_ref, refs = refs[0], refs[1:]
    ins, refs = refs[: len(pieces_in)], refs[len(pieces_in) :]
    (gate_ref, up_ref, down_ref), refs = refs[:3], refs[3:]
    outs, refs = refs[: len(pieces_out)], refs[len(pieces_out) :]
    rows, hidden = refs
    units = local_experts * shard_units
    unit_block = 256 if units % 256 == 0 else 128
    block = 512

    start = 0
    for place, count in enumerate(pieces_in):
        rows[start : start + count, :] = ins[place][...]
        start += count

    extra = rows[:, model_width:].astype(jnp.float32)
    width = extra.shape[1]
    scale = pltpu.roll(extra, width - top, 1) + pltpu.roll(extra, width - 2 * top, 1)
    lane = lax.broadcasted_iota(jnp.int32, extra.shape, 1)
    weights = []
    for expert in range(local_experts):
        name = (own_ref[0] + expert).astype(jnp.float32)
        chosen = jnp.logical_and(lane < top, extra == name)
        weights.append(jnp.sum(jnp.where(chosen, scale, 0.0), axis=1, keepdims=True))

    for begin in range(0, units, unit_block):
        span = slice(begin, begin + unit_block)
        values = rows[:, :model_width]
        gate = jnp.dot(values, gate_ref[:, span], preferred_element_type=jnp.float32)
        up = jnp.dot(values, up_ref[:, span], preferred_element_type=jnp.float32)
        unit = begin + lax.broadcasted_iota(jnp.int32, gate.shape, 1)
        weight = weights[begin // shard_units]
        for expert in range(begin // shard_units + 1, (begin + unit_block - 1) // shard_units + 1):
            weight = jnp.where(unit >= expert * shard_units, weights[expert], weight)
        active = gate / (1.0 + jnp.exp(-gate)) * up * weight
        hidden[:, span] = active.astype(jnp.bfloat16)

    for begin in range(0, model_width, block):
        span = slice(begin, begin + block)
        value = jnp.dot(hidden[...], down_ref[:, span], preferred_element_type=jnp.float32)
        value = value.astype(jnp.bfloat16)
        for place, segments in enumerate(pieces_out):
            filled = 0
            for first, count in segments:
                outs[place][filled : filled + count, span] = value[first : first + count]
                filled += count


def experts_of(own, pieces, pieces_out, gates, ups, downs, shard_units, top):
    units, model_width = downs.shape
    local_experts = units // shard_units
    pieces_in = [piece.shape[0] for piece in pieces]
    total = sum(pieces_in)
    packed = pieces[0].shape[1]
    resident = pl.BlockSpec(memory_space=pltpu.VMEM)
    kernel = functools.partial(
        expert_kernel, pieces_in, pieces_out, local_experts, shard_units, model_width, top
    )
    out_rows = [sum(count for _, count in segments) for segments in pieces_out]
    return pl.pallas_call(
        kernel,
        out_shape=[jax.ShapeDtypeStruct((count, model_width), jnp.bfloat16) for count in out_rows],
        in_specs=[pl.BlockSpec(memory_space=pltpu.SMEM)] + [resident] * (len(pieces) + 3),
        out_specs=[resident] * len(out_rows),
        scratch_shapes=[
            pltpu.VMEM((total, packed), jnp.bfloat16),
            pltpu.VMEM((total, units), jnp.bfloat16),
        ],
        compiler_params=pltpu.CompilerParams(vmem_limit_bytes=12 * 1024 * 1024),
        cost_estimate=pl.CostEstimate(
            flops=6 * total * units * model_width,
            bytes_accessed=4 * total * model_width,
            transcendentals=total * units,
        ),
        name="experts",
    )(own, *pieces, gates, ups, downs)


def pack_kernel(tokens_ref, experts_ref, weights_ref, packed_ref):
    model_width = tokens_ref.shape[1]
    packed_ref[:, :model_width] = tokens_ref[...]
    weights = weights_ref[...]
    high = weights.astype(jnp.bfloat16).astype(jnp.float32)
    listed = jnp.concatenate([experts_ref[...].astype(jnp.float32), high, weights - high], axis=0)
    width = packed_ref.shape[1] - model_width
    place = lax.broadcasted_iota(jnp.int32, (listed.shape[0], width), 0)
    lane = lax.broadcasted_iota(jnp.int32, (listed.shape[0], width), 1)
    chosen = jnp.where(place == lane, 1.0, 0.0).astype(jnp.bfloat16)
    extra = lax.dot_general(
        listed.astype(jnp.bfloat16),
        chosen,
        (((0,), (0,)), ((), ())),
        preferred_element_type=jnp.float32,
    )
    packed_ref[:, model_width:] = extra.astype(jnp.bfloat16)


def with_routing(tokens, routed_experts, route_weights):
    rows, width = tokens.shape
    return pl.pallas_call(
        pack_kernel,
        out_shape=jax.ShapeDtypeStruct((rows, width + 128), jnp.bfloat16),
        in_specs=[pl.BlockSpec(memory_space=pltpu.VMEM)] * 3,
        out_specs=pl.BlockSpec(memory_space=pltpu.VMEM),
        name="pack",
    )(tokens, routed_experts.T, route_weights.T)


def swap_exp(value, bits):
    owners = lax.axis_size("exp")
    return lax.ppermute(value, "exp", [(i, i ^ bits) for i in range(owners)])


def turn_rep(value, shift):
    replicas = lax.axis_size("rep")
    return lax.ppermute(value, "rep", [(i, (i - shift) % replicas) for i in range(replicas)])


def added(*terms):
    total = terms[0].astype(jnp.float32)
    for term in terms[1:]:
        total = total + term.astype(jnp.float32)
    return total


def rounded(*terms):
    return added(*terms).astype(jnp.bfloat16)


def ordered(*values):
    return lax.optimization_barrier(values)


def segments_of(places, rows):
    other = 8
    cuts = [*places, *([other + place for place in cut] for cut in places)]
    return [[(place * rows, rows) for place in cut] for cut in cuts]


def cores_added(parts):
    back = [swap_exp(part, 1) for part in parts[4:7]]
    sent = [rounded(part, other) for part, other in zip(parts[:3], back)]
    *sent, other = ordered(*sent, parts[7])
    return sent, (parts[3], swap_exp(other, 1))


def crossed(sent):
    return [swap_exp(part, bits) for part, bits in zip(sent, (2, 4, 6))]


def plane_added(kept, arrived, rows):
    return (
        added(*(part[:rows] for part in (*kept, *arrived))),
        added(*(part[rows:] for part in (*kept, *arrived))),
    )


def on_device_dense(tokens, routed_experts, route_weights, gate_weight, up_weight, down_weight):
    local_experts, shard_units, model_width = gate_weight.shape
    units = local_experts * shard_units
    top = routed_experts.shape[1]
    rows = tokens.shape[0]
    gate_weight = gate_weight.reshape(units, model_width)
    up_weight = up_weight.reshape(units, model_width)
    down_weight = down_weight.reshape(units, model_width)
    own = jnp.full((1,), lax.axis_index("exp") * local_experts, jnp.int32)
    tokens, own = ordered(tokens, own)
    packed = with_routing(tokens, routed_experts, route_weights)
    two = turn_rep(packed, 2)
    near_own = [swap_exp(packed, bits) for bits in (2, 4, 6)]
    two, gate_weight, up_weight, again = ordered(two, gate_weight, up_weight, packed)
    near_two = [swap_exp(two, bits) for bits in (2, 4, 6)]
    far_one, far_two = turn_rep(again, 1), turn_rep(again, 3)
    first = gathered(packed, *near_own)
    first_other = swap_exp(first, 1)
    gates, ups = fetched(gate_weight, True), fetched(up_weight, True)
    far_one, far_two, gates, ups, down_weight = ordered(
        far_one, far_two, gates, ups, down_weight
    )
    far = gathered(far_one, far_two)
    far_away = [swap_exp(far, bits) for bits in (2, 4, 6)]
    second = gathered(two, *near_two)
    downs = fetched(down_weight, False)
    second, downs = ordered(second, downs)
    near = [first, second, first_other, swap_exp(second, 1)]

    segments = segments_of(([1, 5], [2, 6], [3, 7], [0, 4]), rows)
    parts = list(experts_of(own, near, segments, gates, ups, downs, shard_units, top))
    parts[3], *far_away = ordered(parts[3], *far_away)
    parts[3], far_other = ordered(parts[3], swap_exp(far, 1))
    far = [far, *far_away, far_other, *(swap_exp(piece, 1) for piece in far_away)]
    sent, near_kept = cores_added(parts)
    near_arrived = crossed(sent)
    *sent, far[0], far[1], far[2], far[3] = ordered(*sent, *far[:4])
    segments = segments_of(([2, 3], [4, 5], [6, 7], [0, 1]), rows)
    parts = list(experts_of(own, far, segments, gates, ups, downs, shard_units, top))
    parts[3], *near_arrived = ordered(parts[3], *near_arrived)
    sent, far_kept = cores_added(parts)
    far_arrived = crossed(sent)
    near_sums = plane_added(near_kept, near_arrived, rows)
    far_sums = plane_added(far_kept, far_arrived, rows)
    arrived = [
        turn_rep(near_sums[1].astype(jnp.bfloat16), -2),
        turn_rep(far_sums[0].astype(jnp.bfloat16), -1),
        turn_rep(far_sums[1].astype(jnp.bfloat16), -3),
    ]
    return rounded(near_sums[0], *arrived)


def solution(mesh):
    placed = (
        P(("rep", "exp"), None),
        P(("rep", "exp"), None),
        P(("rep", "exp"), None),
        P("exp", "rep", None),
        P("exp", "rep", None),
        P("exp", "rep", None),
    )
    plane = mesh.shape["exp"] == 8 and mesh.shape["rep"] == 4
    return jax.shard_map(
        on_device_dense if plane else on_device_slots,
        mesh=mesh,
        in_specs=placed,
        out_specs=P(("rep", "exp"), None),
        check_vma=False,
    )
```

```python
import functools

import jax
import jax.numpy as jnp
from jax import lax
from jax.experimental import pallas as pl
from jax.experimental.pallas import tpu as pltpu
from jax.sharding import PartitionSpec as P


def slot_table(experts, expert_count, capacity):
    blocks = experts.shape[0]
    flattened = experts.reshape(blocks, -1)
    onehot = (
        flattened[:, :, None] == jnp.arange(expert_count, dtype=jnp.int32)[None, None, :]
    ).astype(jnp.int32)
    before = jnp.cumsum(onehot, axis=1) - onehot
    position = jnp.sum(before * onehot, axis=2)
    return flattened * capacity + position


def token_picks(slots, top_count, slot_count):
    blocks = slots.shape[0]
    grouped = slots.reshape(blocks, 1, -1, top_count)
    return jnp.any(grouped == jnp.arange(slot_count, dtype=jnp.int32)[None, :, None, None], axis=3)


def routing_column(route_weights, routed_experts):
    as_float = routed_experts.astype(jnp.float32)
    weights_all, experts_all = (
        lax.all_gather(route_weights, "rep", axis=0, tiled=True),
        lax.all_gather(as_float, "rep", axis=0, tiled=True),
    )
    return (weights_all, experts_all.astype(jnp.int32))


def on_device_slots(tokens, routed_experts, route_weights, gate_weight, up_weight, down_weight):
    replicas = lax.axis_size("rep")
    owners = lax.axis_size("exp")
    token_rows, model_width = tokens.shape
    top_count = routed_experts.shape[1]
    local_experts = gate_weight.shape[0]
    expert_count = local_experts * owners
    capacity = max(2, 3 * token_rows * top_count // (2 * expert_count))
    slot_count = expert_count * capacity
    own_slots = slot_table(routed_experts[None], expert_count, capacity)
    column = None
    column_slots = None
    selected = token_picks(own_slots, top_count, slot_count)[0].astype(jnp.bfloat16)
    buffer = jnp.dot(selected, tokens, preferred_element_type=jnp.float32).astype(jnp.bfloat16)
    buffer = buffer.reshape(owners, local_experts, capacity, model_width)
    arrived = lax.all_to_all(buffer, "exp", split_axis=0, concat_axis=2, tiled=True)
    rows_now = lax.all_gather(arrived, "rep", axis=2, tiled=True)[0]
    gate_value = jnp.einsum(
        "emd,efd->emf", rows_now, gate_weight, preferred_element_type=jnp.float32
    )
    up_value = jnp.einsum("emd,efd->emf", rows_now, up_weight, preferred_element_type=jnp.float32)
    hidden = (jax.nn.silu(gate_value) * up_value).astype(jnp.bfloat16)
    outcome = jnp.einsum("emf,efd->emd", hidden, down_weight, preferred_element_type=jnp.float32)
    outcome = lax.optimization_barrier(outcome.astype(jnp.bfloat16))
    outcomes = outcome[None]
    outcomes = outcomes.reshape(local_experts, replicas, owners, capacity, model_width)
    column = routing_column(route_weights, routed_experts)
    column_slots = slot_table(
        column[1].reshape(replicas, token_rows, top_count), expert_count, capacity
    )
    returned = lax.all_to_all(outcomes, "exp", split_axis=2, concat_axis=0, tiled=True)
    returned = returned.reshape(expert_count, replicas, capacity, model_width)
    expert_index = column_slots // capacity
    place_index = column_slots % capacity
    replica_index = jnp.broadcast_to(
        jnp.arange(replicas, dtype=jnp.int32)[:, None], column_slots.shape
    )
    picked = returned[expert_index, replica_index, place_index].astype(jnp.float32)
    column_weights = column[0].reshape(replicas, token_rows, top_count)
    weighted = jnp.sum(
        picked.reshape(replicas, token_rows, top_count, model_width)
        * column_weights[:, :, :, None],
        axis=2,
    )
    summed = lax.psum_scatter(weighted, "rep", scatter_dimension=0, tiled=True)
    return summed.reshape(token_rows, model_width).astype(jnp.bfloat16)


def fetch_kernel(turn, source_ref, result_ref):
    rows, width = source_ref.shape
    block = 512

    def fetch_block(step, carry):
        span = pl.ds(pl.multiple_of(step * block, block), block)
        if turn:
            for part in range(0, rows, 128):
                result_ref[span, part : part + 128] = source_ref[part : part + 128, span].T
        else:
            result_ref[:, span] = source_ref[:, span]
        return carry

    lax.fori_loop(0, width // block, fetch_block, 0)


def fetched(weight, turn):
    rows, width = weight.shape
    return pl.pallas_call(
        functools.partial(fetch_kernel, turn),
        out_shape=jax.ShapeDtypeStruct((width, rows) if turn else (rows, width), jnp.bfloat16),
        in_specs=[pl.BlockSpec(memory_space=pltpu.VMEM)],
        out_specs=pl.BlockSpec(memory_space=pltpu.VMEM),
        compiler_params=pltpu.CompilerParams(vmem_limit_bytes=4 * 1024 * 1024),
        cost_estimate=pl.CostEstimate(
            flops=0, bytes_accessed=4 * rows * width, transcendentals=0
        ),
        name="fetch_turned" if turn else "fetch",
    )(weight)


def gather_kernel(*refs):
    *pieces, whole_ref = refs
    start = 0
    for piece_ref in pieces:
        count = piece_ref.shape[0]
        whole_ref[start : start + count, :] = piece_ref[...]
        start += count


def gathered(*pieces):
    rows = sum(piece.shape[0] for piece in pieces)
    resident = pl.BlockSpec(memory_space=pltpu.VMEM)
    return pl.pallas_call(
        gather_kernel,
        out_shape=jax.ShapeDtypeStruct((rows, pieces[0].shape[1]), jnp.bfloat16),
        in_specs=[resident] * len(pieces),
        out_specs=resident,
        compiler_params=pltpu.CompilerParams(vmem_limit_bytes=2 * 1024 * 1024),
        name="gather",
    )(*pieces)


def expert_kernel(pieces_in, pieces_out, local_experts, shard_units, model_width, top, *refs):
    own_ref, refs = refs[0], refs[1:]
    ins, refs = refs[: len(pieces_in)], refs[len(pieces_in) :]
    (gate_ref, up_ref, down_ref), refs = refs[:3], refs[3:]
    outs, refs = refs[: len(pieces_out)], refs[len(pieces_out) :]
    rows, hidden = refs
    units = local_experts * shard_units
    unit_block = 256 if units % 256 == 0 else 128
    block = 512

    start = 0
    for place, count in enumerate(pieces_in):
        rows[start : start + count, :] = ins[place][...]
        start += count

    extra = rows[:, model_width:].astype(jnp.float32)
    width = extra.shape[1]
    scale = pltpu.roll(extra, width - top, 1) + pltpu.roll(extra, width - 2 * top, 1)
    lane = lax.broadcasted_iota(jnp.int32, extra.shape, 1)
    weights = []
    for expert in range(local_experts):
        name = (own_ref[0] + expert).astype(jnp.float32)
        chosen = jnp.logical_and(lane < top, extra == name)
        weights.append(jnp.sum(jnp.where(chosen, scale, 0.0), axis=1, keepdims=True))

    for begin in range(0, units, unit_block):
        span = slice(begin, begin + unit_block)
        values = rows[:, :model_width]
        gate = jnp.dot(values, gate_ref[:, span], preferred_element_type=jnp.float32)
        up = jnp.dot(values, up_ref[:, span], preferred_element_type=jnp.float32)
        unit = begin + lax.broadcasted_iota(jnp.int32, gate.shape, 1)
        weight = weights[begin // shard_units]
        for expert in range(begin // shard_units + 1, (begin + unit_block - 1) // shard_units + 1):
            weight = jnp.where(unit >= expert * shard_units, weights[expert], weight)
        active = gate / (1.0 + jnp.exp(-gate)) * up * weight
        hidden[:, span] = active.astype(jnp.bfloat16)

    for begin in range(0, model_width, block):
        span = slice(begin, begin + block)
        value = jnp.dot(hidden[...], down_ref[:, span], preferred_element_type=jnp.float32)
        value = value.astype(jnp.bfloat16)
        for place, segments in enumerate(pieces_out):
            filled = 0
            for first, count in segments:
                outs[place][filled : filled + count, span] = value[first : first + count]
                filled += count


def experts_of(own, pieces, pieces_out, gates, ups, downs, shard_units, top):
    units, model_width = downs.shape
    local_experts = units // shard_units
    pieces_in = [piece.shape[0] for piece in pieces]
    total = sum(pieces_in)
    packed = pieces[0].shape[1]
    resident = pl.BlockSpec(memory_space=pltpu.VMEM)
    kernel = functools.partial(
        expert_kernel, pieces_in, pieces_out, local_experts, shard_units, model_width, top
    )
    out_rows = [sum(count for _, count in segments) for segments in pieces_out]
    return pl.pallas_call(
        kernel,
        out_shape=[jax.ShapeDtypeStruct((count, model_width), jnp.bfloat16) for count in out_rows],
        in_specs=[pl.BlockSpec(memory_space=pltpu.SMEM)] + [resident] * (len(pieces) + 3),
        out_specs=[resident] * len(out_rows),
        scratch_shapes=[
            pltpu.VMEM((total, packed), jnp.bfloat16),
            pltpu.VMEM((total, units), jnp.bfloat16),
        ],
        compiler_params=pltpu.CompilerParams(vmem_limit_bytes=12 * 1024 * 1024),
        cost_estimate=pl.CostEstimate(
            flops=6 * total * units * model_width,
            bytes_accessed=4 * total * model_width,
            transcendentals=total * units,
        ),
        name="experts",
    )(own, *pieces, gates, ups, downs)


def pack_kernel(tokens_ref, experts_ref, weights_ref, packed_ref):
    model_width = tokens_ref.shape[1]
    packed_ref[:, :model_width] = tokens_ref[...]
    weights = weights_ref[...]
    high = weights.astype(jnp.bfloat16).astype(jnp.float32)
    listed = jnp.concatenate([experts_ref[...].astype(jnp.float32), high, weights - high], axis=0)
    width = packed_ref.shape[1] - model_width
    place = lax.broadcasted_iota(jnp.int32, (listed.shape[0], width), 0)
    lane = lax.broadcasted_iota(jnp.int32, (listed.shape[0], width), 1)
    chosen = jnp.where(place == lane, 1.0, 0.0).astype(jnp.bfloat16)
    extra = lax.dot_general(
        listed.astype(jnp.bfloat16),
        chosen,
        (((0,), (0,)), ((), ())),
        preferred_element_type=jnp.float32,
    )
    packed_ref[:, model_width:] = extra.astype(jnp.bfloat16)


def with_routing(tokens, routed_experts, route_weights):
    rows, width = tokens.shape
    return pl.pallas_call(
        pack_kernel,
        out_shape=jax.ShapeDtypeStruct((rows, width + 128), jnp.bfloat16),
        in_specs=[pl.BlockSpec(memory_space=pltpu.VMEM)] * 3,
        out_specs=pl.BlockSpec(memory_space=pltpu.VMEM),
        name="pack",
    )(tokens, routed_experts.T, route_weights.T)


def swap_exp(value, bits):
    owners = lax.axis_size("exp")
    return lax.ppermute(value, "exp", [(i, i ^ bits) for i in range(owners)])


def turn_rep(value, shift):
    replicas = lax.axis_size("rep")
    return lax.ppermute(value, "rep", [(i, (i - shift) % replicas) for i in range(replicas)])


def added(*terms):
    total = terms[0].astype(jnp.float32)
    for term in terms[1:]:
        total = total + term.astype(jnp.float32)
    return total


def rounded(*terms):
    return added(*terms).astype(jnp.bfloat16)


def ordered(*values):
    return lax.optimization_barrier(values)


def row_groups(places, rows):
    return [[(place * rows, rows) for place in group] for group in places]


def on_device_dense(tokens, routed_experts, route_weights, gate_weight, up_weight, down_weight):
    local_experts, shard_units, model_width = gate_weight.shape
    units = local_experts * shard_units
    top = routed_experts.shape[1]
    rows = tokens.shape[0]
    gate_weight = gate_weight.reshape(units, model_width)
    up_weight = up_weight.reshape(units, model_width)
    down_weight = down_weight.reshape(units, model_width)
    own = jnp.full((1,), lax.axis_index("exp") * local_experts, jnp.int32)
    tokens, own = ordered(tokens, own)
    packed = with_routing(tokens, routed_experts, route_weights)

    two = turn_rep(packed, 2)
    x_own, y_own, far_own = [swap_exp(packed, bits) for bits in (2, 4, 6)]
    one, three = turn_rep(packed, 1), turn_rep(packed, 3)
    gates = fetched(gate_weight, True)
    two, far_own, y_own, x_own, gates, up_weight = ordered(
        two, far_own, y_own, x_own, gates, up_weight
    )
    x_two, y_two, far_two = [swap_exp(two, bits) for bits in (2, 4, 6)]
    far_one, far_three = turn_rep(far_own, 1), turn_rep(far_own, 3)
    first = gathered(packed, x_own, y_own, far_own)
    first_other = swap_exp(first, 1)
    ups = fetched(up_weight, True)
    one, three, ups, down_weight = ordered(one, three, ups, down_weight)
    pair = gathered(one, three)
    x_pair, y_pair = swap_exp(pair, 2), swap_exp(pair, 4)
    second = gathered(two, x_two, y_two, far_two)
    downs = fetched(down_weight, False)
    second, downs, far_one, far_three = ordered(second, downs, far_one, far_three)

    near = [first, second, first_other, swap_exp(second, 1)]
    groups = row_groups([[5, 1], [6, 2], [7], [13, 9, 14, 10, 15], [4, 0, 3], [12, 8, 11]], rows)
    parts = experts_of(own, near, groups, gates, ups, downs, shard_units, top)
    *parts, x_pair, y_pair = ordered(*parts, x_pair, y_pair)
    to_x, to_y, to_far, other, near_kept, near_other = parts
    back = swap_exp(other, 1)
    to_x = rounded(to_x, back[: 2 * rows])
    to_y = rounded(to_y, back[2 * rows : 4 * rows])
    to_far = rounded(to_far, back[4 * rows :])
    to_x, to_y, to_far, near_other = ordered(to_x, to_y, to_far, near_other)
    near_x, near_y, near_far = swap_exp(to_x, 2), swap_exp(to_y, 4), swap_exp(to_far, 6)
    near_back = swap_exp(near_other, 1)

    far = [pair, x_pair, y_pair, far_one, far_three]
    far = far + [swap_exp(piece, 1) for piece in far]
    to_x, to_y, to_far, *far = ordered(to_x, to_y, to_far, *far)
    groups = row_groups([[6], [7], [2, 3], [4, 5], [14, 15, 10, 11, 12, 13, 8, 9], [0, 1]], rows)
    parts = experts_of(own, far, groups, gates, ups, downs, shard_units, top)
    to_one, to_three, to_x, to_y, other, far_kept = parts
    far_kept, near_x, near_y, near_far = ordered(far_kept, near_x, near_y, near_far)
    back = swap_exp(other, 1)
    to_one, to_three = rounded(to_one, back[:rows]), rounded(to_three, back[rows : 2 * rows])
    to_x = rounded(to_x, back[2 * rows : 4 * rows])
    to_y = rounded(to_y, back[4 * rows : 6 * rows])
    kept = added(near_kept, near_back)
    to_two = rounded(kept[:rows], near_x[:rows], near_y[:rows], near_far)
    to_two, to_one, to_three = ordered(to_two, to_one, to_three)
    from_two = turn_rep(to_two, -2)
    from_one, from_three = turn_rep(to_one, -1), turn_rep(to_three, -3)
    far_x, far_y = swap_exp(to_x, 2), swap_exp(to_y, 4)

    own_sum = kept[rows : 2 * rows] + added(near_x[rows:], near_y[rows:])
    to_far = (kept[2 * rows :] + added(from_one, from_three)).astype(jnp.bfloat16)
    from_far = swap_exp(to_far, 6)
    sums = added(far_kept, back[6 * rows :], far_x, far_y).astype(jnp.bfloat16)
    arrived = [turn_rep(sums[:rows], -1), turn_rep(sums[rows:], -3)]
    return rounded(own_sum, from_two, from_far, *arrived)


def solution(mesh):
    placed = (
        P(("rep", "exp"), None),
        P(("rep", "exp"), None),
        P(("rep", "exp"), None),
        P("exp", "rep", None),
        P("exp", "rep", None),
        P("exp", "rep", None),
    )
    plane = mesh.shape["exp"] == 8 and mesh.shape["rep"] == 4
    return jax.shard_map(
        on_device_dense if plane else on_device_slots,
        mesh=mesh,
        in_specs=placed,
        out_specs=P(("rep", "exp"), None),
        check_vma=False,
    )
```

```python
import functools

import jax
import jax.numpy as jnp
from jax import lax
from jax.experimental import pallas as pl
from jax.experimental.pallas import tpu as pltpu
from jax.sharding import PartitionSpec as P


def slot_table(experts, expert_count, capacity):
    blocks = experts.shape[0]
    flattened = experts.reshape(blocks, -1)
    onehot = (
        flattened[:, :, None] == jnp.arange(expert_count, dtype=jnp.int32)[None, None, :]
    ).astype(jnp.int32)
    before = jnp.cumsum(onehot, axis=1) - onehot
    position = jnp.sum(before * onehot, axis=2)
    return flattened * capacity + position


def token_picks(slots, top_count, slot_count):
    blocks = slots.shape[0]
    grouped = slots.reshape(blocks, 1, -1, top_count)
    return jnp.any(grouped == jnp.arange(slot_count, dtype=jnp.int32)[None, :, None, None], axis=3)


def routing_column(route_weights, routed_experts):
    as_float = routed_experts.astype(jnp.float32)
    weights_all, experts_all = (
        lax.all_gather(route_weights, "rep", axis=0, tiled=True),
        lax.all_gather(as_float, "rep", axis=0, tiled=True),
    )
    return (weights_all, experts_all.astype(jnp.int32))


def on_device_slots(tokens, routed_experts, route_weights, gate_weight, up_weight, down_weight):
    replicas = lax.axis_size("rep")
    owners = lax.axis_size("exp")
    token_rows, model_width = tokens.shape
    top_count = routed_experts.shape[1]
    local_experts = gate_weight.shape[0]
    expert_count = local_experts * owners
    capacity = max(2, 3 * token_rows * top_count // (2 * expert_count))
    slot_count = expert_count * capacity
    own_slots = slot_table(routed_experts[None], expert_count, capacity)
    column = None
    column_slots = None
    selected = token_picks(own_slots, top_count, slot_count)[0].astype(jnp.bfloat16)
    buffer = jnp.dot(selected, tokens, preferred_element_type=jnp.float32).astype(jnp.bfloat16)
    buffer = buffer.reshape(owners, local_experts, capacity, model_width)
    arrived = lax.all_to_all(buffer, "exp", split_axis=0, concat_axis=2, tiled=True)
    rows_now = lax.all_gather(arrived, "rep", axis=2, tiled=True)[0]
    gate_value = jnp.einsum(
        "emd,efd->emf", rows_now, gate_weight, preferred_element_type=jnp.float32
    )
    up_value = jnp.einsum("emd,efd->emf", rows_now, up_weight, preferred_element_type=jnp.float32)
    hidden = (jax.nn.silu(gate_value) * up_value).astype(jnp.bfloat16)
    outcome = jnp.einsum("emf,efd->emd", hidden, down_weight, preferred_element_type=jnp.float32)
    outcome = lax.optimization_barrier(outcome.astype(jnp.bfloat16))
    outcomes = outcome[None]
    outcomes = outcomes.reshape(local_experts, replicas, owners, capacity, model_width)
    column = routing_column(route_weights, routed_experts)
    column_slots = slot_table(
        column[1].reshape(replicas, token_rows, top_count), expert_count, capacity
    )
    returned = lax.all_to_all(outcomes, "exp", split_axis=2, concat_axis=0, tiled=True)
    returned = returned.reshape(expert_count, replicas, capacity, model_width)
    expert_index = column_slots // capacity
    place_index = column_slots % capacity
    replica_index = jnp.broadcast_to(
        jnp.arange(replicas, dtype=jnp.int32)[:, None], column_slots.shape
    )
    picked = returned[expert_index, replica_index, place_index].astype(jnp.float32)
    column_weights = column[0].reshape(replicas, token_rows, top_count)
    weighted = jnp.sum(
        picked.reshape(replicas, token_rows, top_count, model_width)
        * column_weights[:, :, :, None],
        axis=2,
    )
    summed = lax.psum_scatter(weighted, "rep", scatter_dimension=0, tiled=True)
    return summed.reshape(token_rows, model_width).astype(jnp.bfloat16)


def fetch_kernel(turn, source_ref, result_ref):
    rows, width = source_ref.shape
    block = 512

    def fetch_block(step, carry):
        span = pl.ds(pl.multiple_of(step * block, block), block)
        if turn:
            for part in range(0, rows, 128):
                result_ref[span, part : part + 128] = source_ref[part : part + 128, span].T
        else:
            result_ref[:, span] = source_ref[:, span]
        return carry

    lax.fori_loop(0, width // block, fetch_block, 0)


def fetched(weight, turn):
    rows, width = weight.shape
    return pl.pallas_call(
        functools.partial(fetch_kernel, turn),
        out_shape=jax.ShapeDtypeStruct((width, rows) if turn else (rows, width), jnp.bfloat16),
        in_specs=[pl.BlockSpec(memory_space=pltpu.VMEM)],
        out_specs=pl.BlockSpec(memory_space=pltpu.VMEM),
        compiler_params=pltpu.CompilerParams(vmem_limit_bytes=4 * 1024 * 1024),
        cost_estimate=pl.CostEstimate(
            flops=0, bytes_accessed=4 * rows * width, transcendentals=0
        ),
        name="fetch_turned" if turn else "fetch",
    )(weight)


def gather_kernel(*refs):
    *pieces, whole_ref = refs
    start = 0
    for piece_ref in pieces:
        count = piece_ref.shape[0]
        whole_ref[start : start + count, :] = piece_ref[...]
        start += count


def gathered(*pieces):
    rows = sum(piece.shape[0] for piece in pieces)
    resident = pl.BlockSpec(memory_space=pltpu.VMEM)
    return pl.pallas_call(
        gather_kernel,
        out_shape=jax.ShapeDtypeStruct((rows, pieces[0].shape[1]), jnp.bfloat16),
        in_specs=[resident] * len(pieces),
        out_specs=resident,
        compiler_params=pltpu.CompilerParams(vmem_limit_bytes=2 * 1024 * 1024),
        name="gather",
    )(*pieces)


def expert_kernel(pieces_in, pieces_out, local_experts, shard_units, model_width, top, *refs):
    own_ref, refs = refs[0], refs[1:]
    ins, refs = refs[: len(pieces_in)], refs[len(pieces_in) :]
    (gate_ref, up_ref, down_ref), refs = refs[:3], refs[3:]
    outs, refs = refs[: len(pieces_out)], refs[len(pieces_out) :]
    rows, hidden = refs
    units = local_experts * shard_units
    unit_block = 256 if units % 256 == 0 else 128
    block = 512

    start = 0
    for place, count in enumerate(pieces_in):
        rows[start : start + count, :] = ins[place][...]
        start += count

    extra = rows[:, model_width:].astype(jnp.float32)
    width = extra.shape[1]
    scale = pltpu.roll(extra, width - top, 1) + pltpu.roll(extra, width - 2 * top, 1)
    lane = lax.broadcasted_iota(jnp.int32, extra.shape, 1)
    weights = []
    for expert in range(local_experts):
        name = (own_ref[0] + expert).astype(jnp.float32)
        chosen = jnp.logical_and(lane < top, extra == name)
        weights.append(jnp.sum(jnp.where(chosen, scale, 0.0), axis=1, keepdims=True))

    for begin in range(0, units, unit_block):
        span = slice(begin, begin + unit_block)
        values = rows[:, :model_width]
        gate = jnp.dot(values, gate_ref[:, span], preferred_element_type=jnp.float32)
        up = jnp.dot(values, up_ref[:, span], preferred_element_type=jnp.float32)
        unit = begin + lax.broadcasted_iota(jnp.int32, gate.shape, 1)
        weight = weights[begin // shard_units]
        for expert in range(begin // shard_units + 1, (begin + unit_block - 1) // shard_units + 1):
            weight = jnp.where(unit >= expert * shard_units, weights[expert], weight)
        active = gate / (1.0 + jnp.exp(-gate)) * up * weight
        hidden[:, span] = active.astype(jnp.bfloat16)

    for begin in range(0, model_width, block):
        span = slice(begin, begin + block)
        value = jnp.dot(hidden[...], down_ref[:, span], preferred_element_type=jnp.float32)
        value = value.astype(jnp.bfloat16)
        for place, segments in enumerate(pieces_out):
            filled = 0
            for first, count in segments:
                outs[place][filled : filled + count, span] = value[first : first + count]
                filled += count


def experts_of(own, pieces, pieces_out, gates, ups, downs, shard_units, top):
    units, model_width = downs.shape
    local_experts = units // shard_units
    pieces_in = [piece.shape[0] for piece in pieces]
    total = sum(pieces_in)
    packed = pieces[0].shape[1]
    resident = pl.BlockSpec(memory_space=pltpu.VMEM)
    kernel = functools.partial(
        expert_kernel, pieces_in, pieces_out, local_experts, shard_units, model_width, top
    )
    out_rows = [sum(count for _, count in segments) for segments in pieces_out]
    return pl.pallas_call(
        kernel,
        out_shape=[jax.ShapeDtypeStruct((count, model_width), jnp.bfloat16) for count in out_rows],
        in_specs=[pl.BlockSpec(memory_space=pltpu.SMEM)] + [resident] * (len(pieces) + 3),
        out_specs=[resident] * len(out_rows),
        scratch_shapes=[
            pltpu.VMEM((total, packed), jnp.bfloat16),
            pltpu.VMEM((total, units), jnp.bfloat16),
        ],
        compiler_params=pltpu.CompilerParams(vmem_limit_bytes=12 * 1024 * 1024),
        cost_estimate=pl.CostEstimate(
            flops=6 * total * units * model_width,
            bytes_accessed=4 * total * model_width,
            transcendentals=total * units,
        ),
        name="experts",
    )(own, *pieces, gates, ups, downs)


def pack_kernel(
    tokens_ref, experts_ref, weights_ref, packed_ref, experts, weights, sems
):
    model_width = tokens_ref.shape[1]
    copies = [
        pltpu.make_async_copy(experts_ref, experts, sems.at[0]),
        pltpu.make_async_copy(weights_ref, weights, sems.at[1]),
        pltpu.make_async_copy(tokens_ref, packed_ref.at[:, pl.ds(0, model_width)], sems.at[2]),
    ]
    for copy in copies:
        copy.start()
    copies[0].wait()
    copies[1].wait()
    values = weights[...]
    high = values.astype(jnp.bfloat16).astype(jnp.float32)
    listed = jnp.concatenate([experts[...].astype(jnp.float32), high, values - high], axis=0)
    width = packed_ref.shape[1] - model_width
    place = lax.broadcasted_iota(jnp.int32, (listed.shape[0], width), 0)
    lane = lax.broadcasted_iota(jnp.int32, (listed.shape[0], width), 1)
    chosen = jnp.where(place == lane, 1.0, 0.0).astype(jnp.bfloat16)
    extra = lax.dot_general(
        listed.astype(jnp.bfloat16),
        chosen,
        (((0,), (0,)), ((), ())),
        preferred_element_type=jnp.float32,
    )
    packed_ref[:, model_width:] = extra.astype(jnp.bfloat16)
    copies[2].wait()


def with_routing(tokens, routed_experts, route_weights):
    rows, width = tokens.shape
    top = routed_experts.shape[1]
    return pl.pallas_call(
        pack_kernel,
        out_shape=jax.ShapeDtypeStruct((rows, width + 128), jnp.bfloat16),
        in_specs=[pl.BlockSpec(memory_space=pl.ANY)] * 3,
        out_specs=pl.BlockSpec(memory_space=pltpu.VMEM),
        scratch_shapes=[
            pltpu.VMEM((top, rows), jnp.int32),
            pltpu.VMEM((top, rows), jnp.float32),
            pltpu.SemaphoreType.DMA((3,)),
        ],
        compiler_params=pltpu.CompilerParams(vmem_limit_bytes=2 * 1024 * 1024),
        name="pack",
    )(tokens, routed_experts.T, route_weights.T)


def begin_kernel(own_ref, gate_ref, up_ref, down_ref, index_ref):
    index_ref[0] = own_ref[0]


def begun(own, *weights):
    scalar = pl.BlockSpec(memory_space=pltpu.SMEM)
    return pl.pallas_call(
        begin_kernel,
        out_shape=jax.ShapeDtypeStruct((1,), jnp.int32),
        in_specs=[scalar] + [pl.BlockSpec(memory_space=pl.ANY)] * 3,
        out_specs=scalar,
        compiler_params=pltpu.CompilerParams(vmem_limit_bytes=50 * 1024 * 1024),
        name="begin",
    )(own, *weights)


def swap_exp(value, bits):
    owners = lax.axis_size("exp")
    return lax.ppermute(value, "exp", [(i, i ^ bits) for i in range(owners)])


def turn_rep(value, shift):
    replicas = lax.axis_size("rep")
    return lax.ppermute(value, "rep", [(i, (i - shift) % replicas) for i in range(replicas)])


def added(*terms):
    total = terms[0].astype(jnp.float32)
    for term in terms[1:]:
        total = total + term.astype(jnp.float32)
    return total


def rounded(*terms):
    return added(*terms).astype(jnp.bfloat16)


def ordered(*values):
    return lax.optimization_barrier(values)


def row_groups(places, rows):
    return [[(place * rows, rows) for place in group] for group in places]


def on_device_dense(tokens, routed_experts, route_weights, gate_weight, up_weight, down_weight):
    local_experts, shard_units, model_width = gate_weight.shape
    units = local_experts * shard_units
    top = routed_experts.shape[1]
    rows = tokens.shape[0]
    gate_weight = gate_weight.reshape(units, model_width)
    up_weight = up_weight.reshape(units, model_width)
    down_weight = down_weight.reshape(units, model_width)
    own = jnp.full((1,), lax.axis_index("exp") * local_experts, jnp.int32)
    own = begun(own, gate_weight, up_weight, down_weight)
    tokens, own = ordered(tokens, own)
    packed = with_routing(tokens, routed_experts, route_weights)

    two = turn_rep(packed, 2)
    x_own, y_own, far_own = [swap_exp(packed, bits) for bits in (2, 4, 6)]
    gates = fetched(gate_weight, True)
    x_own, y_own, far_own, two, gates, up_weight, again = ordered(
        x_own, y_own, far_own, two, gates, up_weight, packed
    )
    one, three = turn_rep(again, 1), turn_rep(again, 3)
    x_two, y_two, far_two = [swap_exp(two, bits) for bits in (2, 4, 6)]
    far_one, far_three = turn_rep(far_own, 1), turn_rep(far_own, 3)
    first = gathered(packed, x_own, y_own, far_own)
    first_other = swap_exp(first, 1)
    ups = fetched(up_weight, True)
    one, three, ups, down_weight = ordered(one, three, ups, down_weight)
    pair = gathered(one, three)
    x_pair, y_pair = swap_exp(pair, 2), swap_exp(pair, 4)
    second = gathered(two, x_two, y_two, far_two)
    downs = fetched(down_weight, False)
    second, downs = ordered(second, downs)

    near = [first, second, first_other, swap_exp(second, 1)]
    groups = row_groups([[5, 1], [6, 2], [7], [13, 9, 14, 10, 15], [4, 0, 3], [12, 8, 11]], rows)
    parts = experts_of(own, near, groups, gates, ups, downs, shard_units, top)
    *parts, x_pair, y_pair, far_one, far_three = ordered(
        *parts, x_pair, y_pair, far_one, far_three
    )
    to_x, to_y, to_far, other, near_kept, near_other = parts
    back = swap_exp(other, 1)
    to_x = rounded(to_x, back[: 2 * rows])
    to_y = rounded(to_y, back[2 * rows : 4 * rows])
    to_far = rounded(to_far, back[4 * rows :])
    to_x, to_y, to_far, near_other = ordered(to_x, to_y, to_far, near_other)
    near_x, near_y, near_far = swap_exp(to_x, 2), swap_exp(to_y, 4), swap_exp(to_far, 6)
    near_back = swap_exp(near_other, 1)

    far = [pair, x_pair, y_pair, far_one, far_three]
    far = far + [swap_exp(piece, 1) for piece in far]
    to_x, to_y, to_far, *far = ordered(to_x, to_y, to_far, *far)
    groups = row_groups([[6], [7], [2, 3], [4, 5], [14, 15, 10, 11, 12, 13, 8, 9], [0, 1]], rows)
    parts = experts_of(own, far, groups, gates, ups, downs, shard_units, top)
    to_one, to_three, to_x, to_y, other, far_kept = parts
    far_kept, near_x, near_y, near_far = ordered(far_kept, near_x, near_y, near_far)
    back = swap_exp(other, 1)
    to_one, to_three = rounded(to_one, back[:rows]), rounded(to_three, back[rows : 2 * rows])
    to_x = rounded(to_x, back[2 * rows : 4 * rows])
    to_y = rounded(to_y, back[4 * rows : 6 * rows])
    kept = added(near_kept, near_back)
    to_two = rounded(kept[:rows], near_x[:rows], near_y[:rows], near_far)
    to_two, to_one, to_three, to_x, to_y = ordered(to_two, to_one, to_three, to_x, to_y)
    from_two = turn_rep(to_two, -2)
    from_one, from_three = turn_rep(to_one, -1), turn_rep(to_three, -3)
    far_x, far_y = swap_exp(to_x, 2), swap_exp(to_y, 4)

    own_sum = kept[rows : 2 * rows] + added(near_x[rows:], near_y[rows:])
    to_far = (kept[2 * rows :] + added(from_one, from_three)).astype(jnp.bfloat16)
    from_far = swap_exp(to_far, 6)
    sums = added(far_kept, back[6 * rows :], far_x, far_y).astype(jnp.bfloat16)
    arrived = [turn_rep(sums[:rows], -1), turn_rep(sums[rows:], -3)]
    return rounded(own_sum, from_two, from_far, *arrived)


def solution(mesh):
    placed = (
        P(("rep", "exp"), None),
        P(("rep", "exp"), None),
        P(("rep", "exp"), None),
        P("exp", "rep", None),
        P("exp", "rep", None),
        P("exp", "rep", None),
    )
    plane = mesh.shape["exp"] == 8 and mesh.shape["rep"] == 4
    return jax.shard_map(
        on_device_dense if plane else on_device_slots,
        mesh=mesh,
        in_specs=placed,
        out_specs=P(("rep", "exp"), None),
        check_vma=False,
    )
```

```python
import functools

import jax
import jax.numpy as jnp
from jax import lax
from jax.experimental import pallas as pl
from jax.experimental.pallas import tpu as pltpu
from jax.sharding import PartitionSpec as P


def slot_table(experts, expert_count, capacity):
    blocks = experts.shape[0]
    flattened = experts.reshape(blocks, -1)
    onehot = (
        flattened[:, :, None] == jnp.arange(expert_count, dtype=jnp.int32)[None, None, :]
    ).astype(jnp.int32)
    before = jnp.cumsum(onehot, axis=1) - onehot
    position = jnp.sum(before * onehot, axis=2)
    return flattened * capacity + position


def token_picks(slots, top_count, slot_count):
    blocks = slots.shape[0]
    grouped = slots.reshape(blocks, 1, -1, top_count)
    return jnp.any(grouped == jnp.arange(slot_count, dtype=jnp.int32)[None, :, None, None], axis=3)


def routing_column(route_weights, routed_experts):
    as_float = routed_experts.astype(jnp.float32)
    weights_all, experts_all = (
        lax.all_gather(route_weights, "rep", axis=0, tiled=True),
        lax.all_gather(as_float, "rep", axis=0, tiled=True),
    )
    return (weights_all, experts_all.astype(jnp.int32))


def on_device_slots(tokens, routed_experts, route_weights, gate_weight, up_weight, down_weight):
    replicas = lax.axis_size("rep")
    owners = lax.axis_size("exp")
    token_rows, model_width = tokens.shape
    top_count = routed_experts.shape[1]
    local_experts = gate_weight.shape[0]
    expert_count = local_experts * owners
    capacity = max(2, 3 * token_rows * top_count // (2 * expert_count))
    slot_count = expert_count * capacity
    own_slots = slot_table(routed_experts[None], expert_count, capacity)
    column = None
    column_slots = None
    selected = token_picks(own_slots, top_count, slot_count)[0].astype(jnp.bfloat16)
    buffer = jnp.dot(selected, tokens, preferred_element_type=jnp.float32).astype(jnp.bfloat16)
    buffer = buffer.reshape(owners, local_experts, capacity, model_width)
    arrived = lax.all_to_all(buffer, "exp", split_axis=0, concat_axis=2, tiled=True)
    rows_now = lax.all_gather(arrived, "rep", axis=2, tiled=True)[0]
    gate_value = jnp.einsum(
        "emd,efd->emf", rows_now, gate_weight, preferred_element_type=jnp.float32
    )
    up_value = jnp.einsum("emd,efd->emf", rows_now, up_weight, preferred_element_type=jnp.float32)
    hidden = (jax.nn.silu(gate_value) * up_value).astype(jnp.bfloat16)
    outcome = jnp.einsum("emf,efd->emd", hidden, down_weight, preferred_element_type=jnp.float32)
    outcome = lax.optimization_barrier(outcome.astype(jnp.bfloat16))
    outcomes = outcome[None]
    outcomes = outcomes.reshape(local_experts, replicas, owners, capacity, model_width)
    column = routing_column(route_weights, routed_experts)
    column_slots = slot_table(
        column[1].reshape(replicas, token_rows, top_count), expert_count, capacity
    )
    returned = lax.all_to_all(outcomes, "exp", split_axis=2, concat_axis=0, tiled=True)
    returned = returned.reshape(expert_count, replicas, capacity, model_width)
    expert_index = column_slots // capacity
    place_index = column_slots % capacity
    replica_index = jnp.broadcast_to(
        jnp.arange(replicas, dtype=jnp.int32)[:, None], column_slots.shape
    )
    picked = returned[expert_index, replica_index, place_index].astype(jnp.float32)
    column_weights = column[0].reshape(replicas, token_rows, top_count)
    weighted = jnp.sum(
        picked.reshape(replicas, token_rows, top_count, model_width)
        * column_weights[:, :, :, None],
        axis=2,
    )
    summed = lax.psum_scatter(weighted, "rep", scatter_dimension=0, tiled=True)
    return summed.reshape(token_rows, model_width).astype(jnp.bfloat16)


def fetch_kernel(turn, source_ref, result_ref):
    rows, width = source_ref.shape
    block = 512

    def fetch_block(step, carry):
        span = pl.ds(pl.multiple_of(step * block, block), block)
        if turn:
            for part in range(0, rows, 128):
                result_ref[span, part : part + 128] = source_ref[part : part + 128, span].T
        else:
            result_ref[:, span] = source_ref[:, span]
        return carry

    lax.fori_loop(0, width // block, fetch_block, 0)


def fetched(weight, turn):
    rows, width = weight.shape
    return pl.pallas_call(
        functools.partial(fetch_kernel, turn),
        out_shape=jax.ShapeDtypeStruct((width, rows) if turn else (rows, width), jnp.bfloat16),
        in_specs=[pl.BlockSpec(memory_space=pltpu.VMEM)],
        out_specs=pl.BlockSpec(memory_space=pltpu.VMEM),
        compiler_params=pltpu.CompilerParams(vmem_limit_bytes=4 * 1024 * 1024),
        cost_estimate=pl.CostEstimate(
            flops=0, bytes_accessed=4 * rows * width, transcendentals=0
        ),
        name="fetch_turned" if turn else "fetch",
    )(weight)


def gather_kernel(*refs):
    *pieces, whole_ref = refs
    start = 0
    for piece_ref in pieces:
        count = piece_ref.shape[0]
        whole_ref[start : start + count, :] = piece_ref[...]
        start += count


def gathered(*pieces):
    rows = sum(piece.shape[0] for piece in pieces)
    resident = pl.BlockSpec(memory_space=pltpu.VMEM)
    return pl.pallas_call(
        gather_kernel,
        out_shape=jax.ShapeDtypeStruct((rows, pieces[0].shape[1]), jnp.bfloat16),
        in_specs=[resident] * len(pieces),
        out_specs=resident,
        compiler_params=pltpu.CompilerParams(vmem_limit_bytes=2 * 1024 * 1024),
        name="gather",
    )(*pieces)


def expert_kernel(pieces_in, pieces_out, local_experts, shard_units, model_width, top, *refs):
    own_ref, refs = refs[0], refs[1:]
    ins, refs = refs[: len(pieces_in)], refs[len(pieces_in) :]
    (gate_ref, up_ref, down_ref), refs = refs[:3], refs[3:]
    outs, refs = refs[: len(pieces_out)], refs[len(pieces_out) :]
    rows, hidden = refs
    units = local_experts * shard_units
    unit_block = 256 if units % 256 == 0 else 128
    block = 512

    start = 0
    for place, count in enumerate(pieces_in):
        rows[start : start + count, :] = ins[place][...]
        start += count

    extra = rows[:, model_width:].astype(jnp.float32)
    width = extra.shape[1]
    scale = pltpu.roll(extra, width - top, 1) + pltpu.roll(extra, width - 2 * top, 1)
    lane = lax.broadcasted_iota(jnp.int32, extra.shape, 1)
    weights = []
    for expert in range(local_experts):
        name = (own_ref[0] + expert).astype(jnp.float32)
        chosen = jnp.logical_and(lane < top, extra == name)
        weights.append(jnp.sum(jnp.where(chosen, scale, 0.0), axis=1, keepdims=True))

    for begin in range(0, units, unit_block):
        span = slice(begin, begin + unit_block)
        values = rows[:, :model_width]
        gate = jnp.dot(values, gate_ref[:, span], preferred_element_type=jnp.float32)
        up = jnp.dot(values, up_ref[:, span], preferred_element_type=jnp.float32)
        unit = begin + lax.broadcasted_iota(jnp.int32, gate.shape, 1)
        weight = weights[begin // shard_units]
        for expert in range(begin // shard_units + 1, (begin + unit_block - 1) // shard_units + 1):
            weight = jnp.where(unit >= expert * shard_units, weights[expert], weight)
        active = gate / (1.0 + jnp.exp(-gate)) * up * weight
        hidden[:, span] = active.astype(jnp.bfloat16)

    for begin in range(0, model_width, block):
        span = slice(begin, begin + block)
        value = jnp.dot(hidden[...], down_ref[:, span], preferred_element_type=jnp.float32)
        value = value.astype(jnp.bfloat16)
        for place, segments in enumerate(pieces_out):
            filled = 0
            for first, count in segments:
                outs[place][filled : filled + count, span] = value[first : first + count]
                filled += count


def experts_of(own, pieces, pieces_out, gates, ups, downs, shard_units, top):
    units, model_width = downs.shape
    local_experts = units // shard_units
    pieces_in = [piece.shape[0] for piece in pieces]
    total = sum(pieces_in)
    packed = pieces[0].shape[1]
    resident = pl.BlockSpec(memory_space=pltpu.VMEM)
    kernel = functools.partial(
        expert_kernel, pieces_in, pieces_out, local_experts, shard_units, model_width, top
    )
    out_rows = [sum(count for _, count in segments) for segments in pieces_out]
    return pl.pallas_call(
        kernel,
        out_shape=[jax.ShapeDtypeStruct((count, model_width), jnp.bfloat16) for count in out_rows],
        in_specs=[pl.BlockSpec(memory_space=pltpu.SMEM)] + [resident] * (len(pieces) + 3),
        out_specs=[resident] * len(out_rows),
        scratch_shapes=[
            pltpu.VMEM((total, packed), jnp.bfloat16),
            pltpu.VMEM((total, units), jnp.bfloat16),
        ],
        compiler_params=pltpu.CompilerParams(vmem_limit_bytes=12 * 1024 * 1024),
        cost_estimate=pl.CostEstimate(
            flops=6 * total * units * model_width,
            bytes_accessed=4 * total * model_width,
            transcendentals=total * units,
        ),
        name="experts",
    )(own, *pieces, gates, ups, downs)


def pack_kernel(
    tokens_ref, experts_ref, weights_ref, packed_ref, experts, weights, sems
):
    model_width = tokens_ref.shape[1]
    copies = [
        pltpu.make_async_copy(experts_ref, experts, sems.at[0]),
        pltpu.make_async_copy(weights_ref, weights, sems.at[1]),
        pltpu.make_async_copy(tokens_ref, packed_ref.at[:, pl.ds(0, model_width)], sems.at[2]),
    ]
    for copy in copies:
        copy.start()
    copies[0].wait()
    copies[1].wait()
    values = weights[...]
    high = values.astype(jnp.bfloat16).astype(jnp.float32)
    listed = jnp.concatenate([experts[...].astype(jnp.float32), high, values - high], axis=0)
    width = packed_ref.shape[1] - model_width
    place = lax.broadcasted_iota(jnp.int32, (listed.shape[0], width), 0)
    lane = lax.broadcasted_iota(jnp.int32, (listed.shape[0], width), 1)
    chosen = jnp.where(place == lane, 1.0, 0.0).astype(jnp.bfloat16)
    extra = lax.dot_general(
        listed.astype(jnp.bfloat16),
        chosen,
        (((0,), (0,)), ((), ())),
        preferred_element_type=jnp.float32,
    )
    packed_ref[:, model_width:] = extra.astype(jnp.bfloat16)
    copies[2].wait()


def with_routing(tokens, routed_experts, route_weights):
    rows, width = tokens.shape
    top = routed_experts.shape[1]
    return pl.pallas_call(
        pack_kernel,
        out_shape=jax.ShapeDtypeStruct((rows, width + 128), jnp.bfloat16),
        in_specs=[pl.BlockSpec(memory_space=pl.ANY)] * 3,
        out_specs=pl.BlockSpec(memory_space=pltpu.VMEM),
        scratch_shapes=[
            pltpu.VMEM((top, rows), jnp.int32),
            pltpu.VMEM((top, rows), jnp.float32),
            pltpu.SemaphoreType.DMA((3,)),
        ],
        compiler_params=pltpu.CompilerParams(vmem_limit_bytes=2 * 1024 * 1024),
        name="pack",
    )(tokens, routed_experts.T, route_weights.T)


def begin_kernel(own_ref, gate_ref, up_ref, down_ref, index_ref):
    index_ref[0] = own_ref[0]


def begun(own, *weights):
    scalar = pl.BlockSpec(memory_space=pltpu.SMEM)
    return pl.pallas_call(
        begin_kernel,
        out_shape=jax.ShapeDtypeStruct((1,), jnp.int32),
        in_specs=[scalar] + [pl.BlockSpec(memory_space=pl.ANY)] * 3,
        out_specs=scalar,
        compiler_params=pltpu.CompilerParams(vmem_limit_bytes=50 * 1024 * 1024),
        name="begin",
    )(own, *weights)


def swap_exp(value, bits):
    owners = lax.axis_size("exp")
    return lax.ppermute(value, "exp", [(i, i ^ bits) for i in range(owners)])


def turn_rep(value, shift):
    replicas = lax.axis_size("rep")
    return lax.ppermute(value, "rep", [(i, (i - shift) % replicas) for i in range(replicas)])


def added(*terms):
    total = terms[0].astype(jnp.float32)
    for term in terms[1:]:
        total = total + term.astype(jnp.float32)
    return total


def rounded(*terms):
    return added(*terms).astype(jnp.bfloat16)


def ordered(*values):
    return lax.optimization_barrier(values)


def row_groups(places, rows):
    return [[(place * rows, rows) for place in group] for group in places]


def on_device_dense(tokens, routed_experts, route_weights, gate_weight, up_weight, down_weight):
    local_experts, shard_units, model_width = gate_weight.shape
    units = local_experts * shard_units
    top = routed_experts.shape[1]
    rows = tokens.shape[0]
    gate_weight = gate_weight.reshape(units, model_width)
    up_weight = up_weight.reshape(units, model_width)
    down_weight = down_weight.reshape(units, model_width)
    own = jnp.full((1,), lax.axis_index("exp") * local_experts, jnp.int32)
    own = begun(own, gate_weight, up_weight, down_weight)
    tokens, own = ordered(tokens, own)
    packed = with_routing(tokens, routed_experts, route_weights)

    two = turn_rep(packed, 2)
    x_own, y_own, far_own = [swap_exp(packed, bits) for bits in (2, 4, 6)]
    gates, ups = fetched(gate_weight, True), fetched(up_weight, True)
    x_own, y_own, far_own, two, gates, ups, again = ordered(
        x_own, y_own, far_own, two, gates, ups, packed
    )
    one, three = turn_rep(again, 1), turn_rep(again, 3)
    x_two, y_two, far_two = [swap_exp(two, bits) for bits in (2, 4, 6)]
    far_one, far_three = turn_rep(far_own, 1), turn_rep(far_own, 3)
    first = gathered(packed, x_own, y_own, far_own)
    first_other = swap_exp(first, 1)
    second = gathered(two, x_two, y_two, far_two)
    downs = fetched(down_weight, False)
    second, downs, one, three = ordered(second, downs, one, three)
    pair = gathered(one, three)
    x_pair, y_pair = swap_exp(pair, 2), swap_exp(pair, 4)

    near = [first, second, first_other, swap_exp(second, 1)]
    groups = row_groups([[5, 1], [6, 2], [7], [13, 9, 14, 10, 15], [4, 0, 3], [12, 8, 11]], rows)
    parts = experts_of(own, near, groups, gates, ups, downs, shard_units, top)
    *parts, x_pair, y_pair, far_one, far_three = ordered(
        *parts, x_pair, y_pair, far_one, far_three
    )
    to_x, to_y, to_far, other, near_kept, near_other = parts
    back = swap_exp(other, 1)
    to_x = rounded(to_x, back[: 2 * rows])
    to_y = rounded(to_y, back[2 * rows : 4 * rows])
    to_far = rounded(to_far, back[4 * rows :])
    to_x, to_y, to_far, near_other = ordered(to_x, to_y, to_far, near_other)
    near_x, near_y, near_far = swap_exp(to_x, 2), swap_exp(to_y, 4), swap_exp(to_far, 6)
    near_back = swap_exp(near_other, 1)

    far = [pair, x_pair, y_pair, far_one, far_three]
    far = far + [swap_exp(piece, 1) for piece in far]
    to_x, to_y, to_far, *far = ordered(to_x, to_y, to_far, *far)
    groups = row_groups([[6], [7], [2, 3], [4, 5], [14, 15, 10, 11, 12, 13, 8, 9], [0, 1]], rows)
    parts = experts_of(own, far, groups, gates, ups, downs, shard_units, top)
    to_one, to_three, to_x, to_y, other, far_kept = parts
    far_kept, near_x, near_y, near_far = ordered(far_kept, near_x, near_y, near_far)
    back = swap_exp(other, 1)
    to_one, to_three = rounded(to_one, back[:rows]), rounded(to_three, back[rows : 2 * rows])
    to_x = rounded(to_x, back[2 * rows : 4 * rows])
    to_y = rounded(to_y, back[4 * rows : 6 * rows])
    kept = added(near_kept, near_back)
    to_two = rounded(kept[:rows], near_x[:rows], near_y[:rows], near_far)
    to_two, to_one, to_three, to_x, to_y = ordered(to_two, to_one, to_three, to_x, to_y)
    from_two = turn_rep(to_two, -2)
    from_one, from_three = turn_rep(to_one, -1), turn_rep(to_three, -3)
    far_x, far_y = swap_exp(to_x, 2), swap_exp(to_y, 4)

    own_sum = kept[rows : 2 * rows] + added(near_x[rows:], near_y[rows:])
    to_far = (kept[2 * rows :] + added(from_one, from_three)).astype(jnp.bfloat16)
    from_far = swap_exp(to_far, 6)
    sums = added(far_kept, back[6 * rows :], far_x, far_y).astype(jnp.bfloat16)
    arrived = [turn_rep(sums[:rows], -1), turn_rep(sums[rows:], -3)]
    return rounded(own_sum, from_two, from_far, *arrived)


def solution(mesh):
    placed = (
        P(("rep", "exp"), None),
        P(("rep", "exp"), None),
        P(("rep", "exp"), None),
        P("exp", "rep", None),
        P("exp", "rep", None),
        P("exp", "rep", None),
    )
    plane = mesh.shape["exp"] == 8 and mesh.shape["rep"] == 4
    return jax.shard_map(
        on_device_dense if plane else on_device_slots,
        mesh=mesh,
        in_specs=placed,
        out_specs=P(("rep", "exp"), None),
        check_vma=False,
    )
```

```python
import functools

import jax
import jax.numpy as jnp
from jax import lax
from jax.experimental import pallas as pl
from jax.experimental.pallas import tpu as pltpu
from jax.sharding import PartitionSpec as P


def slot_table(experts, expert_count, capacity):
    blocks = experts.shape[0]
    flattened = experts.reshape(blocks, -1)
    onehot = (
        flattened[:, :, None] == jnp.arange(expert_count, dtype=jnp.int32)[None, None, :]
    ).astype(jnp.int32)
    before = jnp.cumsum(onehot, axis=1) - onehot
    position = jnp.sum(before * onehot, axis=2)
    return flattened * capacity + position


def token_picks(slots, top_count, slot_count):
    blocks = slots.shape[0]
    grouped = slots.reshape(blocks, 1, -1, top_count)
    return jnp.any(grouped == jnp.arange(slot_count, dtype=jnp.int32)[None, :, None, None], axis=3)


def routing_column(route_weights, routed_experts):
    as_float = routed_experts.astype(jnp.float32)
    weights_all, experts_all = (
        lax.all_gather(route_weights, "rep", axis=0, tiled=True),
        lax.all_gather(as_float, "rep", axis=0, tiled=True),
    )
    return (weights_all, experts_all.astype(jnp.int32))


def on_device_slots(tokens, routed_experts, route_weights, gate_weight, up_weight, down_weight):
    replicas = lax.axis_size("rep")
    owners = lax.axis_size("exp")
    token_rows, model_width = tokens.shape
    top_count = routed_experts.shape[1]
    local_experts = gate_weight.shape[0]
    expert_count = local_experts * owners
    capacity = max(2, 3 * token_rows * top_count // (2 * expert_count))
    slot_count = expert_count * capacity
    own_slots = slot_table(routed_experts[None], expert_count, capacity)
    column = None
    column_slots = None
    selected = token_picks(own_slots, top_count, slot_count)[0].astype(jnp.bfloat16)
    buffer = jnp.dot(selected, tokens, preferred_element_type=jnp.float32).astype(jnp.bfloat16)
    buffer = buffer.reshape(owners, local_experts, capacity, model_width)
    arrived = lax.all_to_all(buffer, "exp", split_axis=0, concat_axis=2, tiled=True)
    rows_now = lax.all_gather(arrived, "rep", axis=2, tiled=True)[0]
    gate_value = jnp.einsum(
        "emd,efd->emf", rows_now, gate_weight, preferred_element_type=jnp.float32
    )
    up_value = jnp.einsum("emd,efd->emf", rows_now, up_weight, preferred_element_type=jnp.float32)
    hidden = (jax.nn.silu(gate_value) * up_value).astype(jnp.bfloat16)
    outcome = jnp.einsum("emf,efd->emd", hidden, down_weight, preferred_element_type=jnp.float32)
    outcome = lax.optimization_barrier(outcome.astype(jnp.bfloat16))
    outcomes = outcome[None]
    outcomes = outcomes.reshape(local_experts, replicas, owners, capacity, model_width)
    column = routing_column(route_weights, routed_experts)
    column_slots = slot_table(
        column[1].reshape(replicas, token_rows, top_count), expert_count, capacity
    )
    returned = lax.all_to_all(outcomes, "exp", split_axis=2, concat_axis=0, tiled=True)
    returned = returned.reshape(expert_count, replicas, capacity, model_width)
    expert_index = column_slots // capacity
    place_index = column_slots % capacity
    replica_index = jnp.broadcast_to(
        jnp.arange(replicas, dtype=jnp.int32)[:, None], column_slots.shape
    )
    picked = returned[expert_index, replica_index, place_index].astype(jnp.float32)
    column_weights = column[0].reshape(replicas, token_rows, top_count)
    weighted = jnp.sum(
        picked.reshape(replicas, token_rows, top_count, model_width)
        * column_weights[:, :, :, None],
        axis=2,
    )
    summed = lax.psum_scatter(weighted, "rep", scatter_dimension=0, tiled=True)
    return summed.reshape(token_rows, model_width).astype(jnp.bfloat16)


def fetch_kernel(turn, source_ref, result_ref):
    rows, width = source_ref.shape
    block = 512

    def fetch_block(step, carry):
        span = pl.ds(pl.multiple_of(step * block, block), block)
        if turn:
            for part in range(0, rows, 128):
                result_ref[span, part : part + 128] = source_ref[part : part + 128, span].T
        else:
            result_ref[:, span] = source_ref[:, span]
        return carry

    lax.fori_loop(0, width // block, fetch_block, 0)


def fetched(weight, turn):
    rows, width = weight.shape
    return pl.pallas_call(
        functools.partial(fetch_kernel, turn),
        out_shape=jax.ShapeDtypeStruct((width, rows) if turn else (rows, width), jnp.bfloat16),
        in_specs=[pl.BlockSpec(memory_space=pltpu.VMEM)],
        out_specs=pl.BlockSpec(memory_space=pltpu.VMEM),
        compiler_params=pltpu.CompilerParams(vmem_limit_bytes=4 * 1024 * 1024),
        cost_estimate=pl.CostEstimate(
            flops=0, bytes_accessed=4 * rows * width, transcendentals=0
        ),
        name="fetch_turned" if turn else "fetch",
    )(weight)


def gather_kernel(*refs):
    *pieces, whole_ref = refs
    start = 0
    for piece_ref in pieces:
        count = piece_ref.shape[0]
        whole_ref[start : start + count, :] = piece_ref[...]
        start += count


def gathered(*pieces):
    rows = sum(piece.shape[0] for piece in pieces)
    resident = pl.BlockSpec(memory_space=pltpu.VMEM)
    return pl.pallas_call(
        gather_kernel,
        out_shape=jax.ShapeDtypeStruct((rows, pieces[0].shape[1]), jnp.bfloat16),
        in_specs=[resident] * len(pieces),
        out_specs=resident,
        compiler_params=pltpu.CompilerParams(vmem_limit_bytes=2 * 1024 * 1024),
        name="gather",
    )(*pieces)


def expert_kernel(pieces_in, pieces_out, local_experts, shard_units, model_width, top, *refs):
    own_ref, refs = refs[0], refs[1:]
    ins, refs = refs[: len(pieces_in)], refs[len(pieces_in) :]
    (gate_ref, up_ref, down_ref), refs = refs[:3], refs[3:]
    outs, refs = refs[: len(pieces_out)], refs[len(pieces_out) :]
    rows, hidden = refs
    units = local_experts * shard_units
    unit_block = 256 if units % 256 == 0 else 128
    block = 512

    start = 0
    for place, count in enumerate(pieces_in):
        rows[start : start + count, :] = ins[place][...]
        start += count

    extra = rows[:, model_width:].astype(jnp.float32)
    width = extra.shape[1]
    scale = pltpu.roll(extra, width - top, 1) + pltpu.roll(extra, width - 2 * top, 1)
    lane = lax.broadcasted_iota(jnp.int32, extra.shape, 1)
    weights = []
    for expert in range(local_experts):
        name = (own_ref[0] + expert).astype(jnp.float32)
        chosen = jnp.logical_and(lane < top, extra == name)
        weights.append(jnp.sum(jnp.where(chosen, scale, 0.0), axis=1, keepdims=True))

    for begin in range(0, units, unit_block):
        span = slice(begin, begin + unit_block)
        values = rows[:, :model_width]
        gate = jnp.dot(values, gate_ref[:, span], preferred_element_type=jnp.float32)
        up = jnp.dot(values, up_ref[:, span], preferred_element_type=jnp.float32)
        unit = begin + lax.broadcasted_iota(jnp.int32, gate.shape, 1)
        weight = weights[begin // shard_units]
        for expert in range(begin // shard_units + 1, (begin + unit_block - 1) // shard_units + 1):
            weight = jnp.where(unit >= expert * shard_units, weights[expert], weight)
        active = gate / (1.0 + jnp.exp(-gate)) * up * weight
        hidden[:, span] = active.astype(jnp.bfloat16)

    for begin in range(0, model_width, block):
        span = slice(begin, begin + block)
        value = jnp.dot(hidden[...], down_ref[:, span], preferred_element_type=jnp.float32)
        value = value.astype(jnp.bfloat16)
        for place, segments in enumerate(pieces_out):
            filled = 0
            for first, count in segments:
                outs[place][filled : filled + count, span] = value[first : first + count]
                filled += count


def experts_of(own, pieces, pieces_out, gates, ups, downs, shard_units, top):
    units, model_width = downs.shape
    local_experts = units // shard_units
    pieces_in = [piece.shape[0] for piece in pieces]
    total = sum(pieces_in)
    packed = pieces[0].shape[1]
    resident = pl.BlockSpec(memory_space=pltpu.VMEM)
    kernel = functools.partial(
        expert_kernel, pieces_in, pieces_out, local_experts, shard_units, model_width, top
    )
    out_rows = [sum(count for _, count in segments) for segments in pieces_out]
    return pl.pallas_call(
        kernel,
        out_shape=[jax.ShapeDtypeStruct((count, model_width), jnp.bfloat16) for count in out_rows],
        in_specs=[pl.BlockSpec(memory_space=pltpu.SMEM)] + [resident] * (len(pieces) + 3),
        out_specs=[resident] * len(out_rows),
        scratch_shapes=[
            pltpu.VMEM((total, packed), jnp.bfloat16),
            pltpu.VMEM((total, units), jnp.bfloat16),
        ],
        compiler_params=pltpu.CompilerParams(vmem_limit_bytes=12 * 1024 * 1024),
        cost_estimate=pl.CostEstimate(
            flops=6 * total * units * model_width,
            bytes_accessed=4 * total * model_width,
            transcendentals=total * units,
        ),
        name="experts",
    )(own, *pieces, gates, ups, downs)


def pack_kernel(
    tokens_ref, experts_ref, weights_ref, packed_ref, experts, weights, sems
):
    model_width = tokens_ref.shape[1]
    copies = [
        pltpu.make_async_copy(experts_ref, experts, sems.at[0]),
        pltpu.make_async_copy(weights_ref, weights, sems.at[1]),
        pltpu.make_async_copy(tokens_ref, packed_ref.at[:, pl.ds(0, model_width)], sems.at[2]),
    ]
    for copy in copies:
        copy.start()
    copies[0].wait()
    copies[1].wait()
    values = weights[...]
    high = values.astype(jnp.bfloat16).astype(jnp.float32)
    listed = jnp.concatenate([experts[...].astype(jnp.float32), high, values - high], axis=0)
    width = packed_ref.shape[1] - model_width
    place = lax.broadcasted_iota(jnp.int32, (listed.shape[0], width), 0)
    lane = lax.broadcasted_iota(jnp.int32, (listed.shape[0], width), 1)
    chosen = jnp.where(place == lane, 1.0, 0.0).astype(jnp.bfloat16)
    extra = lax.dot_general(
        listed.astype(jnp.bfloat16),
        chosen,
        (((0,), (0,)), ((), ())),
        preferred_element_type=jnp.float32,
    )
    packed_ref[:, model_width:] = extra.astype(jnp.bfloat16)
    copies[2].wait()


def with_routing(tokens, routed_experts, route_weights):
    rows, width = tokens.shape
    top = routed_experts.shape[1]
    return pl.pallas_call(
        pack_kernel,
        out_shape=jax.ShapeDtypeStruct((rows, width + 128), jnp.bfloat16),
        in_specs=[pl.BlockSpec(memory_space=pl.ANY)] * 3,
        out_specs=pl.BlockSpec(memory_space=pltpu.VMEM),
        scratch_shapes=[
            pltpu.VMEM((top, rows), jnp.int32),
            pltpu.VMEM((top, rows), jnp.float32),
            pltpu.SemaphoreType.DMA((3,)),
        ],
        compiler_params=pltpu.CompilerParams(vmem_limit_bytes=2 * 1024 * 1024),
        name="pack",
    )(tokens, routed_experts.T, route_weights.T)


def begin_kernel(own_ref, gate_ref, up_ref, down_ref, index_ref):
    index_ref[0] = own_ref[0]


def begun(own, *weights):
    scalar = pl.BlockSpec(memory_space=pltpu.SMEM)
    return pl.pallas_call(
        begin_kernel,
        out_shape=jax.ShapeDtypeStruct((1,), jnp.int32),
        in_specs=[scalar] + [pl.BlockSpec(memory_space=pl.ANY)] * 3,
        out_specs=scalar,
        compiler_params=pltpu.CompilerParams(vmem_limit_bytes=50 * 1024 * 1024),
        name="begin",
    )(own, *weights)


def swap_exp(value, bits):
    owners = lax.axis_size("exp")
    return lax.ppermute(value, "exp", [(i, i ^ bits) for i in range(owners)])


def swap_rep(value, bits):
    replicas = lax.axis_size("rep")
    return lax.ppermute(value, "rep", [(i, i ^ bits) for i in range(replicas)])


def added(*terms):
    total = terms[0].astype(jnp.float32)
    for term in terms[1:]:
        total = total + term.astype(jnp.float32)
    return total


def rounded(*terms):
    return added(*terms).astype(jnp.bfloat16)


def ordered(*values):
    return lax.optimization_barrier(values)


def row_groups(places, rows):
    return [[(place * rows, rows) for place in group] for group in places]


def on_device_dense(tokens, routed_experts, route_weights, gate_weight, up_weight, down_weight):
    local_experts, shard_units, model_width = gate_weight.shape
    units = local_experts * shard_units
    top = routed_experts.shape[1]
    rows = tokens.shape[0]
    gate_weight = gate_weight.reshape(units, model_width)
    up_weight = up_weight.reshape(units, model_width)
    down_weight = down_weight.reshape(units, model_width)
    own = jnp.full((1,), lax.axis_index("exp") * local_experts, jnp.int32)
    own = begun(own, gate_weight, up_weight, down_weight)
    tokens, own = ordered(tokens, own)
    packed = with_routing(tokens, routed_experts, route_weights)

    three = swap_rep(packed, 3)
    x_own, y_own, far_own = [swap_exp(packed, bits) for bits in (2, 4, 6)]
    gates, ups = fetched(gate_weight, True), fetched(up_weight, True)
    x_own, y_own, far_own, three, gates, ups, again = ordered(
        x_own, y_own, far_own, three, gates, ups, packed
    )
    one, two = swap_rep(again, 1), swap_rep(again, 2)
    x_three, y_three, far_three = [swap_exp(three, bits) for bits in (2, 4, 6)]
    far_one, far_two = swap_rep(far_own, 1), swap_rep(far_own, 2)
    first = gathered(packed, x_own, y_own, far_own)
    first_other = swap_exp(first, 1)
    second = gathered(three, x_three, y_three, far_three)
    downs = fetched(down_weight, False)
    second, downs, one, two = ordered(second, downs, one, two)
    pair = gathered(one, two)
    x_pair, y_pair = swap_exp(pair, 2), swap_exp(pair, 4)

    near = [first, second, first_other, swap_exp(second, 1)]
    groups = row_groups([[5, 1], [6, 2], [7], [13, 9, 14, 10, 15], [4, 0, 3], [12, 8, 11]], rows)
    parts = experts_of(own, near, groups, gates, ups, downs, shard_units, top)
    *parts, x_pair, y_pair, far_one, far_two = ordered(*parts, x_pair, y_pair, far_one, far_two)
    to_x, to_y, to_far, other, near_kept, near_other = parts
    back = swap_exp(other, 1)
    to_x = rounded(to_x, back[: 2 * rows])
    to_y = rounded(to_y, back[2 * rows : 4 * rows])
    to_far = rounded(to_far, back[4 * rows :])
    to_x, to_y, to_far, near_other = ordered(to_x, to_y, to_far, near_other)
    near_x, near_y, near_far = swap_exp(to_x, 2), swap_exp(to_y, 4), swap_exp(to_far, 6)
    near_back = swap_exp(near_other, 1)

    far = [pair, x_pair, y_pair, far_one, far_two]
    far = far + [swap_exp(piece, 1) for piece in far]
    to_x, to_y, to_far, *far = ordered(to_x, to_y, to_far, *far)
    groups = row_groups([[6], [7], [2, 3], [4, 5], [14], [10, 11, 12, 13, 15, 8, 9], [0, 1]], rows)
    parts = experts_of(own, far, groups, gates, ups, downs, shard_units, top)
    to_one, to_far, to_x, to_y, other_one, other, far_kept = parts
    far_kept, near_x, near_y, near_far = ordered(far_kept, near_x, near_y, near_far)
    back = swap_exp(other, 1)
    to_x, to_y = rounded(to_x, back[: 2 * rows]), rounded(to_y, back[2 * rows : 4 * rows])
    to_far = rounded(to_far, back[4 * rows : 5 * rows])
    to_x, to_y, to_far, other_one = ordered(to_x, to_y, to_far, other_one)
    far_x, far_y, far_far = swap_exp(to_x, 2), swap_exp(to_y, 4), swap_exp(to_far, 6)
    to_one = rounded(to_one, swap_exp(other_one, 1))
    kept = added(near_kept, near_back)
    to_three = rounded(kept[:rows], near_x[:rows], near_y[:rows], near_far)
    to_three, to_one = ordered(to_three, to_one)
    from_three, from_one = swap_rep(to_three, 3), swap_rep(to_one, 1)

    own_sum = kept[rows : 2 * rows] + added(near_x[rows:], near_y[rows:])
    to_far = rounded(kept[2 * rows :], from_one)
    from_far = swap_exp(to_far, 6)
    to_one = rounded(far_kept[:rows], back[5 * rows : 6 * rows], far_x[:rows], far_y[:rows])
    to_two = rounded(far_kept[rows:], back[6 * rows :], far_x[rows:], far_y[rows:], far_far)
    arrived = [swap_rep(to_one, 1), swap_rep(to_two, 2)]
    return rounded(own_sum, from_three, from_far, *arrived)


def solution(mesh):
    placed = (
        P(("rep", "exp"), None),
        P(("rep", "exp"), None),
        P(("rep", "exp"), None),
        P("exp", "rep", None),
        P("exp", "rep", None),
        P("exp", "rep", None),
    )
    plane = mesh.shape["exp"] == 8 and mesh.shape["rep"] == 4
    return jax.shard_map(
        on_device_dense if plane else on_device_slots,
        mesh=mesh,
        in_specs=placed,
        out_specs=P(("rep", "exp"), None),
        check_vma=False,
    )
```

```python
import functools

import jax
import jax.numpy as jnp
from jax import lax
from jax.experimental import pallas as pl
from jax.experimental.pallas import tpu as pltpu
from jax.sharding import PartitionSpec as P


def slot_table(experts, expert_count, capacity):
    blocks = experts.shape[0]
    flattened = experts.reshape(blocks, -1)
    onehot = (
        flattened[:, :, None] == jnp.arange(expert_count, dtype=jnp.int32)[None, None, :]
    ).astype(jnp.int32)
    before = jnp.cumsum(onehot, axis=1) - onehot
    position = jnp.sum(before * onehot, axis=2)
    return flattened * capacity + position


def token_picks(slots, top_count, slot_count):
    blocks = slots.shape[0]
    grouped = slots.reshape(blocks, 1, -1, top_count)
    return jnp.any(grouped == jnp.arange(slot_count, dtype=jnp.int32)[None, :, None, None], axis=3)


def routing_column(route_weights, routed_experts):
    as_float = routed_experts.astype(jnp.float32)
    weights_all, experts_all = (
        lax.all_gather(route_weights, "rep", axis=0, tiled=True),
        lax.all_gather(as_float, "rep", axis=0, tiled=True),
    )
    return (weights_all, experts_all.astype(jnp.int32))


def on_device_slots(tokens, routed_experts, route_weights, gate_weight, up_weight, down_weight):
    replicas = lax.axis_size("rep")
    owners = lax.axis_size("exp")
    token_rows, model_width = tokens.shape
    top_count = routed_experts.shape[1]
    local_experts = gate_weight.shape[0]
    expert_count = local_experts * owners
    capacity = max(2, 3 * token_rows * top_count // (2 * expert_count))
    slot_count = expert_count * capacity
    own_slots = slot_table(routed_experts[None], expert_count, capacity)
    column = None
    column_slots = None
    selected = token_picks(own_slots, top_count, slot_count)[0].astype(jnp.bfloat16)
    buffer = jnp.dot(selected, tokens, preferred_element_type=jnp.float32).astype(jnp.bfloat16)
    buffer = buffer.reshape(owners, local_experts, capacity, model_width)
    arrived = lax.all_to_all(buffer, "exp", split_axis=0, concat_axis=2, tiled=True)
    rows_now = lax.all_gather(arrived, "rep", axis=2, tiled=True)[0]
    gate_value = jnp.einsum(
        "emd,efd->emf", rows_now, gate_weight, preferred_element_type=jnp.float32
    )
    up_value = jnp.einsum("emd,efd->emf", rows_now, up_weight, preferred_element_type=jnp.float32)
    hidden = (jax.nn.silu(gate_value) * up_value).astype(jnp.bfloat16)
    outcome = jnp.einsum("emf,efd->emd", hidden, down_weight, preferred_element_type=jnp.float32)
    outcome = lax.optimization_barrier(outcome.astype(jnp.bfloat16))
    outcomes = outcome[None]
    outcomes = outcomes.reshape(local_experts, replicas, owners, capacity, model_width)
    column = routing_column(route_weights, routed_experts)
    column_slots = slot_table(
        column[1].reshape(replicas, token_rows, top_count), expert_count, capacity
    )
    returned = lax.all_to_all(outcomes, "exp", split_axis=2, concat_axis=0, tiled=True)
    returned = returned.reshape(expert_count, replicas, capacity, model_width)
    expert_index = column_slots // capacity
    place_index = column_slots % capacity
    replica_index = jnp.broadcast_to(
        jnp.arange(replicas, dtype=jnp.int32)[:, None], column_slots.shape
    )
    picked = returned[expert_index, replica_index, place_index].astype(jnp.float32)
    column_weights = column[0].reshape(replicas, token_rows, top_count)
    weighted = jnp.sum(
        picked.reshape(replicas, token_rows, top_count, model_width)
        * column_weights[:, :, :, None],
        axis=2,
    )
    summed = lax.psum_scatter(weighted, "rep", scatter_dimension=0, tiled=True)
    return summed.reshape(token_rows, model_width).astype(jnp.bfloat16)


def fetch_kernel(turn, source_ref, result_ref):
    rows, width = source_ref.shape
    block = 512

    def fetch_block(step, carry):
        span = pl.ds(pl.multiple_of(step * block, block), block)
        if turn:
            for part in range(0, rows, 128):
                result_ref[span, part : part + 128] = source_ref[part : part + 128, span].T
        else:
            result_ref[:, span] = source_ref[:, span]
        return carry

    lax.fori_loop(0, width // block, fetch_block, 0)


def fetched(weight, turn):
    rows, width = weight.shape
    return pl.pallas_call(
        functools.partial(fetch_kernel, turn),
        out_shape=jax.ShapeDtypeStruct((width, rows) if turn else (rows, width), jnp.bfloat16),
        in_specs=[pl.BlockSpec(memory_space=pltpu.VMEM)],
        out_specs=pl.BlockSpec(memory_space=pltpu.VMEM),
        compiler_params=pltpu.CompilerParams(vmem_limit_bytes=4 * 1024 * 1024),
        cost_estimate=pl.CostEstimate(
            flops=0, bytes_accessed=4 * rows * width, transcendentals=0
        ),
        name="fetch_turned" if turn else "fetch",
    )(weight)


def gather_kernel(*refs):
    *pieces, whole_ref = refs
    start = 0
    for piece_ref in pieces:
        count = piece_ref.shape[0]
        whole_ref[start : start + count, :] = piece_ref[...]
        start += count


def gathered(*pieces):
    rows = sum(piece.shape[0] for piece in pieces)
    resident = pl.BlockSpec(memory_space=pltpu.VMEM)
    return pl.pallas_call(
        gather_kernel,
        out_shape=jax.ShapeDtypeStruct((rows, pieces[0].shape[1]), jnp.bfloat16),
        in_specs=[resident] * len(pieces),
        out_specs=resident,
        compiler_params=pltpu.CompilerParams(vmem_limit_bytes=2 * 1024 * 1024),
        name="gather",
    )(*pieces)


def expert_kernel(pieces_in, pieces_out, local_experts, shard_units, model_width, top, *refs):
    own_ref, refs = refs[0], refs[1:]
    ins, refs = refs[: len(pieces_in)], refs[len(pieces_in) :]
    (gate_ref, up_ref, down_ref), refs = refs[:3], refs[3:]
    outs, refs = refs[: len(pieces_out)], refs[len(pieces_out) :]
    rows, hidden = refs
    units = local_experts * shard_units
    unit_block = 256 if units % 256 == 0 else 128
    block = 512

    start = 0
    for place, count in enumerate(pieces_in):
        rows[start : start + count, :] = ins[place][...]
        start += count

    extra = rows[:, model_width:].astype(jnp.float32)
    width = extra.shape[1]
    scale = pltpu.roll(extra, width - top, 1) + pltpu.roll(extra, width - 2 * top, 1)
    lane = lax.broadcasted_iota(jnp.int32, extra.shape, 1)
    weights = []
    for expert in range(local_experts):
        name = (own_ref[0] + expert).astype(jnp.float32)
        chosen = jnp.logical_and(lane < top, extra == name)
        weights.append(jnp.sum(jnp.where(chosen, scale, 0.0), axis=1, keepdims=True))

    for begin in range(0, units, unit_block):
        span = slice(begin, begin + unit_block)
        values = rows[:, :model_width]
        gate = jnp.dot(values, gate_ref[:, span], preferred_element_type=jnp.float32)
        up = jnp.dot(values, up_ref[:, span], preferred_element_type=jnp.float32)
        unit = begin + lax.broadcasted_iota(jnp.int32, gate.shape, 1)
        weight = weights[begin // shard_units]
        for expert in range(begin // shard_units + 1, (begin + unit_block - 1) // shard_units + 1):
            weight = jnp.where(unit >= expert * shard_units, weights[expert], weight)
        active = gate / (1.0 + jnp.exp(-gate)) * up * weight
        hidden[:, span] = active.astype(jnp.bfloat16)

    for begin in range(0, model_width, block):
        span = slice(begin, begin + block)
        value = jnp.dot(hidden[...], down_ref[:, span], preferred_element_type=jnp.float32)
        value = value.astype(jnp.bfloat16)
        for place, segments in enumerate(pieces_out):
            filled = 0
            for first, count in segments:
                outs[place][filled : filled + count, span] = value[first : first + count]
                filled += count


def experts_of(own, pieces, pieces_out, gates, ups, downs, shard_units, top):
    units, model_width = downs.shape
    local_experts = units // shard_units
    pieces_in = [piece.shape[0] for piece in pieces]
    total = sum(pieces_in)
    packed = pieces[0].shape[1]
    resident = pl.BlockSpec(memory_space=pltpu.VMEM)
    kernel = functools.partial(
        expert_kernel, pieces_in, pieces_out, local_experts, shard_units, model_width, top
    )
    out_rows = [sum(count for _, count in segments) for segments in pieces_out]
    return pl.pallas_call(
        kernel,
        out_shape=[jax.ShapeDtypeStruct((count, model_width), jnp.bfloat16) for count in out_rows],
        in_specs=[pl.BlockSpec(memory_space=pltpu.SMEM)] + [resident] * (len(pieces) + 3),
        out_specs=[resident] * len(out_rows),
        scratch_shapes=[
            pltpu.VMEM((total, packed), jnp.bfloat16),
            pltpu.VMEM((total, units), jnp.bfloat16),
        ],
        compiler_params=pltpu.CompilerParams(vmem_limit_bytes=12 * 1024 * 1024),
        cost_estimate=pl.CostEstimate(
            flops=6 * total * units * model_width,
            bytes_accessed=4 * total * model_width,
            transcendentals=total * units,
        ),
        name="experts",
    )(own, *pieces, gates, ups, downs)


def pack_kernel(
    tokens_ref, experts_ref, weights_ref, packed_ref, experts, weights, sems
):
    model_width = tokens_ref.shape[1]
    copies = [
        pltpu.make_async_copy(experts_ref, experts, sems.at[0]),
        pltpu.make_async_copy(weights_ref, weights, sems.at[1]),
        pltpu.make_async_copy(tokens_ref, packed_ref.at[:, pl.ds(0, model_width)], sems.at[2]),
    ]
    for copy in copies:
        copy.start()
    copies[0].wait()
    copies[1].wait()
    values = weights[...]
    high = values.astype(jnp.bfloat16).astype(jnp.float32)
    listed = jnp.concatenate([experts[...].astype(jnp.float32), high, values - high], axis=0)
    width = packed_ref.shape[1] - model_width
    place = lax.broadcasted_iota(jnp.int32, (listed.shape[0], width), 0)
    lane = lax.broadcasted_iota(jnp.int32, (listed.shape[0], width), 1)
    chosen = jnp.where(place == lane, 1.0, 0.0).astype(jnp.bfloat16)
    extra = lax.dot_general(
        listed.astype(jnp.bfloat16),
        chosen,
        (((0,), (0,)), ((), ())),
        preferred_element_type=jnp.float32,
    )
    packed_ref[:, model_width:] = extra.astype(jnp.bfloat16)
    copies[2].wait()


def with_routing(tokens, routed_experts, route_weights):
    rows, width = tokens.shape
    top = routed_experts.shape[1]
    return pl.pallas_call(
        pack_kernel,
        out_shape=jax.ShapeDtypeStruct((rows, width + 128), jnp.bfloat16),
        in_specs=[pl.BlockSpec(memory_space=pl.ANY)] * 3,
        out_specs=pl.BlockSpec(memory_space=pltpu.VMEM),
        scratch_shapes=[
            pltpu.VMEM((top, rows), jnp.int32),
            pltpu.VMEM((top, rows), jnp.float32),
            pltpu.SemaphoreType.DMA((3,)),
        ],
        compiler_params=pltpu.CompilerParams(vmem_limit_bytes=2 * 1024 * 1024),
        name="pack",
    )(tokens, routed_experts.T, route_weights.T)


def begin_kernel(own_ref, gate_ref, up_ref, down_ref, index_ref):
    index_ref[0] = own_ref[0]


def begun(own, *weights):
    scalar = pl.BlockSpec(memory_space=pltpu.SMEM)
    return pl.pallas_call(
        begin_kernel,
        out_shape=jax.ShapeDtypeStruct((1,), jnp.int32),
        in_specs=[scalar] + [pl.BlockSpec(memory_space=pl.ANY)] * 3,
        out_specs=scalar,
        compiler_params=pltpu.CompilerParams(
            vmem_limit_bytes=50 * 1024 * 1024, has_side_effects=True
        ),
        name="begin",
    )(own, *weights)


def swap_exp(value, bits):
    owners = lax.axis_size("exp")
    return lax.ppermute(value, "exp", [(i, i ^ bits) for i in range(owners)])


def swap_rep(value, bits):
    replicas = lax.axis_size("rep")
    return lax.ppermute(value, "rep", [(i, i ^ bits) for i in range(replicas)])


def added(*terms):
    total = terms[0].astype(jnp.float32)
    for term in terms[1:]:
        total = total + term.astype(jnp.float32)
    return total


def rounded(*terms):
    return added(*terms).astype(jnp.bfloat16)


def ordered(*values):
    return lax.optimization_barrier(values)


def row_groups(places, rows):
    return [[(place * rows, rows) for place in group] for group in places]


def on_device_dense(tokens, routed_experts, route_weights, gate_weight, up_weight, down_weight):
    local_experts, shard_units, model_width = gate_weight.shape
    units = local_experts * shard_units
    top = routed_experts.shape[1]
    rows = tokens.shape[0]
    gate_weight = gate_weight.reshape(units, model_width)
    up_weight = up_weight.reshape(units, model_width)
    down_weight = down_weight.reshape(units, model_width)
    own = jnp.full((1,), lax.axis_index("exp") * local_experts, jnp.int32)
    begin = begun(own, gate_weight, up_weight, down_weight)
    tokens, own, begin = ordered(tokens, own, begin)
    packed = with_routing(tokens, routed_experts, route_weights)

    three = swap_rep(packed, 3)
    x_own, y_own, far_own = [swap_exp(packed, bits) for bits in (2, 4, 6)]
    gates, ups = fetched(gate_weight, True), fetched(up_weight, True)
    one = swap_rep(packed, 1)
    x_own, y_own, far_own, one, three, gates, ups, again = ordered(
        x_own, y_own, far_own, one, three, gates, ups, packed
    )
    two = swap_rep(again, 2)
    x_three, y_three, far_three = [swap_exp(three, bits) for bits in (2, 4, 6)]
    far_one, far_two = swap_rep(far_own, 1), swap_rep(far_own, 2)
    first = gathered(packed, x_own, y_own, far_own)
    first_other = swap_exp(first, 1)
    second = gathered(three, x_three, y_three, far_three)
    two, down_weight = ordered(two, down_weight)
    downs = fetched(down_weight, False)
    second, downs = ordered(second, downs)
    pair = gathered(one, two)
    x_pair, y_pair = swap_exp(pair, 2), swap_exp(pair, 4)

    near = [first, second, first_other, swap_exp(second, 1)]
    groups = row_groups([[5, 1], [6, 2], [7], [13, 9, 14, 10, 15], [4, 0, 3], [12, 8, 11]], rows)
    parts = experts_of(own, near, groups, gates, ups, downs, shard_units, top)
    *parts, x_pair, y_pair, far_one, far_two = ordered(*parts, x_pair, y_pair, far_one, far_two)
    to_x, to_y, to_far, other, near_kept, near_other = parts
    back = swap_exp(other, 1)
    to_x = rounded(to_x, back[: 2 * rows])
    to_y = rounded(to_y, back[2 * rows : 4 * rows])
    to_far = rounded(to_far, back[4 * rows :])
    to_x, to_y, to_far, near_other = ordered(to_x, to_y, to_far, near_other)
    near_x, near_y, near_far = swap_exp(to_x, 2), swap_exp(to_y, 4), swap_exp(to_far, 6)
    near_back = swap_exp(near_other, 1)

    far = [pair, x_pair, y_pair, far_one, far_two]
    far = far + [swap_exp(piece, 1) for piece in far]
    to_x, to_y, to_far, *far = ordered(to_x, to_y, to_far, *far)
    groups = row_groups([[6], [7], [2, 3], [4, 5], [14], [10, 11, 12, 13, 15, 8, 9], [0, 1]], rows)
    parts = experts_of(own, far, groups, gates, ups, downs, shard_units, top)
    to_one, to_far, to_x, to_y, other_one, other, far_kept = parts
    far_kept, near_x, near_y, near_far = ordered(far_kept, near_x, near_y, near_far)
    back = swap_exp(other, 1)
    to_x, to_y = rounded(to_x, back[: 2 * rows]), rounded(to_y, back[2 * rows : 4 * rows])
    to_far = rounded(to_far, back[4 * rows : 5 * rows])
    to_x, to_y, to_far, other_one = ordered(to_x, to_y, to_far, other_one)
    far_x, far_y, far_far = swap_exp(to_x, 2), swap_exp(to_y, 4), swap_exp(to_far, 6)
    to_one = rounded(to_one, swap_exp(other_one, 1))
    kept = added(near_kept, near_back)
    to_three = rounded(kept[:rows], near_x[:rows], near_y[:rows], near_far)
    to_three, to_one = ordered(to_three, to_one)
    from_three, from_one = swap_rep(to_three, 3), swap_rep(to_one, 1)

    own_sum = kept[rows : 2 * rows] + added(near_x[rows:], near_y[rows:])
    to_far = rounded(kept[2 * rows :], from_one)
    from_far = swap_exp(to_far, 6)
    to_one = rounded(far_kept[:rows], back[5 * rows : 6 * rows], far_x[:rows], far_y[:rows])
    to_two = rounded(far_kept[rows:], back[6 * rows :], far_x[rows:], far_y[rows:], far_far)
    arrived = [swap_rep(to_one, 1), swap_rep(to_two, 2)]
    return rounded(own_sum, from_three, from_far, *arrived)


def solution(mesh):
    placed = (
        P(("rep", "exp"), None),
        P(("rep", "exp"), None),
        P(("rep", "exp"), None),
        P("exp", "rep", None),
        P("exp", "rep", None),
        P("exp", "rep", None),
    )
    plane = mesh.shape["exp"] == 8 and mesh.shape["rep"] == 4
    return jax.shard_map(
        on_device_dense if plane else on_device_slots,
        mesh=mesh,
        in_specs=placed,
        out_specs=P(("rep", "exp"), None),
        check_vma=False,
    )
```

```python
import functools

import jax
import jax.numpy as jnp
from jax import lax
from jax.experimental import pallas as pl
from jax.experimental.pallas import tpu as pltpu
from jax.sharding import PartitionSpec as P


def slot_table(experts, expert_count, capacity):
    blocks = experts.shape[0]
    flattened = experts.reshape(blocks, -1)
    onehot = (
        flattened[:, :, None] == jnp.arange(expert_count, dtype=jnp.int32)[None, None, :]
    ).astype(jnp.int32)
    before = jnp.cumsum(onehot, axis=1) - onehot
    position = jnp.sum(before * onehot, axis=2)
    return flattened * capacity + position


def token_picks(slots, top_count, slot_count):
    blocks = slots.shape[0]
    grouped = slots.reshape(blocks, 1, -1, top_count)
    return jnp.any(grouped == jnp.arange(slot_count, dtype=jnp.int32)[None, :, None, None], axis=3)


def routing_column(route_weights, routed_experts):
    as_float = routed_experts.astype(jnp.float32)
    weights_all, experts_all = (
        lax.all_gather(route_weights, "rep", axis=0, tiled=True),
        lax.all_gather(as_float, "rep", axis=0, tiled=True),
    )
    return (weights_all, experts_all.astype(jnp.int32))


def on_device_slots(tokens, routed_experts, route_weights, gate_weight, up_weight, down_weight):
    replicas = lax.axis_size("rep")
    owners = lax.axis_size("exp")
    token_rows, model_width = tokens.shape
    top_count = routed_experts.shape[1]
    local_experts = gate_weight.shape[0]
    expert_count = local_experts * owners
    capacity = max(2, 3 * token_rows * top_count // (2 * expert_count))
    slot_count = expert_count * capacity
    own_slots = slot_table(routed_experts[None], expert_count, capacity)
    column = None
    column_slots = None
    selected = token_picks(own_slots, top_count, slot_count)[0].astype(jnp.bfloat16)
    buffer = jnp.dot(selected, tokens, preferred_element_type=jnp.float32).astype(jnp.bfloat16)
    buffer = buffer.reshape(owners, local_experts, capacity, model_width)
    arrived = lax.all_to_all(buffer, "exp", split_axis=0, concat_axis=2, tiled=True)
    rows_now = lax.all_gather(arrived, "rep", axis=2, tiled=True)[0]
    gate_value = jnp.einsum(
        "emd,efd->emf", rows_now, gate_weight, preferred_element_type=jnp.float32
    )
    up_value = jnp.einsum("emd,efd->emf", rows_now, up_weight, preferred_element_type=jnp.float32)
    hidden = (jax.nn.silu(gate_value) * up_value).astype(jnp.bfloat16)
    outcome = jnp.einsum("emf,efd->emd", hidden, down_weight, preferred_element_type=jnp.float32)
    outcome = lax.optimization_barrier(outcome.astype(jnp.bfloat16))
    outcomes = outcome[None]
    outcomes = outcomes.reshape(local_experts, replicas, owners, capacity, model_width)
    column = routing_column(route_weights, routed_experts)
    column_slots = slot_table(
        column[1].reshape(replicas, token_rows, top_count), expert_count, capacity
    )
    returned = lax.all_to_all(outcomes, "exp", split_axis=2, concat_axis=0, tiled=True)
    returned = returned.reshape(expert_count, replicas, capacity, model_width)
    expert_index = column_slots // capacity
    place_index = column_slots % capacity
    replica_index = jnp.broadcast_to(
        jnp.arange(replicas, dtype=jnp.int32)[:, None], column_slots.shape
    )
    picked = returned[expert_index, replica_index, place_index].astype(jnp.float32)
    column_weights = column[0].reshape(replicas, token_rows, top_count)
    weighted = jnp.sum(
        picked.reshape(replicas, token_rows, top_count, model_width)
        * column_weights[:, :, :, None],
        axis=2,
    )
    summed = lax.psum_scatter(weighted, "rep", scatter_dimension=0, tiled=True)
    return summed.reshape(token_rows, model_width).astype(jnp.bfloat16)


def fetch_kernel(turn, source_ref, result_ref):
    rows, width = source_ref.shape
    block = 512

    def fetch_block(step, carry):
        span = pl.ds(pl.multiple_of(step * block, block), block)
        if turn:
            for part in range(0, rows, 128):
                result_ref[span, part : part + 128] = source_ref[part : part + 128, span].T
        else:
            result_ref[:, span] = source_ref[:, span]
        return carry

    lax.fori_loop(0, width // block, fetch_block, 0)


def fetched(weight, turn):
    rows, width = weight.shape
    return pl.pallas_call(
        functools.partial(fetch_kernel, turn),
        out_shape=jax.ShapeDtypeStruct((width, rows) if turn else (rows, width), jnp.bfloat16),
        in_specs=[pl.BlockSpec(memory_space=pltpu.VMEM)],
        out_specs=pl.BlockSpec(memory_space=pltpu.VMEM),
        compiler_params=pltpu.CompilerParams(vmem_limit_bytes=4 * 1024 * 1024),
        cost_estimate=pl.CostEstimate(
            flops=0, bytes_accessed=4 * rows * width, transcendentals=0
        ),
        name="fetch_turned" if turn else "fetch",
    )(weight)


def gather_kernel(*refs):
    *pieces, whole_ref = refs
    start = 0
    for piece_ref in pieces:
        count = piece_ref.shape[0]
        whole_ref[start : start + count, :] = piece_ref[...]
        start += count


def gathered(*pieces):
    rows = sum(piece.shape[0] for piece in pieces)
    resident = pl.BlockSpec(memory_space=pltpu.VMEM)
    return pl.pallas_call(
        gather_kernel,
        out_shape=jax.ShapeDtypeStruct((rows, pieces[0].shape[1]), jnp.bfloat16),
        in_specs=[resident] * len(pieces),
        out_specs=resident,
        compiler_params=pltpu.CompilerParams(vmem_limit_bytes=2 * 1024 * 1024),
        name="gather",
    )(*pieces)


def expert_kernel(pieces_in, pieces_out, local_experts, shard_units, model_width, top, *refs):
    own_ref, refs = refs[0], refs[1:]
    ins, refs = refs[: len(pieces_in)], refs[len(pieces_in) :]
    (gate_ref, up_ref, down_ref), refs = refs[:3], refs[3:]
    outs, refs = refs[: len(pieces_out)], refs[len(pieces_out) :]
    rows, hidden = refs
    units = local_experts * shard_units
    unit_block = 256 if units % 256 == 0 else 128
    block = 512

    start = 0
    for place, count in enumerate(pieces_in):
        rows[start : start + count, :] = ins[place][...]
        start += count

    extra = rows[:, model_width:].astype(jnp.float32)
    width = extra.shape[1]
    scale = pltpu.roll(extra, width - top, 1) + pltpu.roll(extra, width - 2 * top, 1)
    lane = lax.broadcasted_iota(jnp.int32, extra.shape, 1)
    weights = []
    for expert in range(local_experts):
        name = (own_ref[0] + expert).astype(jnp.float32)
        chosen = jnp.logical_and(lane < top, extra == name)
        weights.append(jnp.sum(jnp.where(chosen, scale, 0.0), axis=1, keepdims=True))

    for begin in range(0, units, unit_block):
        span = slice(begin, begin + unit_block)
        values = rows[:, :model_width]
        gate = jnp.dot(values, gate_ref[:, span], preferred_element_type=jnp.float32)
        up = jnp.dot(values, up_ref[:, span], preferred_element_type=jnp.float32)
        unit = begin + lax.broadcasted_iota(jnp.int32, gate.shape, 1)
        weight = weights[begin // shard_units]
        for expert in range(begin // shard_units + 1, (begin + unit_block - 1) // shard_units + 1):
            weight = jnp.where(unit >= expert * shard_units, weights[expert], weight)
        active = gate / (1.0 + jnp.exp(-gate)) * up * weight
        hidden[:, span] = active.astype(jnp.bfloat16)

    for begin in range(0, model_width, block):
        span = slice(begin, begin + block)
        value = jnp.dot(hidden[...], down_ref[:, span], preferred_element_type=jnp.float32)
        value = value.astype(jnp.bfloat16)
        for place, segments in enumerate(pieces_out):
            filled = 0
            for first, count in segments:
                outs[place][filled : filled + count, span] = value[first : first + count]
                filled += count


def experts_of(own, pieces, pieces_out, gates, ups, downs, shard_units, top):
    units, model_width = downs.shape
    local_experts = units // shard_units
    pieces_in = [piece.shape[0] for piece in pieces]
    total = sum(pieces_in)
    packed = pieces[0].shape[1]
    resident = pl.BlockSpec(memory_space=pltpu.VMEM)
    kernel = functools.partial(
        expert_kernel, pieces_in, pieces_out, local_experts, shard_units, model_width, top
    )
    out_rows = [sum(count for _, count in segments) for segments in pieces_out]
    return pl.pallas_call(
        kernel,
        out_shape=[jax.ShapeDtypeStruct((count, model_width), jnp.bfloat16) for count in out_rows],
        in_specs=[pl.BlockSpec(memory_space=pltpu.SMEM)] + [resident] * (len(pieces) + 3),
        out_specs=[resident] * len(out_rows),
        scratch_shapes=[
            pltpu.VMEM((total, packed), jnp.bfloat16),
            pltpu.VMEM((total, units), jnp.bfloat16),
        ],
        compiler_params=pltpu.CompilerParams(vmem_limit_bytes=12 * 1024 * 1024),
        cost_estimate=pl.CostEstimate(
            flops=6 * total * units * model_width,
            bytes_accessed=4 * total * model_width,
            transcendentals=total * units,
        ),
        name="experts",
    )(own, *pieces, gates, ups, downs)


def pack_kernel(
    tokens_ref, experts_ref, weights_ref, packed_ref, experts, weights, sems
):
    model_width = tokens_ref.shape[1]
    copies = [
        pltpu.make_async_copy(experts_ref, experts, sems.at[0]),
        pltpu.make_async_copy(weights_ref, weights, sems.at[1]),
        pltpu.make_async_copy(tokens_ref, packed_ref.at[:, pl.ds(0, model_width)], sems.at[2]),
    ]
    for copy in copies:
        copy.start()
    copies[0].wait()
    copies[1].wait()
    values = weights[...]
    high = values.astype(jnp.bfloat16).astype(jnp.float32)
    listed = jnp.concatenate([experts[...].astype(jnp.float32), high, values - high], axis=0)
    width = packed_ref.shape[1] - model_width
    place = lax.broadcasted_iota(jnp.int32, (listed.shape[0], width), 0)
    lane = lax.broadcasted_iota(jnp.int32, (listed.shape[0], width), 1)
    chosen = jnp.where(place == lane, 1.0, 0.0).astype(jnp.bfloat16)
    extra = lax.dot_general(
        listed.astype(jnp.bfloat16),
        chosen,
        (((0,), (0,)), ((), ())),
        preferred_element_type=jnp.float32,
    )
    packed_ref[:, model_width:] = extra.astype(jnp.bfloat16)
    copies[2].wait()


def with_routing(tokens, routed_experts, route_weights):
    rows, width = tokens.shape
    top = routed_experts.shape[1]
    return pl.pallas_call(
        pack_kernel,
        out_shape=jax.ShapeDtypeStruct((rows, width + 128), jnp.bfloat16),
        in_specs=[pl.BlockSpec(memory_space=pl.ANY)] * 3,
        out_specs=pl.BlockSpec(memory_space=pltpu.VMEM),
        scratch_shapes=[
            pltpu.VMEM((top, rows), jnp.int32),
            pltpu.VMEM((top, rows), jnp.float32),
            pltpu.SemaphoreType.DMA((3,)),
        ],
        compiler_params=pltpu.CompilerParams(vmem_limit_bytes=2 * 1024 * 1024),
        name="pack",
    )(tokens, routed_experts.T, route_weights.T)


def begin_kernel(own_ref, gate_ref, up_ref, down_ref, index_ref):
    index_ref[0] = own_ref[0]


def begun(own, *weights):
    scalar = pl.BlockSpec(memory_space=pltpu.SMEM)
    return pl.pallas_call(
        begin_kernel,
        out_shape=jax.ShapeDtypeStruct((1,), jnp.int32),
        in_specs=[scalar] + [pl.BlockSpec(memory_space=pl.ANY)] * 3,
        out_specs=scalar,
        compiler_params=pltpu.CompilerParams(
            vmem_limit_bytes=50 * 1024 * 1024, has_side_effects=True
        ),
        name="begin",
    )(own, *weights)


def swap_exp(value, bits):
    owners = lax.axis_size("exp")
    return lax.ppermute(value, "exp", [(i, i ^ bits) for i in range(owners)])


def swap_rep(value, bits):
    replicas = lax.axis_size("rep")
    return lax.ppermute(value, "rep", [(i, i ^ bits) for i in range(replicas)])


def added(*terms):
    total = terms[0].astype(jnp.float32)
    for term in terms[1:]:
        total = total + term.astype(jnp.float32)
    return total


def rounded(*terms):
    return added(*terms).astype(jnp.bfloat16)


def ordered(*values):
    return lax.optimization_barrier(values)


def row_groups(places, rows):
    return [[(place * rows, rows) for place in group] for group in places]


def on_device_dense(tokens, routed_experts, route_weights, gate_weight, up_weight, down_weight):
    local_experts, shard_units, model_width = gate_weight.shape
    units = local_experts * shard_units
    top = routed_experts.shape[1]
    rows = tokens.shape[0]
    gate_weight = gate_weight.reshape(units, model_width)
    up_weight = up_weight.reshape(units, model_width)
    down_weight = down_weight.reshape(units, model_width)
    own = jnp.full((1,), lax.axis_index("exp") * local_experts, jnp.int32)
    begin = begun(own, gate_weight, up_weight, down_weight)
    tokens, own, begin = ordered(tokens, own, begin)
    packed = with_routing(tokens, routed_experts, route_weights)

    three = swap_rep(packed, 3)
    x_own, y_own, far_own = [swap_exp(packed, bits) for bits in (2, 4, 6)]
    gates, ups = fetched(gate_weight, True), fetched(up_weight, True)
    one = swap_rep(packed, 1)
    x_own, y_own, far_own, one, three, gates, ups, again = ordered(
        x_own, y_own, far_own, one, three, gates, ups, packed
    )
    two = swap_rep(again, 2)
    x_three, y_three, far_three = [swap_exp(three, bits) for bits in (2, 4, 6)]
    far_one, far_two = swap_rep(far_own, 1), swap_rep(far_own, 2)
    first = gathered(packed, x_own, y_own, far_own)
    first_other = swap_exp(first, 1)
    second = gathered(three, x_three, y_three, far_three)
    two, down_weight = ordered(two, down_weight)
    downs = fetched(down_weight, False)
    second, downs = ordered(second, downs)
    pair = gathered(one, two)
    x_pair, y_pair = swap_exp(pair, 2), swap_exp(pair, 4)

    near = [first, second, first_other, swap_exp(second, 1)]
    groups = row_groups([[5, 1], [6, 2], [7], [13, 9, 14, 10, 15], [4, 0, 3], [12, 8, 11]], rows)
    parts = experts_of(own, near, groups, gates, ups, downs, shard_units, top)
    *parts, x_pair, y_pair, far_one, far_two = ordered(*parts, x_pair, y_pair, far_one, far_two)
    to_x, to_y, to_far, other, near_kept, near_other = parts
    back = swap_exp(other, 1)
    to_x = rounded(to_x, back[: 2 * rows])
    to_y = rounded(to_y, back[2 * rows : 4 * rows])
    to_far = rounded(to_far, back[4 * rows :])
    to_x, to_y, to_far, near_other = ordered(to_x, to_y, to_far, near_other)
    near_x, near_y, near_far = swap_exp(to_x, 2), swap_exp(to_y, 4), swap_rep(to_far, 3)
    near_back = swap_exp(near_other, 1)

    far = [pair, x_pair, y_pair, far_one, far_two]
    far = far + [swap_exp(piece, 1) for piece in far]
    to_x, to_y, to_far, *far = ordered(to_x, to_y, to_far, *far)
    groups = row_groups([[6], [7], [2, 3], [4, 5], [10, 11, 12, 13, 8, 9], [14, 15], [0, 1]], rows)
    parts = experts_of(own, far, groups, gates, ups, downs, shard_units, top)
    to_one, to_two, to_x, to_y, other, other_far, far_kept = parts
    far_kept, near_far, near_y, near_x = ordered(far_kept, near_far, near_y, near_x)
    back = swap_exp(other, 1)
    kept = added(near_kept, near_back)
    to_three = rounded(kept[:rows], near_x[:rows], near_y[:rows])
    back, to_three = ordered(back, to_three)
    from_three = swap_rep(to_three, 3)
    to_x, to_y = rounded(to_x, back[: 2 * rows]), rounded(to_y, back[2 * rows : 4 * rows])
    to_x, to_y, other_far = ordered(to_x, to_y, other_far)
    far_x, far_y = swap_exp(to_x, 2), swap_exp(to_y, 4)
    back_far = swap_exp(other_far, 1)
    to_one, to_two = rounded(to_one, back_far[:rows]), rounded(to_two, back_far[rows:])
    from_two, from_one = swap_rep(to_two, 2), swap_rep(to_one, 1)

    own_sum = kept[rows : 2 * rows] + added(near_x[rows:], near_y[rows:])
    from_one, from_two, from_three = ordered(from_one, from_two, from_three)
    to_far = rounded(kept[2 * rows :], from_one, from_two, near_far)
    from_far = swap_exp(to_far, 6)
    to_one = rounded(far_kept[:rows], back[4 * rows : 5 * rows], far_x[:rows], far_y[:rows])
    to_two = rounded(far_kept[rows:], back[5 * rows :], far_x[rows:], far_y[rows:])
    arrived = [swap_rep(to_one, 1), swap_rep(to_two, 2)]
    return rounded(own_sum, from_three, from_far, *arrived)


def solution(mesh):
    placed = (
        P(("rep", "exp"), None),
        P(("rep", "exp"), None),
        P(("rep", "exp"), None),
        P("exp", "rep", None),
        P("exp", "rep", None),
        P("exp", "rep", None),
    )
    plane = mesh.shape["exp"] == 8 and mesh.shape["rep"] == 4
    return jax.shard_map(
        on_device_dense if plane else on_device_slots,
        mesh=mesh,
        in_specs=placed,
        out_specs=P(("rep", "exp"), None),
        check_vma=False,
    )
```

```python
import functools

import jax
import jax.numpy as jnp
from jax import lax
from jax.experimental import pallas as pl
from jax.experimental.pallas import tpu as pltpu
from jax.sharding import PartitionSpec as P


def slot_table(experts, expert_count, capacity):
    blocks = experts.shape[0]
    flattened = experts.reshape(blocks, -1)
    onehot = (
        flattened[:, :, None] == jnp.arange(expert_count, dtype=jnp.int32)[None, None, :]
    ).astype(jnp.int32)
    before = jnp.cumsum(onehot, axis=1) - onehot
    position = jnp.sum(before * onehot, axis=2)
    return flattened * capacity + position


def token_picks(slots, top_count, slot_count):
    blocks = slots.shape[0]
    grouped = slots.reshape(blocks, 1, -1, top_count)
    return jnp.any(grouped == jnp.arange(slot_count, dtype=jnp.int32)[None, :, None, None], axis=3)


def routing_column(route_weights, routed_experts):
    as_float = routed_experts.astype(jnp.float32)
    weights_all, experts_all = (
        lax.all_gather(route_weights, "rep", axis=0, tiled=True),
        lax.all_gather(as_float, "rep", axis=0, tiled=True),
    )
    return (weights_all, experts_all.astype(jnp.int32))


def on_device_slots(tokens, routed_experts, route_weights, gate_weight, up_weight, down_weight):
    replicas = lax.axis_size("rep")
    owners = lax.axis_size("exp")
    token_rows, model_width = tokens.shape
    top_count = routed_experts.shape[1]
    local_experts = gate_weight.shape[0]
    expert_count = local_experts * owners
    capacity = max(2, 3 * token_rows * top_count // (2 * expert_count))
    slot_count = expert_count * capacity
    own_slots = slot_table(routed_experts[None], expert_count, capacity)
    column = None
    column_slots = None
    selected = token_picks(own_slots, top_count, slot_count)[0].astype(jnp.bfloat16)
    buffer = jnp.dot(selected, tokens, preferred_element_type=jnp.float32).astype(jnp.bfloat16)
    buffer = buffer.reshape(owners, local_experts, capacity, model_width)
    arrived = lax.all_to_all(buffer, "exp", split_axis=0, concat_axis=2, tiled=True)
    rows_now = lax.all_gather(arrived, "rep", axis=2, tiled=True)[0]
    gate_value = jnp.einsum(
        "emd,efd->emf", rows_now, gate_weight, preferred_element_type=jnp.float32
    )
    up_value = jnp.einsum("emd,efd->emf", rows_now, up_weight, preferred_element_type=jnp.float32)
    hidden = (jax.nn.silu(gate_value) * up_value).astype(jnp.bfloat16)
    outcome = jnp.einsum("emf,efd->emd", hidden, down_weight, preferred_element_type=jnp.float32)
    outcome = lax.optimization_barrier(outcome.astype(jnp.bfloat16))
    outcomes = outcome[None]
    outcomes = outcomes.reshape(local_experts, replicas, owners, capacity, model_width)
    column = routing_column(route_weights, routed_experts)
    column_slots = slot_table(
        column[1].reshape(replicas, token_rows, top_count), expert_count, capacity
    )
    returned = lax.all_to_all(outcomes, "exp", split_axis=2, concat_axis=0, tiled=True)
    returned = returned.reshape(expert_count, replicas, capacity, model_width)
    expert_index = column_slots // capacity
    place_index = column_slots % capacity
    replica_index = jnp.broadcast_to(
        jnp.arange(replicas, dtype=jnp.int32)[:, None], column_slots.shape
    )
    picked = returned[expert_index, replica_index, place_index].astype(jnp.float32)
    column_weights = column[0].reshape(replicas, token_rows, top_count)
    weighted = jnp.sum(
        picked.reshape(replicas, token_rows, top_count, model_width)
        * column_weights[:, :, :, None],
        axis=2,
    )
    summed = lax.psum_scatter(weighted, "rep", scatter_dimension=0, tiled=True)
    return summed.reshape(token_rows, model_width).astype(jnp.bfloat16)


def fetch_kernel(turn, source_ref, result_ref):
    rows, width = source_ref.shape
    block = 512

    def fetch_block(step, carry):
        span = pl.ds(pl.multiple_of(step * block, block), block)
        if turn:
            for part in range(0, rows, 128):
                result_ref[span, part : part + 128] = source_ref[part : part + 128, span].T
        else:
            result_ref[:, span] = source_ref[:, span]
        return carry

    lax.fori_loop(0, width // block, fetch_block, 0)


def fetched(weight, turn):
    rows, width = weight.shape
    return pl.pallas_call(
        functools.partial(fetch_kernel, turn),
        out_shape=jax.ShapeDtypeStruct((width, rows) if turn else (rows, width), jnp.bfloat16),
        in_specs=[pl.BlockSpec(memory_space=pltpu.VMEM)],
        out_specs=pl.BlockSpec(memory_space=pltpu.VMEM),
        compiler_params=pltpu.CompilerParams(vmem_limit_bytes=4 * 1024 * 1024),
        cost_estimate=pl.CostEstimate(
            flops=0, bytes_accessed=4 * rows * width, transcendentals=0
        ),
        name="fetch_turned" if turn else "fetch",
    )(weight)


def gather_kernel(*refs):
    *pieces, whole_ref = refs
    start = 0
    for piece_ref in pieces:
        count = piece_ref.shape[0]
        whole_ref[start : start + count, :] = piece_ref[...]
        start += count


def gathered(*pieces):
    rows = sum(piece.shape[0] for piece in pieces)
    resident = pl.BlockSpec(memory_space=pltpu.VMEM)
    return pl.pallas_call(
        gather_kernel,
        out_shape=jax.ShapeDtypeStruct((rows, pieces[0].shape[1]), jnp.bfloat16),
        in_specs=[resident] * len(pieces),
        out_specs=resident,
        compiler_params=pltpu.CompilerParams(vmem_limit_bytes=2 * 1024 * 1024),
        name="gather",
    )(*pieces)


def expert_kernel(pieces_in, pieces_out, local_experts, shard_units, model_width, top, *refs):
    own_ref, refs = refs[0], refs[1:]
    ins, refs = refs[: len(pieces_in)], refs[len(pieces_in) :]
    (gate_ref, up_ref, down_ref), refs = refs[:3], refs[3:]
    outs, refs = refs[: len(pieces_out)], refs[len(pieces_out) :]
    rows, hidden = refs
    units = local_experts * shard_units
    unit_block = 256 if units % 256 == 0 else 128
    block = 512

    start = 0
    for place, count in enumerate(pieces_in):
        rows[start : start + count, :] = ins[place][...]
        start += count

    extra = rows[:, model_width:].astype(jnp.float32)
    width = extra.shape[1]
    scale = pltpu.roll(extra, width - top, 1) + pltpu.roll(extra, width - 2 * top, 1)
    lane = lax.broadcasted_iota(jnp.int32, extra.shape, 1)
    weights = []
    for expert in range(local_experts):
        name = (own_ref[0] + expert).astype(jnp.float32)
        chosen = jnp.logical_and(lane < top, extra == name)
        weights.append(jnp.sum(jnp.where(chosen, scale, 0.0), axis=1, keepdims=True))

    for begin in range(0, units, unit_block):
        span = slice(begin, begin + unit_block)
        values = rows[:, :model_width]
        gate = jnp.dot(values, gate_ref[:, span], preferred_element_type=jnp.float32)
        up = jnp.dot(values, up_ref[:, span], preferred_element_type=jnp.float32)
        unit = begin + lax.broadcasted_iota(jnp.int32, gate.shape, 1)
        weight = weights[begin // shard_units]
        for expert in range(begin // shard_units + 1, (begin + unit_block - 1) // shard_units + 1):
            weight = jnp.where(unit >= expert * shard_units, weights[expert], weight)
        active = gate / (1.0 + jnp.exp(-gate)) * up * weight
        hidden[:, span] = active.astype(jnp.bfloat16)

    for begin in range(0, model_width, block):
        span = slice(begin, begin + block)
        value = jnp.dot(hidden[...], down_ref[:, span], preferred_element_type=jnp.float32)
        value = value.astype(jnp.bfloat16)
        for place, segments in enumerate(pieces_out):
            filled = 0
            for first, count in segments:
                outs[place][filled : filled + count, span] = value[first : first + count]
                filled += count


def experts_of(own, pieces, pieces_out, gates, ups, downs, shard_units, top):
    units, model_width = downs.shape
    local_experts = units // shard_units
    pieces_in = [piece.shape[0] for piece in pieces]
    total = sum(pieces_in)
    packed = pieces[0].shape[1]
    resident = pl.BlockSpec(memory_space=pltpu.VMEM)
    kernel = functools.partial(
        expert_kernel, pieces_in, pieces_out, local_experts, shard_units, model_width, top
    )
    out_rows = [sum(count for _, count in segments) for segments in pieces_out]
    return pl.pallas_call(
        kernel,
        out_shape=[jax.ShapeDtypeStruct((count, model_width), jnp.bfloat16) for count in out_rows],
        in_specs=[pl.BlockSpec(memory_space=pltpu.SMEM)] + [resident] * (len(pieces) + 3),
        out_specs=[resident] * len(out_rows),
        scratch_shapes=[
            pltpu.VMEM((total, packed), jnp.bfloat16),
            pltpu.VMEM((total, units), jnp.bfloat16),
        ],
        compiler_params=pltpu.CompilerParams(vmem_limit_bytes=12 * 1024 * 1024),
        cost_estimate=pl.CostEstimate(
            flops=6 * total * units * model_width,
            bytes_accessed=4 * total * model_width,
            transcendentals=total * units,
        ),
        name="experts",
    )(own, *pieces, gates, ups, downs)


def pack_kernel(
    tokens_ref, experts_ref, weights_ref, packed_ref, experts, weights, sems
):
    model_width = tokens_ref.shape[1]
    copies = [
        pltpu.make_async_copy(experts_ref, experts, sems.at[0]),
        pltpu.make_async_copy(weights_ref, weights, sems.at[1]),
        pltpu.make_async_copy(tokens_ref, packed_ref.at[:, pl.ds(0, model_width)], sems.at[2]),
    ]
    for copy in copies:
        copy.start()
    copies[0].wait()
    copies[1].wait()
    values = weights[...]
    high = values.astype(jnp.bfloat16).astype(jnp.float32)
    listed = jnp.concatenate([experts[...].astype(jnp.float32), high, values - high], axis=0)
    width = packed_ref.shape[1] - model_width
    place = lax.broadcasted_iota(jnp.int32, (listed.shape[0], width), 0)
    lane = lax.broadcasted_iota(jnp.int32, (listed.shape[0], width), 1)
    chosen = jnp.where(place == lane, 1.0, 0.0).astype(jnp.bfloat16)
    extra = lax.dot_general(
        listed.astype(jnp.bfloat16),
        chosen,
        (((0,), (0,)), ((), ())),
        preferred_element_type=jnp.float32,
    )
    packed_ref[:, model_width:] = extra.astype(jnp.bfloat16)
    copies[2].wait()


def with_routing(tokens, routed_experts, route_weights):
    rows, width = tokens.shape
    top = routed_experts.shape[1]
    return pl.pallas_call(
        pack_kernel,
        out_shape=jax.ShapeDtypeStruct((rows, width + 128), jnp.bfloat16),
        in_specs=[pl.BlockSpec(memory_space=pl.ANY)] * 3,
        out_specs=pl.BlockSpec(memory_space=pltpu.VMEM),
        scratch_shapes=[
            pltpu.VMEM((top, rows), jnp.int32),
            pltpu.VMEM((top, rows), jnp.float32),
            pltpu.SemaphoreType.DMA((3,)),
        ],
        compiler_params=pltpu.CompilerParams(vmem_limit_bytes=2 * 1024 * 1024),
        name="pack",
    )(tokens, routed_experts.T, route_weights.T)


def begin_kernel(own_ref, gate_ref, up_ref, down_ref, index_ref):
    index_ref[0] = own_ref[0]


def begun(own, *weights):
    scalar = pl.BlockSpec(memory_space=pltpu.SMEM)
    return pl.pallas_call(
        begin_kernel,
        out_shape=jax.ShapeDtypeStruct((1,), jnp.int32),
        in_specs=[scalar] + [pl.BlockSpec(memory_space=pl.ANY)] * 3,
        out_specs=scalar,
        compiler_params=pltpu.CompilerParams(
            vmem_limit_bytes=50 * 1024 * 1024, has_side_effects=True
        ),
        name="begin",
    )(own, *weights)


def swap_exp(value, bits):
    owners = lax.axis_size("exp")
    return lax.ppermute(value, "exp", [(i, i ^ bits) for i in range(owners)])


def swap_rep(value, bits):
    replicas = lax.axis_size("rep")
    return lax.ppermute(value, "rep", [(i, i ^ bits) for i in range(replicas)])


def added(*terms):
    total = terms[0].astype(jnp.float32)
    for term in terms[1:]:
        total = total + term.astype(jnp.float32)
    return total


def rounded(*terms):
    return added(*terms).astype(jnp.bfloat16)


def ordered(*values):
    return lax.optimization_barrier(values)


def row_groups(places, rows):
    return [[(place * rows, rows) for place in group] for group in places]


def on_device_dense(tokens, routed_experts, route_weights, gate_weight, up_weight, down_weight):
    local_experts, shard_units, model_width = gate_weight.shape
    units = local_experts * shard_units
    top = routed_experts.shape[1]
    rows = tokens.shape[0]
    gate_weight = gate_weight.reshape(units, model_width)
    up_weight = up_weight.reshape(units, model_width)
    down_weight = down_weight.reshape(units, model_width)
    own = jnp.full((1,), lax.axis_index("exp") * local_experts, jnp.int32)
    begin = begun(own, gate_weight, up_weight, down_weight)
    tokens, own, begin = ordered(tokens, own, begin)
    packed = with_routing(tokens, routed_experts, route_weights)

    three = swap_rep(packed, 3)
    x_own, y_own, far_own = [swap_exp(packed, bits) for bits in (2, 4, 6)]
    gates, ups = fetched(gate_weight, True), fetched(up_weight, True)
    one = swap_rep(packed, 1)
    three, one, far_own, y_own, x_own, gates, ups, again = ordered(
        three, one, far_own, y_own, x_own, gates, ups, packed
    )
    two = swap_rep(again, 2)
    x_three, y_three, far_three = [swap_exp(three, bits) for bits in (2, 4, 6)]
    far_one, far_two = swap_rep(far_own, 1), swap_rep(far_own, 2)
    first = gathered(packed, x_own, y_own, far_own)
    first_other = swap_exp(first, 1)
    second = gathered(three, x_three, y_three, far_three)
    two, down_weight = ordered(two, down_weight)
    downs = fetched(down_weight, False)
    second, downs, far_one, far_two = ordered(second, downs, far_one, far_two)
    pair = gathered(one, two)
    x_pair, y_pair = swap_exp(pair, 2), swap_exp(pair, 4)

    near = [first, second, first_other, swap_exp(second, 1)]
    groups = row_groups([[5, 1], [6, 2], [7], [13, 9, 14, 10, 15], [4, 0, 3], [12, 8, 11]], rows)
    parts = experts_of(own, near, groups, gates, ups, downs, shard_units, top)
    *parts, x_pair, y_pair = ordered(*parts, x_pair, y_pair)
    to_x, to_y, to_far, other, near_kept, near_other = parts
    back = swap_exp(other, 1)
    to_x = rounded(to_x, back[: 2 * rows])
    to_y = rounded(to_y, back[2 * rows : 4 * rows])
    to_far = rounded(to_far, back[4 * rows :])
    to_x, to_y, to_far, near_other = ordered(to_x, to_y, to_far, near_other)
    near_x, near_y, near_far = swap_exp(to_x, 2), swap_exp(to_y, 4), swap_rep(to_far, 3)
    near_back = swap_exp(near_other, 1)

    far = [pair, x_pair, y_pair, far_one, far_two]
    far = far + [swap_exp(piece, 1) for piece in far]
    to_x, to_y, to_far, *far = ordered(to_x, to_y, to_far, *far)
    groups = row_groups([[6], [7], [2, 3], [4, 5], [10, 11, 12, 13, 8, 9], [14, 15], [0, 1]], rows)
    parts = experts_of(own, far, groups, gates, ups, downs, shard_units, top)
    to_one, to_two, to_x, to_y, other, other_far, far_kept = parts
    far_kept, near_x, near_y, near_far = ordered(far_kept, near_x, near_y, near_far)
    back = swap_exp(other, 1)
    kept = added(near_kept, near_back)
    to_three = rounded(kept[:rows], near_x[:rows], near_y[:rows])
    back, to_three = ordered(back, to_three)
    from_three = swap_rep(to_three, 3)
    to_x, to_y = rounded(to_x, back[: 2 * rows]), rounded(to_y, back[2 * rows : 4 * rows])
    to_x, to_y, other_far = ordered(to_x, to_y, other_far)
    far_x, far_y = swap_exp(to_x, 2), swap_exp(to_y, 4)
    back_far = swap_exp(other_far, 1)
    to_one, to_two = rounded(to_one, back_far[:rows]), rounded(to_two, back_far[rows:])
    from_two, from_one = swap_rep(to_two, 2), swap_rep(to_one, 1)

    own_sum = kept[rows : 2 * rows] + added(near_x[rows:], near_y[rows:])
    from_one, from_two, from_three = ordered(from_one, from_two, from_three)
    to_far = rounded(kept[2 * rows :], from_one, from_two, near_far)
    from_far = swap_exp(to_far, 6)
    to_one = rounded(far_kept[:rows], back[4 * rows : 5 * rows], far_x[:rows], far_y[:rows])
    to_two = rounded(far_kept[rows:], back[5 * rows :], far_x[rows:], far_y[rows:])
    arrived = [swap_rep(to_one, 1), swap_rep(to_two, 2)]
    return rounded(own_sum, from_three, from_far, *arrived)


def solution(mesh):
    placed = (
        P(("rep", "exp"), None),
        P(("rep", "exp"), None),
        P(("rep", "exp"), None),
        P("exp", "rep", None),
        P("exp", "rep", None),
        P("exp", "rep", None),
    )
    plane = mesh.shape["exp"] == 8 and mesh.shape["rep"] == 4
    return jax.shard_map(
        on_device_dense if plane else on_device_slots,
        mesh=mesh,
        in_specs=placed,
        out_specs=P(("rep", "exp"), None),
        check_vma=False,
    )
```

```python
import functools

import jax
import jax.numpy as jnp
from jax import lax
from jax.experimental import pallas as pl
from jax.experimental.pallas import tpu as pltpu
from jax.sharding import PartitionSpec as P


def slot_table(experts, expert_count, capacity):
    blocks = experts.shape[0]
    flattened = experts.reshape(blocks, -1)
    onehot = (
        flattened[:, :, None] == jnp.arange(expert_count, dtype=jnp.int32)[None, None, :]
    ).astype(jnp.int32)
    before = jnp.cumsum(onehot, axis=1) - onehot
    position = jnp.sum(before * onehot, axis=2)
    return flattened * capacity + position


def token_picks(slots, top_count, slot_count):
    blocks = slots.shape[0]
    grouped = slots.reshape(blocks, 1, -1, top_count)
    return jnp.any(grouped == jnp.arange(slot_count, dtype=jnp.int32)[None, :, None, None], axis=3)


def routing_column(route_weights, routed_experts):
    as_float = routed_experts.astype(jnp.float32)
    weights_all, experts_all = (
        lax.all_gather(route_weights, "rep", axis=0, tiled=True),
        lax.all_gather(as_float, "rep", axis=0, tiled=True),
    )
    return (weights_all, experts_all.astype(jnp.int32))


def on_device_slots(tokens, routed_experts, route_weights, gate_weight, up_weight, down_weight):
    replicas = lax.axis_size("rep")
    owners = lax.axis_size("exp")
    token_rows, model_width = tokens.shape
    top_count = routed_experts.shape[1]
    local_experts = gate_weight.shape[0]
    expert_count = local_experts * owners
    capacity = max(2, 3 * token_rows * top_count // (2 * expert_count))
    slot_count = expert_count * capacity
    own_slots = slot_table(routed_experts[None], expert_count, capacity)
    column = None
    column_slots = None
    selected = token_picks(own_slots, top_count, slot_count)[0].astype(jnp.bfloat16)
    buffer = jnp.dot(selected, tokens, preferred_element_type=jnp.float32).astype(jnp.bfloat16)
    buffer = buffer.reshape(owners, local_experts, capacity, model_width)
    arrived = lax.all_to_all(buffer, "exp", split_axis=0, concat_axis=2, tiled=True)
    rows_now = lax.all_gather(arrived, "rep", axis=2, tiled=True)[0]
    gate_value = jnp.einsum(
        "emd,efd->emf", rows_now, gate_weight, preferred_element_type=jnp.float32
    )
    up_value = jnp.einsum("emd,efd->emf", rows_now, up_weight, preferred_element_type=jnp.float32)
    hidden = (jax.nn.silu(gate_value) * up_value).astype(jnp.bfloat16)
    outcome = jnp.einsum("emf,efd->emd", hidden, down_weight, preferred_element_type=jnp.float32)
    outcome = lax.optimization_barrier(outcome.astype(jnp.bfloat16))
    outcomes = outcome[None]
    outcomes = outcomes.reshape(local_experts, replicas, owners, capacity, model_width)
    column = routing_column(route_weights, routed_experts)
    column_slots = slot_table(
        column[1].reshape(replicas, token_rows, top_count), expert_count, capacity
    )
    returned = lax.all_to_all(outcomes, "exp", split_axis=2, concat_axis=0, tiled=True)
    returned = returned.reshape(expert_count, replicas, capacity, model_width)
    expert_index = column_slots // capacity
    place_index = column_slots % capacity
    replica_index = jnp.broadcast_to(
        jnp.arange(replicas, dtype=jnp.int32)[:, None], column_slots.shape
    )
    picked = returned[expert_index, replica_index, place_index].astype(jnp.float32)
    column_weights = column[0].reshape(replicas, token_rows, top_count)
    weighted = jnp.sum(
        picked.reshape(replicas, token_rows, top_count, model_width)
        * column_weights[:, :, :, None],
        axis=2,
    )
    summed = lax.psum_scatter(weighted, "rep", scatter_dimension=0, tiled=True)
    return summed.reshape(token_rows, model_width).astype(jnp.bfloat16)


def fetch_kernel(turn, source_ref, result_ref):
    rows, width = source_ref.shape
    block = 512

    def fetch_block(step, carry):
        span = pl.ds(pl.multiple_of(step * block, block), block)
        if turn:
            for part in range(0, rows, 128):
                result_ref[span, part : part + 128] = source_ref[part : part + 128, span].T
        else:
            result_ref[:, span] = source_ref[:, span]
        return carry

    lax.fori_loop(0, width // block, fetch_block, 0)


def fetched(weight, turn):
    rows, width = weight.shape
    return pl.pallas_call(
        functools.partial(fetch_kernel, turn),
        out_shape=jax.ShapeDtypeStruct((width, rows) if turn else (rows, width), jnp.bfloat16),
        in_specs=[pl.BlockSpec(memory_space=pltpu.VMEM)],
        out_specs=pl.BlockSpec(memory_space=pltpu.VMEM),
        compiler_params=pltpu.CompilerParams(vmem_limit_bytes=4 * 1024 * 1024),
        cost_estimate=pl.CostEstimate(
            flops=0, bytes_accessed=4 * rows * width, transcendentals=0
        ),
        name="fetch_turned" if turn else "fetch",
    )(weight)


def gather_kernel(*refs):
    *pieces, whole_ref = refs
    start = 0
    for piece_ref in pieces:
        count = piece_ref.shape[0]
        whole_ref[start : start + count, :] = piece_ref[...]
        start += count


def gathered(*pieces):
    rows = sum(piece.shape[0] for piece in pieces)
    resident = pl.BlockSpec(memory_space=pltpu.VMEM)
    return pl.pallas_call(
        gather_kernel,
        out_shape=jax.ShapeDtypeStruct((rows, pieces[0].shape[1]), jnp.bfloat16),
        in_specs=[resident] * len(pieces),
        out_specs=resident,
        compiler_params=pltpu.CompilerParams(vmem_limit_bytes=2 * 1024 * 1024),
        name="gather",
    )(*pieces)


def expert_kernel(pieces_in, pieces_out, local_experts, shard_units, model_width, top, *refs):
    own_ref, refs = refs[0], refs[1:]
    ins, refs = refs[: len(pieces_in)], refs[len(pieces_in) :]
    (gate_ref, up_ref, down_ref), refs = refs[:3], refs[3:]
    outs, refs = refs[: len(pieces_out)], refs[len(pieces_out) :]
    rows, hidden = refs
    units = local_experts * shard_units
    unit_block = 256 if units % 256 == 0 else 128
    block = 512

    start = 0
    for place, count in enumerate(pieces_in):
        rows[start : start + count, :] = ins[place][...]
        start += count

    extra = rows[:, model_width:].astype(jnp.float32)
    width = extra.shape[1]
    scale = pltpu.roll(extra, width - top, 1) + pltpu.roll(extra, width - 2 * top, 1)
    lane = lax.broadcasted_iota(jnp.int32, extra.shape, 1)
    weights = []
    for expert in range(local_experts):
        name = (own_ref[0] + expert).astype(jnp.float32)
        chosen = jnp.logical_and(lane < top, extra == name)
        weights.append(jnp.sum(jnp.where(chosen, scale, 0.0), axis=1, keepdims=True))

    for begin in range(0, units, unit_block):
        span = slice(begin, begin + unit_block)
        values = rows[:, :model_width]
        gate = jnp.dot(values, gate_ref[:, span], preferred_element_type=jnp.float32)
        up = jnp.dot(values, up_ref[:, span], preferred_element_type=jnp.float32)
        unit = begin + lax.broadcasted_iota(jnp.int32, gate.shape, 1)
        weight = weights[begin // shard_units]
        for expert in range(begin // shard_units + 1, (begin + unit_block - 1) // shard_units + 1):
            weight = jnp.where(unit >= expert * shard_units, weights[expert], weight)
        active = gate / (1.0 + jnp.exp(-gate)) * up * weight
        hidden[:, span] = active.astype(jnp.bfloat16)

    for begin in range(0, model_width, block):
        span = slice(begin, begin + block)
        value = jnp.dot(hidden[...], down_ref[:, span], preferred_element_type=jnp.float32)
        value = value.astype(jnp.bfloat16)
        for place, segments in enumerate(pieces_out):
            filled = 0
            for first, count in segments:
                outs[place][filled : filled + count, span] = value[first : first + count]
                filled += count


def experts_of(own, pieces, pieces_out, gates, ups, downs, shard_units, top):
    units, model_width = downs.shape
    local_experts = units // shard_units
    pieces_in = [piece.shape[0] for piece in pieces]
    total = sum(pieces_in)
    packed = pieces[0].shape[1]
    resident = pl.BlockSpec(memory_space=pltpu.VMEM)
    kernel = functools.partial(
        expert_kernel, pieces_in, pieces_out, local_experts, shard_units, model_width, top
    )
    out_rows = [sum(count for _, count in segments) for segments in pieces_out]
    return pl.pallas_call(
        kernel,
        out_shape=[jax.ShapeDtypeStruct((count, model_width), jnp.bfloat16) for count in out_rows],
        in_specs=[pl.BlockSpec(memory_space=pltpu.SMEM)] + [resident] * (len(pieces) + 3),
        out_specs=[resident] * len(out_rows),
        scratch_shapes=[
            pltpu.VMEM((total, packed), jnp.bfloat16),
            pltpu.VMEM((total, units), jnp.bfloat16),
        ],
        compiler_params=pltpu.CompilerParams(vmem_limit_bytes=12 * 1024 * 1024),
        cost_estimate=pl.CostEstimate(
            flops=6 * total * units * model_width,
            bytes_accessed=4 * total * model_width,
            transcendentals=total * units,
        ),
        name="experts",
    )(own, *pieces, gates, ups, downs)


def pack_kernel(
    tokens_ref, experts_ref, weights_ref, packed_ref, experts, weights, sems
):
    model_width = tokens_ref.shape[1]
    copies = [
        pltpu.make_async_copy(experts_ref, experts, sems.at[0]),
        pltpu.make_async_copy(weights_ref, weights, sems.at[1]),
        pltpu.make_async_copy(tokens_ref, packed_ref.at[:, pl.ds(0, model_width)], sems.at[2]),
    ]
    for copy in copies:
        copy.start()
    copies[0].wait()
    copies[1].wait()
    values = weights[...]
    high = values.astype(jnp.bfloat16).astype(jnp.float32)
    listed = jnp.concatenate([experts[...].astype(jnp.float32), high, values - high], axis=0)
    width = packed_ref.shape[1] - model_width
    place = lax.broadcasted_iota(jnp.int32, (listed.shape[0], width), 0)
    lane = lax.broadcasted_iota(jnp.int32, (listed.shape[0], width), 1)
    chosen = jnp.where(place == lane, 1.0, 0.0).astype(jnp.bfloat16)
    extra = lax.dot_general(
        listed.astype(jnp.bfloat16),
        chosen,
        (((0,), (0,)), ((), ())),
        preferred_element_type=jnp.float32,
    )
    packed_ref[:, model_width:] = extra.astype(jnp.bfloat16)
    copies[2].wait()


def with_routing(tokens, routed_experts, route_weights):
    rows, width = tokens.shape
    top = routed_experts.shape[1]
    return pl.pallas_call(
        pack_kernel,
        out_shape=jax.ShapeDtypeStruct((rows, width + 128), jnp.bfloat16),
        in_specs=[pl.BlockSpec(memory_space=pl.ANY)] * 3,
        out_specs=pl.BlockSpec(memory_space=pltpu.VMEM),
        scratch_shapes=[
            pltpu.VMEM((top, rows), jnp.int32),
            pltpu.VMEM((top, rows), jnp.float32),
            pltpu.SemaphoreType.DMA((3,)),
        ],
        compiler_params=pltpu.CompilerParams(vmem_limit_bytes=2 * 1024 * 1024),
        name="pack",
    )(tokens, routed_experts.T, route_weights.T)


def begin_kernel(own_ref, gate_ref, up_ref, down_ref, index_ref):
    index_ref[0] = own_ref[0]


def begun(own, *weights):
    scalar = pl.BlockSpec(memory_space=pltpu.SMEM)
    return pl.pallas_call(
        begin_kernel,
        out_shape=jax.ShapeDtypeStruct((1,), jnp.int32),
        in_specs=[scalar] + [pl.BlockSpec(memory_space=pl.ANY)] * 3,
        out_specs=scalar,
        compiler_params=pltpu.CompilerParams(
            vmem_limit_bytes=50 * 1024 * 1024, has_side_effects=True
        ),
        name="begin",
    )(own, *weights)


def swap_exp(value, bits):
    owners = lax.axis_size("exp")
    return lax.ppermute(value, "exp", [(i, i ^ bits) for i in range(owners)])


def swap_rep(value, bits):
    replicas = lax.axis_size("rep")
    return lax.ppermute(value, "rep", [(i, i ^ bits) for i in range(replicas)])


def added(*terms):
    total = terms[0].astype(jnp.float32)
    for term in terms[1:]:
        total = total + term.astype(jnp.float32)
    return total


def rounded(*terms):
    return added(*terms).astype(jnp.bfloat16)


def ordered(*values):
    return lax.optimization_barrier(values)


def row_groups(places, rows):
    return [[(place * rows, rows) for place in group] for group in places]


def on_device_dense(tokens, routed_experts, route_weights, gate_weight, up_weight, down_weight):
    local_experts, shard_units, model_width = gate_weight.shape
    units = local_experts * shard_units
    top = routed_experts.shape[1]
    rows = tokens.shape[0]
    gate_weight = gate_weight.reshape(units, model_width)
    up_weight = up_weight.reshape(units, model_width)
    down_weight = down_weight.reshape(units, model_width)
    own = jnp.full((1,), lax.axis_index("exp") * local_experts, jnp.int32)
    begin = begun(own, gate_weight, up_weight, down_weight)
    tokens, own, begin = ordered(tokens, own, begin)
    packed = with_routing(tokens, routed_experts, route_weights)

    two = swap_rep(packed, 2)
    x_own, y_own, far_own = [swap_exp(packed, bits) for bits in (2, 4, 6)]
    gates, ups = fetched(gate_weight, True), fetched(up_weight, True)
    one = swap_rep(packed, 1)
    x_own, y_own, far_own, one, two, gates, ups = ordered(
        x_own, y_own, far_own, one, two, gates, ups
    )
    three = swap_rep(two, 1)
    x_two, y_two, far_two = [swap_exp(two, bits) for bits in (2, 4, 6)]
    far_one, far_three = swap_rep(far_own, 1), swap_rep(far_two, 1)
    first = gathered(packed, x_own, y_own, far_own)
    first_other = swap_exp(first, 1)
    second = gathered(two, x_two, y_two, far_two)
    three, down_weight = ordered(three, down_weight)
    downs = fetched(down_weight, False)
    second, downs = ordered(second, downs)
    pair = gathered(one, three)
    x_pair, y_pair = swap_exp(pair, 2), swap_exp(pair, 4)

    near = [first, second, first_other, swap_exp(second, 1)]
    groups = row_groups([[5, 1], [6, 2], [7], [13, 9, 14, 10, 15], [4, 0, 3], [12, 8, 11]], rows)
    parts = experts_of(own, near, groups, gates, ups, downs, shard_units, top)
    *parts, x_pair, y_pair, far_one, far_three = ordered(
        *parts, x_pair, y_pair, far_one, far_three
    )
    to_x, to_y, to_far, other, near_kept, near_other = parts
    back = swap_exp(other, 1)
    to_x = rounded(to_x, back[: 2 * rows])
    to_y = rounded(to_y, back[2 * rows : 4 * rows])
    to_far = rounded(to_far, back[4 * rows :])
    to_x, to_y, to_far, near_other = ordered(to_x, to_y, to_far, near_other)
    near_x, near_y, near_far = swap_exp(to_x, 2), swap_exp(to_y, 4), swap_rep(to_far, 2)
    near_back = swap_exp(near_other, 1)

    far = [pair, x_pair, y_pair, far_one, far_three]
    far = far + [swap_exp(piece, 1) for piece in far]
    to_x, to_y, to_far, *far = ordered(to_x, to_y, to_far, *far)
    groups = row_groups([[6], [7], [2, 3], [4, 5], [10, 11, 12, 13, 8, 9], [14, 15], [0, 1]], rows)
    parts = experts_of(own, far, groups, gates, ups, downs, shard_units, top)
    to_one, to_three, to_x, to_y, other, other_far, far_kept = parts
    far_kept, near_far, near_y, near_x = ordered(far_kept, near_far, near_y, near_x)
    back = swap_exp(other, 1)
    kept = added(near_kept, near_back)
    to_two = rounded(kept[:rows], near_x[:rows], near_y[:rows])
    back, to_two = ordered(back, to_two)
    from_two = swap_rep(to_two, 2)
    to_x, to_y = rounded(to_x, back[: 2 * rows]), rounded(to_y, back[2 * rows : 4 * rows])
    to_x, to_y, other_far = ordered(to_x, to_y, other_far)
    far_x, far_y = swap_exp(to_x, 2), swap_exp(to_y, 4)
    back_far = swap_exp(other_far, 1)
    to_one, to_three = rounded(to_one, back_far[:rows]), rounded(to_three, back_far[rows:])
    from_three, from_one = swap_rep(to_three, 3), swap_rep(to_one, 1)

    own_sum = kept[rows : 2 * rows] + added(near_x[rows:], near_y[rows:])
    from_one, from_three, from_two = ordered(from_one, from_three, from_two)
    to_far = rounded(kept[2 * rows :], from_one, from_three, near_far)
    from_far = swap_exp(to_far, 6)
    to_one = rounded(far_kept[:rows], back[4 * rows : 5 * rows], far_x[:rows], far_y[:rows])
    to_three = rounded(far_kept[rows:], back[5 * rows :], far_x[rows:], far_y[rows:])
    arrived = [swap_rep(to_one, 1), swap_rep(to_three, 3)]
    return rounded(own_sum, from_two, from_far, *arrived)


def solution(mesh):
    placed = (
        P(("rep", "exp"), None),
        P(("rep", "exp"), None),
        P(("rep", "exp"), None),
        P("exp", "rep", None),
        P("exp", "rep", None),
        P("exp", "rep", None),
    )
    plane = mesh.shape["exp"] == 8 and mesh.shape["rep"] == 4
    return jax.shard_map(
        on_device_dense if plane else on_device_slots,
        mesh=mesh,
        in_specs=placed,
        out_specs=P(("rep", "exp"), None),
        check_vma=False,
    )
```

```python
import functools

import jax
import jax.numpy as jnp
from jax import lax
from jax.experimental import pallas as pl
from jax.experimental.pallas import tpu as pltpu
from jax.sharding import PartitionSpec as P


def slot_table(experts, expert_count, capacity):
    blocks = experts.shape[0]
    flattened = experts.reshape(blocks, -1)
    onehot = (
        flattened[:, :, None] == jnp.arange(expert_count, dtype=jnp.int32)[None, None, :]
    ).astype(jnp.int32)
    before = jnp.cumsum(onehot, axis=1) - onehot
    position = jnp.sum(before * onehot, axis=2)
    return flattened * capacity + position


def token_picks(slots, top_count, slot_count):
    blocks = slots.shape[0]
    grouped = slots.reshape(blocks, 1, -1, top_count)
    return jnp.any(grouped == jnp.arange(slot_count, dtype=jnp.int32)[None, :, None, None], axis=3)


def routing_column(route_weights, routed_experts):
    as_float = routed_experts.astype(jnp.float32)
    weights_all, experts_all = (
        lax.all_gather(route_weights, "rep", axis=0, tiled=True),
        lax.all_gather(as_float, "rep", axis=0, tiled=True),
    )
    return (weights_all, experts_all.astype(jnp.int32))


def on_device_slots(tokens, routed_experts, route_weights, gate_weight, up_weight, down_weight):
    replicas = lax.axis_size("rep")
    owners = lax.axis_size("exp")
    token_rows, model_width = tokens.shape
    top_count = routed_experts.shape[1]
    local_experts = gate_weight.shape[0]
    expert_count = local_experts * owners
    capacity = max(2, 3 * token_rows * top_count // (2 * expert_count))
    slot_count = expert_count * capacity
    own_slots = slot_table(routed_experts[None], expert_count, capacity)
    column = None
    column_slots = None
    selected = token_picks(own_slots, top_count, slot_count)[0].astype(jnp.bfloat16)
    buffer = jnp.dot(selected, tokens, preferred_element_type=jnp.float32).astype(jnp.bfloat16)
    buffer = buffer.reshape(owners, local_experts, capacity, model_width)
    arrived = lax.all_to_all(buffer, "exp", split_axis=0, concat_axis=2, tiled=True)
    rows_now = lax.all_gather(arrived, "rep", axis=2, tiled=True)[0]
    gate_value = jnp.einsum(
        "emd,efd->emf", rows_now, gate_weight, preferred_element_type=jnp.float32
    )
    up_value = jnp.einsum("emd,efd->emf", rows_now, up_weight, preferred_element_type=jnp.float32)
    hidden = (jax.nn.silu(gate_value) * up_value).astype(jnp.bfloat16)
    outcome = jnp.einsum("emf,efd->emd", hidden, down_weight, preferred_element_type=jnp.float32)
    outcome = lax.optimization_barrier(outcome.astype(jnp.bfloat16))
    outcomes = outcome[None]
    outcomes = outcomes.reshape(local_experts, replicas, owners, capacity, model_width)
    column = routing_column(route_weights, routed_experts)
    column_slots = slot_table(
        column[1].reshape(replicas, token_rows, top_count), expert_count, capacity
    )
    returned = lax.all_to_all(outcomes, "exp", split_axis=2, concat_axis=0, tiled=True)
    returned = returned.reshape(expert_count, replicas, capacity, model_width)
    expert_index = column_slots // capacity
    place_index = column_slots % capacity
    replica_index = jnp.broadcast_to(
        jnp.arange(replicas, dtype=jnp.int32)[:, None], column_slots.shape
    )
    picked = returned[expert_index, replica_index, place_index].astype(jnp.float32)
    column_weights = column[0].reshape(replicas, token_rows, top_count)
    weighted = jnp.sum(
        picked.reshape(replicas, token_rows, top_count, model_width)
        * column_weights[:, :, :, None],
        axis=2,
    )
    summed = lax.psum_scatter(weighted, "rep", scatter_dimension=0, tiled=True)
    return summed.reshape(token_rows, model_width).astype(jnp.bfloat16)


def fetch_kernel(turn, source_ref, result_ref):
    rows, width = source_ref.shape
    block = 512

    def fetch_block(step, carry):
        span = pl.ds(pl.multiple_of(step * block, block), block)
        if turn:
            for part in range(0, rows, 128):
                result_ref[span, part : part + 128] = source_ref[part : part + 128, span].T
        else:
            result_ref[:, span] = source_ref[:, span]
        return carry

    lax.fori_loop(0, width // block, fetch_block, 0)


def fetched(weight, turn):
    rows, width = weight.shape
    return pl.pallas_call(
        functools.partial(fetch_kernel, turn),
        out_shape=jax.ShapeDtypeStruct((width, rows) if turn else (rows, width), jnp.bfloat16),
        in_specs=[pl.BlockSpec(memory_space=pltpu.VMEM)],
        out_specs=pl.BlockSpec(memory_space=pltpu.VMEM),
        compiler_params=pltpu.CompilerParams(vmem_limit_bytes=4 * 1024 * 1024),
        cost_estimate=pl.CostEstimate(
            flops=0, bytes_accessed=4 * rows * width, transcendentals=0
        ),
        name="fetch_turned" if turn else "fetch",
    )(weight)


def gather_kernel(*refs):
    *pieces, whole_ref = refs
    start = 0
    for piece_ref in pieces:
        count = piece_ref.shape[0]
        whole_ref[start : start + count, :] = piece_ref[...]
        start += count


def gathered(*pieces):
    rows = sum(piece.shape[0] for piece in pieces)
    resident = pl.BlockSpec(memory_space=pltpu.VMEM)
    return pl.pallas_call(
        gather_kernel,
        out_shape=jax.ShapeDtypeStruct((rows, pieces[0].shape[1]), jnp.bfloat16),
        in_specs=[resident] * len(pieces),
        out_specs=resident,
        compiler_params=pltpu.CompilerParams(vmem_limit_bytes=2 * 1024 * 1024),
        name="gather",
    )(*pieces)


def expert_kernel(pieces_in, pieces_out, local_experts, shard_units, model_width, top, *refs):
    own_ref, refs = refs[0], refs[1:]
    ins, refs = refs[: len(pieces_in)], refs[len(pieces_in) :]
    (gate_ref, up_ref, down_ref), refs = refs[:3], refs[3:]
    outs, refs = refs[: len(pieces_out)], refs[len(pieces_out) :]
    rows, hidden = refs
    units = local_experts * shard_units
    unit_block = 256 if units % 256 == 0 else 128
    block = 512

    start = 0
    for place, count in enumerate(pieces_in):
        rows[start : start + count, :] = ins[place][...]
        start += count

    extra = rows[:, model_width:].astype(jnp.float32)
    width = extra.shape[1]
    scale = pltpu.roll(extra, width - top, 1) + pltpu.roll(extra, width - 2 * top, 1)
    lane = lax.broadcasted_iota(jnp.int32, extra.shape, 1)
    weights = []
    for expert in range(local_experts):
        name = (own_ref[0] + expert).astype(jnp.float32)
        chosen = jnp.logical_and(lane < top, extra == name)
        weights.append(jnp.sum(jnp.where(chosen, scale, 0.0), axis=1, keepdims=True))

    for begin in range(0, units, unit_block):
        span = slice(begin, begin + unit_block)
        values = rows[:, :model_width]
        gate = jnp.dot(values, gate_ref[:, span], preferred_element_type=jnp.float32)
        up = jnp.dot(values, up_ref[:, span], preferred_element_type=jnp.float32)
        unit = begin + lax.broadcasted_iota(jnp.int32, gate.shape, 1)
        weight = weights[begin // shard_units]
        for expert in range(begin // shard_units + 1, (begin + unit_block - 1) // shard_units + 1):
            weight = jnp.where(unit >= expert * shard_units, weights[expert], weight)
        active = gate / (1.0 + jnp.exp(-gate)) * up * weight
        hidden[:, span] = active.astype(jnp.bfloat16)

    for begin in range(0, model_width, block):
        span = slice(begin, begin + block)
        value = jnp.dot(hidden[...], down_ref[:, span], preferred_element_type=jnp.float32)
        value = value.astype(jnp.bfloat16)
        for place, segments in enumerate(pieces_out):
            filled = 0
            for first, count in segments:
                outs[place][filled : filled + count, span] = value[first : first + count]
                filled += count


def experts_of(own, pieces, pieces_out, gates, ups, downs, shard_units, top):
    units, model_width = downs.shape
    local_experts = units // shard_units
    pieces_in = [piece.shape[0] for piece in pieces]
    total = sum(pieces_in)
    packed = pieces[0].shape[1]
    resident = pl.BlockSpec(memory_space=pltpu.VMEM)
    kernel = functools.partial(
        expert_kernel, pieces_in, pieces_out, local_experts, shard_units, model_width, top
    )
    out_rows = [sum(count for _, count in segments) for segments in pieces_out]
    return pl.pallas_call(
        kernel,
        out_shape=[jax.ShapeDtypeStruct((count, model_width), jnp.bfloat16) for count in out_rows],
        in_specs=[pl.BlockSpec(memory_space=pltpu.SMEM)] + [resident] * (len(pieces) + 3),
        out_specs=[resident] * len(out_rows),
        scratch_shapes=[
            pltpu.VMEM((total, packed), jnp.bfloat16),
            pltpu.VMEM((total, units), jnp.bfloat16),
        ],
        compiler_params=pltpu.CompilerParams(vmem_limit_bytes=12 * 1024 * 1024),
        cost_estimate=pl.CostEstimate(
            flops=6 * total * units * model_width,
            bytes_accessed=4 * total * model_width,
            transcendentals=total * units,
        ),
        name="experts",
    )(own, *pieces, gates, ups, downs)


def pack_kernel(
    tokens_ref, experts_ref, weights_ref, packed_ref, experts, weights, sems
):
    model_width = tokens_ref.shape[1]
    copies = [
        pltpu.make_async_copy(experts_ref, experts, sems.at[0]),
        pltpu.make_async_copy(weights_ref, weights, sems.at[1]),
        pltpu.make_async_copy(tokens_ref, packed_ref.at[:, pl.ds(0, model_width)], sems.at[2]),
    ]
    for copy in copies:
        copy.start()
    copies[0].wait()
    copies[1].wait()
    values = weights[...]
    high = values.astype(jnp.bfloat16).astype(jnp.float32)
    listed = jnp.concatenate([experts[...].astype(jnp.float32), high, values - high], axis=0)
    width = packed_ref.shape[1] - model_width
    place = lax.broadcasted_iota(jnp.int32, (listed.shape[0], width), 0)
    lane = lax.broadcasted_iota(jnp.int32, (listed.shape[0], width), 1)
    chosen = jnp.where(place == lane, 1.0, 0.0).astype(jnp.bfloat16)
    extra = lax.dot_general(
        listed.astype(jnp.bfloat16),
        chosen,
        (((0,), (0,)), ((), ())),
        preferred_element_type=jnp.float32,
    )
    packed_ref[:, model_width:] = extra.astype(jnp.bfloat16)
    copies[2].wait()


def with_routing(tokens, routed_experts, route_weights):
    rows, width = tokens.shape
    top = routed_experts.shape[1]
    return pl.pallas_call(
        pack_kernel,
        out_shape=jax.ShapeDtypeStruct((rows, width + 128), jnp.bfloat16),
        in_specs=[pl.BlockSpec(memory_space=pl.ANY)] * 3,
        out_specs=pl.BlockSpec(memory_space=pltpu.VMEM),
        scratch_shapes=[
            pltpu.VMEM((top, rows), jnp.int32),
            pltpu.VMEM((top, rows), jnp.float32),
            pltpu.SemaphoreType.DMA((3,)),
        ],
        compiler_params=pltpu.CompilerParams(vmem_limit_bytes=2 * 1024 * 1024),
        name="pack",
    )(tokens, routed_experts.T, route_weights.T)


def begin_kernel(own_ref, gate_ref, up_ref, down_ref, index_ref):
    index_ref[0] = own_ref[0]


def begun(own, *weights):
    scalar = pl.BlockSpec(memory_space=pltpu.SMEM)
    return pl.pallas_call(
        begin_kernel,
        out_shape=jax.ShapeDtypeStruct((1,), jnp.int32),
        in_specs=[scalar] + [pl.BlockSpec(memory_space=pl.ANY)] * 3,
        out_specs=scalar,
        compiler_params=pltpu.CompilerParams(
            vmem_limit_bytes=50 * 1024 * 1024, has_side_effects=True
        ),
        name="begin",
    )(own, *weights)


def swap_exp(value, bits):
    owners = lax.axis_size("exp")
    return lax.ppermute(value, "exp", [(i, i ^ bits) for i in range(owners)])


def swap_rep(value, bits):
    replicas = lax.axis_size("rep")
    return lax.ppermute(value, "rep", [(i, i ^ bits) for i in range(replicas)])


def added(*terms):
    total = terms[0].astype(jnp.float32)
    for term in terms[1:]:
        total = total + term.astype(jnp.float32)
    return total


def rounded(*terms):
    return added(*terms).astype(jnp.bfloat16)


def ordered(*values):
    return lax.optimization_barrier(values)


def row_groups(places, rows):
    return [[(place * rows, rows) for place in group] for group in places]


def on_device_dense(tokens, routed_experts, route_weights, gate_weight, up_weight, down_weight):
    local_experts, shard_units, model_width = gate_weight.shape
    units = local_experts * shard_units
    top = routed_experts.shape[1]
    rows = tokens.shape[0]
    gate_weight = gate_weight.reshape(units, model_width)
    up_weight = up_weight.reshape(units, model_width)
    down_weight = down_weight.reshape(units, model_width)
    own = jnp.full((1,), lax.axis_index("exp") * local_experts, jnp.int32)
    begin = begun(own, gate_weight, up_weight, down_weight)
    tokens, own, begin = ordered(tokens, own, begin)
    packed = with_routing(tokens, routed_experts, route_weights)

    two = swap_rep(packed, 2)
    x_own, y_own, far_own = [swap_exp(packed, bits) for bits in (2, 4, 6)]
    gates, ups = fetched(gate_weight, True), fetched(up_weight, True)
    one = swap_rep(packed, 1)
    x_own, y_own, far_own, one, two, gates, ups = ordered(
        x_own, y_own, far_own, one, two, gates, ups
    )
    three = swap_rep(two, 1)
    x_two, y_two, far_two = [swap_exp(two, bits) for bits in (2, 4, 6)]
    first = gathered(packed, x_own, y_own, far_own)
    first_other = swap_exp(first, 1)
    second = gathered(two, x_two, y_two, far_two)
    three, down_weight = ordered(three, down_weight)
    downs = fetched(down_weight, False)
    second, downs = ordered(second, downs)
    pair = gathered(one, three)
    pair, far_own, far_two = ordered(pair, far_own, far_two)
    x_pair, y_pair = swap_exp(pair, 2), swap_exp(pair, 4)
    far_one, far_three = swap_rep(far_own, 1), swap_rep(far_two, 1)

    near = [first, second, first_other, swap_exp(second, 1)]
    groups = row_groups([[5, 1], [6, 2], [7], [13, 9, 14, 10, 15], [4, 0, 3], [12, 8, 11]], rows)
    parts = experts_of(own, near, groups, gates, ups, downs, shard_units, top)
    *parts, x_pair, y_pair, far_one, far_three = ordered(
        *parts, x_pair, y_pair, far_one, far_three
    )
    to_x, to_y, to_far, other, near_kept, near_other = parts
    back = swap_exp(other, 1)
    to_x = rounded(to_x, back[: 2 * rows])
    to_y = rounded(to_y, back[2 * rows : 4 * rows])
    to_far = rounded(to_far, back[4 * rows :])
    to_x, to_y, to_far, near_other = ordered(to_x, to_y, to_far, near_other)
    near_x, near_y, near_far = swap_exp(to_x, 2), swap_exp(to_y, 4), swap_rep(to_far, 2)
    near_back = swap_exp(near_other, 1)

    far = [pair, x_pair, y_pair, far_one, far_three]
    far = far + [swap_exp(piece, 1) for piece in far]
    to_x, to_y, to_far, *far = ordered(to_x, to_y, to_far, *far)
    groups = row_groups([[6], [7], [2, 3], [4, 5], [10, 11, 12, 13, 8, 9], [14, 15], [0, 1]], rows)
    parts = experts_of(own, far, groups, gates, ups, downs, shard_units, top)
    to_one, to_three, to_x, to_y, other, other_far, far_kept = parts
    far_kept, near_far, near_y, near_x = ordered(far_kept, near_far, near_y, near_x)
    back = swap_exp(other, 1)
    kept = added(near_kept, near_back)
    to_two = rounded(kept[:rows], near_x[:rows], near_y[:rows])
    back, to_two = ordered(back, to_two)
    from_two = swap_rep(to_two, 2)
    to_x, to_y = rounded(to_x, back[: 2 * rows]), rounded(to_y, back[2 * rows : 4 * rows])
    to_x, to_y, other_far = ordered(to_x, to_y, other_far)
    far_x, far_y = swap_exp(to_x, 2), swap_exp(to_y, 4)
    back_far = swap_exp(other_far, 1)
    to_one, to_three = rounded(to_one, back_far[:rows]), rounded(to_three, back_far[rows:])
    from_three, from_one = swap_rep(to_three, 3), swap_rep(to_one, 1)

    own_sum = kept[rows : 2 * rows] + added(near_x[rows:], near_y[rows:])
    from_one, from_three, from_two = ordered(from_one, from_three, from_two)
    to_far = rounded(kept[2 * rows :], from_one, from_three, near_far)
    from_far = swap_exp(to_far, 6)
    to_one = rounded(far_kept[:rows], back[4 * rows : 5 * rows], far_x[:rows], far_y[:rows])
    to_three = rounded(far_kept[rows:], back[5 * rows :], far_x[rows:], far_y[rows:])
    arrived = [swap_rep(to_one, 1), swap_rep(to_three, 3)]
    return rounded(own_sum, from_two, from_far, *arrived)


def solution(mesh):
    placed = (
        P(("rep", "exp"), None),
        P(("rep", "exp"), None),
        P(("rep", "exp"), None),
        P("exp", "rep", None),
        P("exp", "rep", None),
        P("exp", "rep", None),
    )
    plane = mesh.shape["exp"] == 8 and mesh.shape["rep"] == 4
    return jax.shard_map(
        on_device_dense if plane else on_device_slots,
        mesh=mesh,
        in_specs=placed,
        out_specs=P(("rep", "exp"), None),
        check_vma=False,
    )
```

```python
import functools

import jax
import jax.numpy as jnp
from jax import lax
from jax.experimental import pallas as pl
from jax.experimental.pallas import tpu as pltpu
from jax.sharding import PartitionSpec as P


def slot_table(experts, expert_count, capacity):
    blocks = experts.shape[0]
    flattened = experts.reshape(blocks, -1)
    onehot = (
        flattened[:, :, None] == jnp.arange(expert_count, dtype=jnp.int32)[None, None, :]
    ).astype(jnp.int32)
    before = jnp.cumsum(onehot, axis=1) - onehot
    position = jnp.sum(before * onehot, axis=2)
    return flattened * capacity + position


def token_picks(slots, top_count, slot_count):
    blocks = slots.shape[0]
    grouped = slots.reshape(blocks, 1, -1, top_count)
    return jnp.any(grouped == jnp.arange(slot_count, dtype=jnp.int32)[None, :, None, None], axis=3)


def routing_column(route_weights, routed_experts):
    as_float = routed_experts.astype(jnp.float32)
    weights_all, experts_all = (
        lax.all_gather(route_weights, "rep", axis=0, tiled=True),
        lax.all_gather(as_float, "rep", axis=0, tiled=True),
    )
    return (weights_all, experts_all.astype(jnp.int32))


def on_device_slots(tokens, routed_experts, route_weights, gate_weight, up_weight, down_weight):
    replicas = lax.axis_size("rep")
    owners = lax.axis_size("exp")
    token_rows, model_width = tokens.shape
    top_count = routed_experts.shape[1]
    local_experts = gate_weight.shape[0]
    expert_count = local_experts * owners
    capacity = max(2, 3 * token_rows * top_count // (2 * expert_count))
    slot_count = expert_count * capacity
    own_slots = slot_table(routed_experts[None], expert_count, capacity)
    column = None
    column_slots = None
    selected = token_picks(own_slots, top_count, slot_count)[0].astype(jnp.bfloat16)
    buffer = jnp.dot(selected, tokens, preferred_element_type=jnp.float32).astype(jnp.bfloat16)
    buffer = buffer.reshape(owners, local_experts, capacity, model_width)
    arrived = lax.all_to_all(buffer, "exp", split_axis=0, concat_axis=2, tiled=True)
    rows_now = lax.all_gather(arrived, "rep", axis=2, tiled=True)[0]
    gate_value = jnp.einsum(
        "emd,efd->emf", rows_now, gate_weight, preferred_element_type=jnp.float32
    )
    up_value = jnp.einsum("emd,efd->emf", rows_now, up_weight, preferred_element_type=jnp.float32)
    hidden = (jax.nn.silu(gate_value) * up_value).astype(jnp.bfloat16)
    outcome = jnp.einsum("emf,efd->emd", hidden, down_weight, preferred_element_type=jnp.float32)
    outcome = lax.optimization_barrier(outcome.astype(jnp.bfloat16))
    outcomes = outcome[None]
    outcomes = outcomes.reshape(local_experts, replicas, owners, capacity, model_width)
    column = routing_column(route_weights, routed_experts)
    column_slots = slot_table(
        column[1].reshape(replicas, token_rows, top_count), expert_count, capacity
    )
    returned = lax.all_to_all(outcomes, "exp", split_axis=2, concat_axis=0, tiled=True)
    returned = returned.reshape(expert_count, replicas, capacity, model_width)
    expert_index = column_slots // capacity
    place_index = column_slots % capacity
    replica_index = jnp.broadcast_to(
        jnp.arange(replicas, dtype=jnp.int32)[:, None], column_slots.shape
    )
    picked = returned[expert_index, replica_index, place_index].astype(jnp.float32)
    column_weights = column[0].reshape(replicas, token_rows, top_count)
    weighted = jnp.sum(
        picked.reshape(replicas, token_rows, top_count, model_width)
        * column_weights[:, :, :, None],
        axis=2,
    )
    summed = lax.psum_scatter(weighted, "rep", scatter_dimension=0, tiled=True)
    return summed.reshape(token_rows, model_width).astype(jnp.bfloat16)


def fetch_kernel(turn, source_ref, result_ref):
    rows, width = source_ref.shape
    block = 512

    def fetch_block(step, carry):
        span = pl.ds(pl.multiple_of(step * block, block), block)
        if turn:
            for part in range(0, rows, 128):
                result_ref[span, part : part + 128] = source_ref[part : part + 128, span].T
        else:
            result_ref[:, span] = source_ref[:, span]
        return carry

    lax.fori_loop(0, width // block, fetch_block, 0)


def fetched(weight, turn):
    rows, width = weight.shape
    return pl.pallas_call(
        functools.partial(fetch_kernel, turn),
        out_shape=jax.ShapeDtypeStruct((width, rows) if turn else (rows, width), jnp.bfloat16),
        in_specs=[pl.BlockSpec(memory_space=pltpu.VMEM)],
        out_specs=pl.BlockSpec(memory_space=pltpu.VMEM),
        compiler_params=pltpu.CompilerParams(vmem_limit_bytes=4 * 1024 * 1024),
        cost_estimate=pl.CostEstimate(
            flops=0, bytes_accessed=4 * rows * width, transcendentals=0
        ),
        name="fetch_turned" if turn else "fetch",
    )(weight)


def gather_kernel(*refs):
    *pieces, whole_ref = refs
    start = 0
    for piece_ref in pieces:
        count = piece_ref.shape[0]
        whole_ref[start : start + count, :] = piece_ref[...]
        start += count


def gathered(*pieces):
    rows = sum(piece.shape[0] for piece in pieces)
    resident = pl.BlockSpec(memory_space=pltpu.VMEM)
    return pl.pallas_call(
        gather_kernel,
        out_shape=jax.ShapeDtypeStruct((rows, pieces[0].shape[1]), jnp.bfloat16),
        in_specs=[resident] * len(pieces),
        out_specs=resident,
        compiler_params=pltpu.CompilerParams(vmem_limit_bytes=2 * 1024 * 1024),
        name="gather",
    )(*pieces)


def expert_kernel(pieces_in, pieces_out, local_experts, shard_units, model_width, top, *refs):
    own_ref, refs = refs[0], refs[1:]
    ins, refs = refs[: len(pieces_in)], refs[len(pieces_in) :]
    (gate_ref, up_ref, down_ref), refs = refs[:3], refs[3:]
    outs, refs = refs[: len(pieces_out)], refs[len(pieces_out) :]
    rows, hidden = refs
    units = local_experts * shard_units
    unit_block = 256 if units % 256 == 0 else 128
    block = 512

    start = 0
    for place, count in enumerate(pieces_in):
        rows[start : start + count, :] = ins[place][...]
        start += count

    extra = rows[:, model_width:].astype(jnp.float32)
    width = extra.shape[1]
    scale = pltpu.roll(extra, width - top, 1) + pltpu.roll(extra, width - 2 * top, 1)
    lane = lax.broadcasted_iota(jnp.int32, extra.shape, 1)
    weights = []
    for expert in range(local_experts):
        name = (own_ref[0] + expert).astype(jnp.float32)
        chosen = jnp.logical_and(lane < top, extra == name)
        weights.append(jnp.sum(jnp.where(chosen, scale, 0.0), axis=1, keepdims=True))

    for begin in range(0, units, unit_block):
        span = slice(begin, begin + unit_block)
        values = rows[:, :model_width]
        gate = jnp.dot(values, gate_ref[:, span], preferred_element_type=jnp.float32)
        up = jnp.dot(values, up_ref[:, span], preferred_element_type=jnp.float32)
        unit = begin + lax.broadcasted_iota(jnp.int32, gate.shape, 1)
        weight = weights[begin // shard_units]
        for expert in range(begin // shard_units + 1, (begin + unit_block - 1) // shard_units + 1):
            weight = jnp.where(unit >= expert * shard_units, weights[expert], weight)
        active = gate / (1.0 + jnp.exp(-gate)) * up * weight
        hidden[:, span] = active.astype(jnp.bfloat16)

    for begin in range(0, model_width, block):
        span = slice(begin, begin + block)
        value = jnp.dot(hidden[...], down_ref[:, span], preferred_element_type=jnp.float32)
        value = value.astype(jnp.bfloat16)
        for place, segments in enumerate(pieces_out):
            filled = 0
            for first, count in segments:
                outs[place][filled : filled + count, span] = value[first : first + count]
                filled += count


def experts_of(own, pieces, pieces_out, gates, ups, downs, shard_units, top):
    units, model_width = downs.shape
    local_experts = units // shard_units
    pieces_in = [piece.shape[0] for piece in pieces]
    total = sum(pieces_in)
    packed = pieces[0].shape[1]
    resident = pl.BlockSpec(memory_space=pltpu.VMEM)
    kernel = functools.partial(
        expert_kernel, pieces_in, pieces_out, local_experts, shard_units, model_width, top
    )
    out_rows = [sum(count for _, count in segments) for segments in pieces_out]
    return pl.pallas_call(
        kernel,
        out_shape=[jax.ShapeDtypeStruct((count, model_width), jnp.bfloat16) for count in out_rows],
        in_specs=[pl.BlockSpec(memory_space=pltpu.SMEM)] + [resident] * (len(pieces) + 3),
        out_specs=[resident] * len(out_rows),
        scratch_shapes=[
            pltpu.VMEM((total, packed), jnp.bfloat16),
            pltpu.VMEM((total, units), jnp.bfloat16),
        ],
        compiler_params=pltpu.CompilerParams(vmem_limit_bytes=12 * 1024 * 1024),
        cost_estimate=pl.CostEstimate(
            flops=6 * total * units * model_width,
            bytes_accessed=4 * total * model_width,
            transcendentals=total * units,
        ),
        name="experts",
    )(own, *pieces, gates, ups, downs)


def pack_kernel(
    tokens_ref, experts_ref, weights_ref, packed_ref, experts, weights, sems
):
    model_width = tokens_ref.shape[1]
    copies = [
        pltpu.make_async_copy(experts_ref, experts, sems.at[0]),
        pltpu.make_async_copy(weights_ref, weights, sems.at[1]),
        pltpu.make_async_copy(tokens_ref, packed_ref.at[:, pl.ds(0, model_width)], sems.at[2]),
    ]
    for copy in copies:
        copy.start()
    copies[0].wait()
    copies[1].wait()
    values = weights[...]
    high = values.astype(jnp.bfloat16).astype(jnp.float32)
    listed = jnp.concatenate([experts[...].astype(jnp.float32), high, values - high], axis=0)
    width = packed_ref.shape[1] - model_width
    place = lax.broadcasted_iota(jnp.int32, (listed.shape[0], width), 0)
    lane = lax.broadcasted_iota(jnp.int32, (listed.shape[0], width), 1)
    chosen = jnp.where(place == lane, 1.0, 0.0).astype(jnp.bfloat16)
    extra = lax.dot_general(
        listed.astype(jnp.bfloat16),
        chosen,
        (((0,), (0,)), ((), ())),
        preferred_element_type=jnp.float32,
    )
    packed_ref[:, model_width:] = extra.astype(jnp.bfloat16)
    copies[2].wait()


def with_routing(tokens, routed_experts, route_weights):
    rows, width = tokens.shape
    top = routed_experts.shape[1]
    return pl.pallas_call(
        pack_kernel,
        out_shape=jax.ShapeDtypeStruct((rows, width + 128), jnp.bfloat16),
        in_specs=[pl.BlockSpec(memory_space=pl.ANY)] * 3,
        out_specs=pl.BlockSpec(memory_space=pltpu.VMEM),
        scratch_shapes=[
            pltpu.VMEM((top, rows), jnp.int32),
            pltpu.VMEM((top, rows), jnp.float32),
            pltpu.SemaphoreType.DMA((3,)),
        ],
        compiler_params=pltpu.CompilerParams(vmem_limit_bytes=2 * 1024 * 1024),
        name="pack",
    )(tokens, routed_experts.T, route_weights.T)


def begin_kernel(own_ref, gate_ref, up_ref, down_ref, index_ref):
    index_ref[0] = own_ref[0]


def begun(own, *weights):
    scalar = pl.BlockSpec(memory_space=pltpu.SMEM)
    return pl.pallas_call(
        begin_kernel,
        out_shape=jax.ShapeDtypeStruct((1,), jnp.int32),
        in_specs=[scalar] + [pl.BlockSpec(memory_space=pl.ANY)] * 3,
        out_specs=scalar,
        compiler_params=pltpu.CompilerParams(
            vmem_limit_bytes=50 * 1024 * 1024, has_side_effects=True
        ),
        name="begin",
    )(own, *weights)


def swap_exp(value, bits):
    owners = lax.axis_size("exp")
    return lax.ppermute(value, "exp", [(i, i ^ bits) for i in range(owners)])


def swap_rep(value, bits):
    replicas = lax.axis_size("rep")
    return lax.ppermute(value, "rep", [(i, i ^ bits) for i in range(replicas)])


def added(*terms):
    total = terms[0].astype(jnp.float32)
    for term in terms[1:]:
        total = total + term.astype(jnp.float32)
    return total


def rounded(*terms):
    return added(*terms).astype(jnp.bfloat16)


def ordered(*values):
    return lax.optimization_barrier(values)


def row_groups(places, rows):
    return [[(place * rows, rows) for place in group] for group in places]


def on_device_dense(tokens, routed_experts, route_weights, gate_weight, up_weight, down_weight):
    local_experts, shard_units, model_width = gate_weight.shape
    units = local_experts * shard_units
    top = routed_experts.shape[1]
    rows = tokens.shape[0]
    gate_weight = gate_weight.reshape(units, model_width)
    up_weight = up_weight.reshape(units, model_width)
    down_weight = down_weight.reshape(units, model_width)
    own = jnp.full((1,), lax.axis_index("exp") * local_experts, jnp.int32)
    begin = begun(own, gate_weight, up_weight, down_weight)
    tokens, own, begin = ordered(tokens, own, begin)
    packed = with_routing(tokens, routed_experts, route_weights)

    two = swap_rep(packed, 2)
    x_own, y_own, far_own = [swap_exp(packed, bits) for bits in (2, 4, 6)]
    gates, ups = fetched(gate_weight, True), fetched(up_weight, True)
    one = swap_rep(packed, 1)
    x_own, y_own, far_own, one, two, gates, ups = ordered(
        x_own, y_own, far_own, one, two, gates, ups
    )
    three = swap_rep(two, 1)
    x_two, y_two, far_two = [swap_exp(two, bits) for bits in (2, 4, 6)]
    first = gathered(packed, x_own, y_own, far_own)
    first_other = swap_exp(first, 1)
    second = gathered(two, x_two, y_two, far_two)
    downs = fetched(down_weight, False)
    second, downs, three = ordered(second, downs, three)
    pair = gathered(one, three)
    pair, far_own = ordered(pair, far_own)
    x_pair, y_pair = swap_exp(pair, 2), swap_exp(pair, 4)
    far_one, far_three = swap_rep(far_own, 1), swap_rep(far_two, 1)

    near = [first, second, first_other, swap_exp(second, 1)]
    groups = row_groups([[5, 1], [6, 2], [7], [13, 9, 14, 10, 15], [4, 0, 3], [12, 8, 11]], rows)
    parts = experts_of(own, near, groups, gates, ups, downs, shard_units, top)
    *parts, x_pair, y_pair, far_one, far_three = ordered(
        *parts, x_pair, y_pair, far_one, far_three
    )
    to_x, to_y, to_far, other, near_kept, near_other = parts
    back = swap_exp(other, 1)
    to_x = rounded(to_x, back[: 2 * rows])
    to_y = rounded(to_y, back[2 * rows : 4 * rows])
    to_far = rounded(to_far, back[4 * rows :])
    to_x, to_y, to_far, near_other = ordered(to_x, to_y, to_far, near_other)
    near_x, near_y, near_far = swap_exp(to_x, 2), swap_exp(to_y, 4), swap_rep(to_far, 2)
    near_back = swap_exp(near_other, 1)

    far = [pair, x_pair, y_pair, far_one, far_three]
    far = far + [swap_exp(piece, 1) for piece in far]
    to_x, to_y, to_far, *far = ordered(to_x, to_y, to_far, *far)
    groups = row_groups([[6], [7], [2, 3], [4, 5], [10, 11, 12, 13, 8, 9], [14, 15], [0, 1]], rows)
    parts = experts_of(own, far, groups, gates, ups, downs, shard_units, top)
    to_one, to_three, to_x, to_y, other, other_far, far_kept = parts
    far_kept, near_far, near_y, near_x = ordered(far_kept, near_far, near_y, near_x)
    back = swap_exp(other, 1)
    kept = added(near_kept, near_back)
    to_two = rounded(kept[:rows], near_x[:rows], near_y[:rows])
    back, to_two = ordered(back, to_two)
    from_two = swap_rep(to_two, 2)
    to_x, to_y = rounded(to_x, back[: 2 * rows]), rounded(to_y, back[2 * rows : 4 * rows])
    to_x, to_y, other_far = ordered(to_x, to_y, other_far)
    far_x, far_y = swap_exp(to_x, 2), swap_exp(to_y, 4)
    back_far = swap_exp(other_far, 1)
    to_one, to_three = rounded(to_one, back_far[:rows]), rounded(to_three, back_far[rows:])
    from_three, from_one = swap_rep(to_three, 3), swap_rep(to_one, 1)

    own_sum = kept[rows : 2 * rows] + added(near_x[rows:], near_y[rows:])
    from_one, from_three, from_two = ordered(from_one, from_three, from_two)
    to_far = rounded(kept[2 * rows :], from_one, from_three, near_far)
    from_far = swap_exp(to_far, 6)
    to_one = rounded(far_kept[:rows], back[4 * rows : 5 * rows], far_x[:rows], far_y[:rows])
    to_three = rounded(far_kept[rows:], back[5 * rows :], far_x[rows:], far_y[rows:])
    arrived = [swap_rep(to_one, 1), swap_rep(to_three, 3)]
    return rounded(own_sum, from_two, from_far, *arrived)


def solution(mesh):
    placed = (
        P(("rep", "exp"), None),
        P(("rep", "exp"), None),
        P(("rep", "exp"), None),
        P("exp", "rep", None),
        P("exp", "rep", None),
        P("exp", "rep", None),
    )
    plane = mesh.shape["exp"] == 8 and mesh.shape["rep"] == 4
    return jax.shard_map(
        on_device_dense if plane else on_device_slots,
        mesh=mesh,
        in_specs=placed,
        out_specs=P(("rep", "exp"), None),
        check_vma=False,
    )
```

```python
import functools

import jax
import jax.numpy as jnp
from jax import lax
from jax.experimental import pallas as pl
from jax.experimental.pallas import tpu as pltpu
from jax.sharding import PartitionSpec as P


def slot_table(experts, expert_count, capacity):
    blocks = experts.shape[0]
    flattened = experts.reshape(blocks, -1)
    onehot = (
        flattened[:, :, None] == jnp.arange(expert_count, dtype=jnp.int32)[None, None, :]
    ).astype(jnp.int32)
    before = jnp.cumsum(onehot, axis=1) - onehot
    position = jnp.sum(before * onehot, axis=2)
    return flattened * capacity + position


def token_picks(slots, top_count, slot_count):
    blocks = slots.shape[0]
    grouped = slots.reshape(blocks, 1, -1, top_count)
    return jnp.any(grouped == jnp.arange(slot_count, dtype=jnp.int32)[None, :, None, None], axis=3)


def routing_column(route_weights, routed_experts):
    as_float = routed_experts.astype(jnp.float32)
    weights_all, experts_all = (
        lax.all_gather(route_weights, "rep", axis=0, tiled=True),
        lax.all_gather(as_float, "rep", axis=0, tiled=True),
    )
    return (weights_all, experts_all.astype(jnp.int32))


def on_device_slots(tokens, routed_experts, route_weights, gate_weight, up_weight, down_weight):
    replicas = lax.axis_size("rep")
    owners = lax.axis_size("exp")
    token_rows, model_width = tokens.shape
    top_count = routed_experts.shape[1]
    local_experts = gate_weight.shape[0]
    expert_count = local_experts * owners
    capacity = max(2, 3 * token_rows * top_count // (2 * expert_count))
    slot_count = expert_count * capacity
    own_slots = slot_table(routed_experts[None], expert_count, capacity)
    column = None
    column_slots = None
    selected = token_picks(own_slots, top_count, slot_count)[0].astype(jnp.bfloat16)
    buffer = jnp.dot(selected, tokens, preferred_element_type=jnp.float32).astype(jnp.bfloat16)
    buffer = buffer.reshape(owners, local_experts, capacity, model_width)
    arrived = lax.all_to_all(buffer, "exp", split_axis=0, concat_axis=2, tiled=True)
    rows_now = lax.all_gather(arrived, "rep", axis=2, tiled=True)[0]
    gate_value = jnp.einsum(
        "emd,efd->emf", rows_now, gate_weight, preferred_element_type=jnp.float32
    )
    up_value = jnp.einsum("emd,efd->emf", rows_now, up_weight, preferred_element_type=jnp.float32)
    hidden = (jax.nn.silu(gate_value) * up_value).astype(jnp.bfloat16)
    outcome = jnp.einsum("emf,efd->emd", hidden, down_weight, preferred_element_type=jnp.float32)
    outcome = lax.optimization_barrier(outcome.astype(jnp.bfloat16))
    outcomes = outcome[None]
    outcomes = outcomes.reshape(local_experts, replicas, owners, capacity, model_width)
    column = routing_column(route_weights, routed_experts)
    column_slots = slot_table(
        column[1].reshape(replicas, token_rows, top_count), expert_count, capacity
    )
    returned = lax.all_to_all(outcomes, "exp", split_axis=2, concat_axis=0, tiled=True)
    returned = returned.reshape(expert_count, replicas, capacity, model_width)
    expert_index = column_slots // capacity
    place_index = column_slots % capacity
    replica_index = jnp.broadcast_to(
        jnp.arange(replicas, dtype=jnp.int32)[:, None], column_slots.shape
    )
    picked = returned[expert_index, replica_index, place_index].astype(jnp.float32)
    column_weights = column[0].reshape(replicas, token_rows, top_count)
    weighted = jnp.sum(
        picked.reshape(replicas, token_rows, top_count, model_width)
        * column_weights[:, :, :, None],
        axis=2,
    )
    summed = lax.psum_scatter(weighted, "rep", scatter_dimension=0, tiled=True)
    return summed.reshape(token_rows, model_width).astype(jnp.bfloat16)


def fetch_kernel(turn, source_ref, result_ref):
    rows, width = source_ref.shape
    block = 512

    def fetch_block(step, carry):
        span = pl.ds(pl.multiple_of(step * block, block), block)
        if turn:
            for part in range(0, rows, 128):
                result_ref[span, part : part + 128] = source_ref[part : part + 128, span].T
        else:
            result_ref[:, span] = source_ref[:, span]
        return carry

    lax.fori_loop(0, width // block, fetch_block, 0)


def fetched(weight, turn):
    rows, width = weight.shape
    return pl.pallas_call(
        functools.partial(fetch_kernel, turn),
        out_shape=jax.ShapeDtypeStruct((width, rows) if turn else (rows, width), jnp.bfloat16),
        in_specs=[pl.BlockSpec(memory_space=pltpu.VMEM)],
        out_specs=pl.BlockSpec(memory_space=pltpu.VMEM),
        compiler_params=pltpu.CompilerParams(vmem_limit_bytes=4 * 1024 * 1024),
        cost_estimate=pl.CostEstimate(
            flops=0, bytes_accessed=4 * rows * width, transcendentals=0
        ),
        name="fetch_turned" if turn else "fetch",
    )(weight)


def gather_kernel(*refs):
    *pieces, whole_ref = refs
    start = 0
    for piece_ref in pieces:
        count = piece_ref.shape[0]
        whole_ref[start : start + count, :] = piece_ref[...]
        start += count


def gathered(*pieces):
    rows = sum(piece.shape[0] for piece in pieces)
    resident = pl.BlockSpec(memory_space=pltpu.VMEM)
    return pl.pallas_call(
        gather_kernel,
        out_shape=jax.ShapeDtypeStruct((rows, pieces[0].shape[1]), jnp.bfloat16),
        in_specs=[resident] * len(pieces),
        out_specs=resident,
        compiler_params=pltpu.CompilerParams(vmem_limit_bytes=2 * 1024 * 1024),
        name="gather",
    )(*pieces)


def expert_kernel(pieces_in, pieces_out, local_experts, shard_units, model_width, top, *refs):
    own_ref, refs = refs[0], refs[1:]
    ins, refs = refs[: len(pieces_in)], refs[len(pieces_in) :]
    (gate_ref, up_ref, down_ref), refs = refs[:3], refs[3:]
    outs, refs = refs[: len(pieces_out)], refs[len(pieces_out) :]
    rows, hidden = refs
    units = local_experts * shard_units
    unit_block = 256 if units % 256 == 0 else 128
    block = 512

    start = 0
    for place, count in enumerate(pieces_in):
        rows[start : start + count, :] = ins[place][...]
        start += count

    extra = rows[:, model_width:].astype(jnp.float32)
    width = extra.shape[1]
    scale = pltpu.roll(extra, width - top, 1) + pltpu.roll(extra, width - 2 * top, 1)
    lane = lax.broadcasted_iota(jnp.int32, extra.shape, 1)
    weights = []
    for expert in range(local_experts):
        name = (own_ref[0] + expert).astype(jnp.float32)
        chosen = jnp.logical_and(lane < top, extra == name)
        weights.append(jnp.sum(jnp.where(chosen, scale, 0.0), axis=1, keepdims=True))

    for begin in range(0, units, unit_block):
        span = slice(begin, begin + unit_block)
        values = rows[:, :model_width]
        gate = jnp.dot(values, gate_ref[:, span], preferred_element_type=jnp.float32)
        up = jnp.dot(values, up_ref[:, span], preferred_element_type=jnp.float32)
        unit = begin + lax.broadcasted_iota(jnp.int32, gate.shape, 1)
        weight = weights[begin // shard_units]
        for expert in range(begin // shard_units + 1, (begin + unit_block - 1) // shard_units + 1):
            weight = jnp.where(unit >= expert * shard_units, weights[expert], weight)
        active = gate / (1.0 + jnp.exp(-gate)) * up * weight
        hidden[:, span] = active.astype(jnp.bfloat16)

    for begin in range(0, model_width, block):
        span = slice(begin, begin + block)
        value = jnp.dot(hidden[...], down_ref[:, span], preferred_element_type=jnp.float32)
        value = value.astype(jnp.bfloat16)
        for place, segments in enumerate(pieces_out):
            filled = 0
            for first, count in segments:
                outs[place][filled : filled + count, span] = value[first : first + count]
                filled += count


def experts_of(own, pieces, pieces_out, gates, ups, downs, shard_units, top):
    units, model_width = downs.shape
    local_experts = units // shard_units
    pieces_in = [piece.shape[0] for piece in pieces]
    total = sum(pieces_in)
    packed = pieces[0].shape[1]
    resident = pl.BlockSpec(memory_space=pltpu.VMEM)
    kernel = functools.partial(
        expert_kernel, pieces_in, pieces_out, local_experts, shard_units, model_width, top
    )
    out_rows = [sum(count for _, count in segments) for segments in pieces_out]
    return pl.pallas_call(
        kernel,
        out_shape=[jax.ShapeDtypeStruct((count, model_width), jnp.bfloat16) for count in out_rows],
        in_specs=[pl.BlockSpec(memory_space=pltpu.SMEM)] + [resident] * (len(pieces) + 3),
        out_specs=[resident] * len(out_rows),
        scratch_shapes=[
            pltpu.VMEM((total, packed), jnp.bfloat16),
            pltpu.VMEM((total, units), jnp.bfloat16),
        ],
        compiler_params=pltpu.CompilerParams(vmem_limit_bytes=12 * 1024 * 1024),
        cost_estimate=pl.CostEstimate(
            flops=6 * total * units * model_width,
            bytes_accessed=4 * total * model_width,
            transcendentals=total * units,
        ),
        name="experts",
    )(own, *pieces, gates, ups, downs)


def pack_kernel(
    tokens_ref, experts_ref, weights_ref, packed_ref, experts, weights, sems
):
    model_width = tokens_ref.shape[1]
    copies = [
        pltpu.make_async_copy(experts_ref, experts, sems.at[0]),
        pltpu.make_async_copy(weights_ref, weights, sems.at[1]),
        pltpu.make_async_copy(tokens_ref, packed_ref.at[:, pl.ds(0, model_width)], sems.at[2]),
    ]
    for copy in copies:
        copy.start()
    copies[0].wait()
    copies[1].wait()
    values = weights[...]
    high = values.astype(jnp.bfloat16).astype(jnp.float32)
    listed = jnp.concatenate([experts[...].astype(jnp.float32), high, values - high], axis=0)
    width = packed_ref.shape[1] - model_width
    place = lax.broadcasted_iota(jnp.int32, (listed.shape[0], width), 0)
    lane = lax.broadcasted_iota(jnp.int32, (listed.shape[0], width), 1)
    chosen = jnp.where(place == lane, 1.0, 0.0).astype(jnp.bfloat16)
    extra = lax.dot_general(
        listed.astype(jnp.bfloat16),
        chosen,
        (((0,), (0,)), ((), ())),
        preferred_element_type=jnp.float32,
    )
    packed_ref[:, model_width:] = extra.astype(jnp.bfloat16)
    copies[2].wait()


def with_routing(tokens, routed_experts, route_weights):
    rows, width = tokens.shape
    top = routed_experts.shape[1]
    return pl.pallas_call(
        pack_kernel,
        out_shape=jax.ShapeDtypeStruct((rows, width + 128), jnp.bfloat16),
        in_specs=[pl.BlockSpec(memory_space=pl.ANY)] * 3,
        out_specs=pl.BlockSpec(memory_space=pltpu.VMEM),
        scratch_shapes=[
            pltpu.VMEM((top, rows), jnp.int32),
            pltpu.VMEM((top, rows), jnp.float32),
            pltpu.SemaphoreType.DMA((3,)),
        ],
        compiler_params=pltpu.CompilerParams(vmem_limit_bytes=2 * 1024 * 1024),
        name="pack",
    )(tokens, routed_experts.T, route_weights.T)


def begin_kernel(own_ref, gate_ref, up_ref, down_ref, index_ref):
    index_ref[0] = own_ref[0]


def begun(own, *weights):
    scalar = pl.BlockSpec(memory_space=pltpu.SMEM)
    return pl.pallas_call(
        begin_kernel,
        out_shape=jax.ShapeDtypeStruct((1,), jnp.int32),
        in_specs=[scalar] + [pl.BlockSpec(memory_space=pl.ANY)] * 3,
        out_specs=scalar,
        compiler_params=pltpu.CompilerParams(
            vmem_limit_bytes=50 * 1024 * 1024, has_side_effects=True
        ),
        name="begin",
    )(own, *weights)


def swap_exp(value, bits):
    owners = lax.axis_size("exp")
    return lax.ppermute(value, "exp", [(i, i ^ bits) for i in range(owners)])


def swap_rep(value, bits):
    replicas = lax.axis_size("rep")
    return lax.ppermute(value, "rep", [(i, i ^ bits) for i in range(replicas)])


def added(*terms):
    total = terms[0].astype(jnp.float32)
    for term in terms[1:]:
        total = total + term.astype(jnp.float32)
    return total


def rounded(*terms):
    return added(*terms).astype(jnp.bfloat16)


def ordered(*values):
    return lax.optimization_barrier(values)


def row_groups(places, rows):
    return [[(place * rows, rows) for place in group] for group in places]


def on_device_dense(tokens, routed_experts, route_weights, gate_weight, up_weight, down_weight):
    local_experts, shard_units, model_width = gate_weight.shape
    units = local_experts * shard_units
    top = routed_experts.shape[1]
    rows = tokens.shape[0]
    gate_weight = gate_weight.reshape(units, model_width)
    up_weight = up_weight.reshape(units, model_width)
    down_weight = down_weight.reshape(units, model_width)
    own = jnp.full((1,), lax.axis_index("exp") * local_experts, jnp.int32)
    begin = begun(own, gate_weight, up_weight, down_weight)
    tokens, own, begin = ordered(tokens, own, begin)
    packed = with_routing(tokens, routed_experts, route_weights)

    two = swap_rep(packed, 2)
    x_own, y_own, far_own = [swap_exp(packed, bits) for bits in (2, 4, 6)]
    gates, ups = fetched(gate_weight, True), fetched(up_weight, True)
    one = swap_rep(packed, 1)
    two, one, far_own, y_own, x_own, gates, ups = ordered(
        two, one, far_own, y_own, x_own, gates, ups
    )
    three = swap_rep(two, 1)
    x_two, y_two, far_two = [swap_exp(two, bits) for bits in (2, 4, 6)]
    first = gathered(packed, x_own, y_own, far_own)
    first_other = swap_exp(first, 1)
    second = gathered(two, x_two, y_two, far_two)
    downs = fetched(down_weight, False)
    far_one = swap_rep(far_own, 1)
    second, downs, three, far_one = ordered(second, downs, three, far_one)
    pair = gathered(one, three)
    x_pair, y_pair = swap_exp(pair, 2), swap_exp(pair, 4)
    far_three = swap_rep(far_two, 1)

    near = [first, second, first_other, swap_exp(second, 1)]
    groups = row_groups([[5, 1], [6, 2], [7], [13, 9, 14, 10, 15], [4, 0, 3], [12, 8, 11]], rows)
    parts = experts_of(own, near, groups, gates, ups, downs, shard_units, top)
    *parts, x_pair, y_pair, far_three = ordered(*parts, x_pair, y_pair, far_three)
    to_x, to_y, to_far, other, near_kept, near_other = parts
    back = swap_exp(other, 1)
    to_x = rounded(to_x, back[: 2 * rows])
    to_y = rounded(to_y, back[2 * rows : 4 * rows])
    to_far = rounded(to_far, back[4 * rows :])
    to_x, to_y, to_far, near_other = ordered(to_x, to_y, to_far, near_other)
    near_x, near_y, near_far = swap_exp(to_x, 2), swap_exp(to_y, 4), swap_rep(to_far, 2)
    near_back = swap_exp(near_other, 1)

    far = [pair, x_pair, y_pair, far_one, far_three]
    far = far + [swap_exp(piece, 1) for piece in far]
    to_x, to_y, to_far, *far = ordered(to_x, to_y, to_far, *far)
    groups = row_groups([[6], [7], [2, 3], [4, 5], [10, 11, 12, 13, 8, 9], [14, 15], [0, 1]], rows)
    parts = experts_of(own, far, groups, gates, ups, downs, shard_units, top)
    to_one, to_three, to_x, to_y, other, other_far, far_kept = parts
    far_kept, near_far, near_y, near_x = ordered(far_kept, near_far, near_y, near_x)
    back = swap_exp(other, 1)
    kept = added(near_kept, near_back)
    to_two = rounded(kept[:rows], near_x[:rows], near_y[:rows])
    back, to_two = ordered(back, to_two)
    from_two = swap_rep(to_two, 2)
    to_x, to_y = rounded(to_x, back[: 2 * rows]), rounded(to_y, back[2 * rows : 4 * rows])
    to_x, to_y, other_far = ordered(to_x, to_y, other_far)
    far_x, far_y = swap_exp(to_x, 2), swap_exp(to_y, 4)
    back_far = swap_exp(other_far, 1)
    to_one, to_three = rounded(to_one, back_far[:rows]), rounded(to_three, back_far[rows:])
    from_three, from_one = swap_rep(to_three, 3), swap_rep(to_one, 1)

    own_sum = kept[rows : 2 * rows] + added(near_x[rows:], near_y[rows:])
    from_two, from_three, from_one = ordered(from_two, from_three, from_one)
    to_far = rounded(kept[2 * rows :], from_one, from_three, near_far)
    from_far = swap_exp(to_far, 6)
    to_one = rounded(far_kept[:rows], back[4 * rows : 5 * rows], far_x[:rows], far_y[:rows])
    to_three = rounded(far_kept[rows:], back[5 * rows :], far_x[rows:], far_y[rows:])
    arrived = [swap_rep(to_one, 1), swap_rep(to_three, 3)]
    return rounded(own_sum, from_two, from_far, *arrived)


def solution(mesh):
    placed = (
        P(("rep", "exp"), None),
        P(("rep", "exp"), None),
        P(("rep", "exp"), None),
        P("exp", "rep", None),
        P("exp", "rep", None),
        P("exp", "rep", None),
    )
    plane = mesh.shape["exp"] == 8 and mesh.shape["rep"] == 4
    return jax.shard_map(
        on_device_dense if plane else on_device_slots,
        mesh=mesh,
        in_specs=placed,
        out_specs=P(("rep", "exp"), None),
        check_vma=False,
    )
```

```python
import functools

import jax
import jax.numpy as jnp
from jax import lax
from jax.experimental import pallas as pl
from jax.experimental.pallas import tpu as pltpu
from jax.sharding import PartitionSpec as P


def slot_table(experts, expert_count, capacity):
    blocks = experts.shape[0]
    flattened = experts.reshape(blocks, -1)
    onehot = (
        flattened[:, :, None] == jnp.arange(expert_count, dtype=jnp.int32)[None, None, :]
    ).astype(jnp.int32)
    before = jnp.cumsum(onehot, axis=1) - onehot
    position = jnp.sum(before * onehot, axis=2)
    return flattened * capacity + position


def token_picks(slots, top_count, slot_count):
    blocks = slots.shape[0]
    grouped = slots.reshape(blocks, 1, -1, top_count)
    return jnp.any(grouped == jnp.arange(slot_count, dtype=jnp.int32)[None, :, None, None], axis=3)


def routing_column(route_weights, routed_experts):
    as_float = routed_experts.astype(jnp.float32)
    weights_all, experts_all = (
        lax.all_gather(route_weights, "rep", axis=0, tiled=True),
        lax.all_gather(as_float, "rep", axis=0, tiled=True),
    )
    return (weights_all, experts_all.astype(jnp.int32))


def on_device_slots(tokens, routed_experts, route_weights, gate_weight, up_weight, down_weight):
    replicas = lax.axis_size("rep")
    owners = lax.axis_size("exp")
    token_rows, model_width = tokens.shape
    top_count = routed_experts.shape[1]
    local_experts = gate_weight.shape[0]
    expert_count = local_experts * owners
    capacity = max(2, 3 * token_rows * top_count // (2 * expert_count))
    slot_count = expert_count * capacity
    own_slots = slot_table(routed_experts[None], expert_count, capacity)
    column = None
    column_slots = None
    selected = token_picks(own_slots, top_count, slot_count)[0].astype(jnp.bfloat16)
    buffer = jnp.dot(selected, tokens, preferred_element_type=jnp.float32).astype(jnp.bfloat16)
    buffer = buffer.reshape(owners, local_experts, capacity, model_width)
    arrived = lax.all_to_all(buffer, "exp", split_axis=0, concat_axis=2, tiled=True)
    rows_now = lax.all_gather(arrived, "rep", axis=2, tiled=True)[0]
    gate_value = jnp.einsum(
        "emd,efd->emf", rows_now, gate_weight, preferred_element_type=jnp.float32
    )
    up_value = jnp.einsum("emd,efd->emf", rows_now, up_weight, preferred_element_type=jnp.float32)
    hidden = (jax.nn.silu(gate_value) * up_value).astype(jnp.bfloat16)
    outcome = jnp.einsum("emf,efd->emd", hidden, down_weight, preferred_element_type=jnp.float32)
    outcome = lax.optimization_barrier(outcome.astype(jnp.bfloat16))
    outcomes = outcome[None]
    outcomes = outcomes.reshape(local_experts, replicas, owners, capacity, model_width)
    column = routing_column(route_weights, routed_experts)
    column_slots = slot_table(
        column[1].reshape(replicas, token_rows, top_count), expert_count, capacity
    )
    returned = lax.all_to_all(outcomes, "exp", split_axis=2, concat_axis=0, tiled=True)
    returned = returned.reshape(expert_count, replicas, capacity, model_width)
    expert_index = column_slots // capacity
    place_index = column_slots % capacity
    replica_index = jnp.broadcast_to(
        jnp.arange(replicas, dtype=jnp.int32)[:, None], column_slots.shape
    )
    picked = returned[expert_index, replica_index, place_index].astype(jnp.float32)
    column_weights = column[0].reshape(replicas, token_rows, top_count)
    weighted = jnp.sum(
        picked.reshape(replicas, token_rows, top_count, model_width)
        * column_weights[:, :, :, None],
        axis=2,
    )
    summed = lax.psum_scatter(weighted, "rep", scatter_dimension=0, tiled=True)
    return summed.reshape(token_rows, model_width).astype(jnp.bfloat16)


def fetch_kernel(turn, source_ref, result_ref):
    rows, width = source_ref.shape
    block = 512

    def fetch_block(step, carry):
        span = pl.ds(pl.multiple_of(step * block, block), block)
        if turn:
            for part in range(0, rows, 128):
                result_ref[span, part : part + 128] = source_ref[part : part + 128, span].T
        else:
            result_ref[:, span] = source_ref[:, span]
        return carry

    lax.fori_loop(0, width // block, fetch_block, 0)


def fetched(weight, turn):
    rows, width = weight.shape
    return pl.pallas_call(
        functools.partial(fetch_kernel, turn),
        out_shape=jax.ShapeDtypeStruct((width, rows) if turn else (rows, width), jnp.bfloat16),
        in_specs=[pl.BlockSpec(memory_space=pltpu.VMEM)],
        out_specs=pl.BlockSpec(memory_space=pltpu.VMEM),
        compiler_params=pltpu.CompilerParams(vmem_limit_bytes=4 * 1024 * 1024),
        cost_estimate=pl.CostEstimate(
            flops=0, bytes_accessed=4 * rows * width, transcendentals=0
        ),
        name="fetch_turned" if turn else "fetch",
    )(weight)


def gather_kernel(*refs):
    *pieces, whole_ref = refs
    start = 0
    for piece_ref in pieces:
        count = piece_ref.shape[0]
        whole_ref[start : start + count, :] = piece_ref[...]
        start += count


def gathered(*pieces):
    rows = sum(piece.shape[0] for piece in pieces)
    resident = pl.BlockSpec(memory_space=pltpu.VMEM)
    return pl.pallas_call(
        gather_kernel,
        out_shape=jax.ShapeDtypeStruct((rows, pieces[0].shape[1]), jnp.bfloat16),
        in_specs=[resident] * len(pieces),
        out_specs=resident,
        compiler_params=pltpu.CompilerParams(vmem_limit_bytes=2 * 1024 * 1024),
        name="gather",
    )(*pieces)


def expert_kernel(pieces_in, pieces_out, local_experts, shard_units, model_width, top, *refs):
    own_ref, refs = refs[0], refs[1:]
    ins, refs = refs[: len(pieces_in)], refs[len(pieces_in) :]
    (gate_ref, up_ref, down_ref), refs = refs[:3], refs[3:]
    outs, refs = refs[: len(pieces_out)], refs[len(pieces_out) :]
    rows, hidden = refs
    units = local_experts * shard_units
    unit_block = 256 if units % 256 == 0 else 128
    block = 512

    start = 0
    for place, count in enumerate(pieces_in):
        rows[start : start + count, :] = ins[place][...]
        start += count

    extra = rows[:, model_width:].astype(jnp.float32)
    width = extra.shape[1]
    scale = pltpu.roll(extra, width - top, 1) + pltpu.roll(extra, width - 2 * top, 1)
    lane = lax.broadcasted_iota(jnp.int32, extra.shape, 1)
    weights = []
    for expert in range(local_experts):
        name = (own_ref[0] + expert).astype(jnp.float32)
        chosen = jnp.logical_and(lane < top, extra == name)
        weights.append(jnp.sum(jnp.where(chosen, scale, 0.0), axis=1, keepdims=True))

    for begin in range(0, units, unit_block):
        span = slice(begin, begin + unit_block)
        values = rows[:, :model_width]
        gate = jnp.dot(values, gate_ref[:, span], preferred_element_type=jnp.float32)
        up = jnp.dot(values, up_ref[:, span], preferred_element_type=jnp.float32)
        unit = begin + lax.broadcasted_iota(jnp.int32, gate.shape, 1)
        weight = weights[begin // shard_units]
        for expert in range(begin // shard_units + 1, (begin + unit_block - 1) // shard_units + 1):
            weight = jnp.where(unit >= expert * shard_units, weights[expert], weight)
        active = gate / (1.0 + jnp.exp(-gate)) * up * weight
        hidden[:, span] = active.astype(jnp.bfloat16)

    for begin in range(0, model_width, block):
        span = slice(begin, begin + block)
        value = jnp.dot(hidden[...], down_ref[:, span], preferred_element_type=jnp.float32)
        value = value.astype(jnp.bfloat16)
        for place, segments in enumerate(pieces_out):
            filled = 0
            for first, count in segments:
                outs[place][filled : filled + count, span] = value[first : first + count]
                filled += count


def experts_of(own, pieces, pieces_out, gates, ups, downs, shard_units, top):
    units, model_width = downs.shape
    local_experts = units // shard_units
    pieces_in = [piece.shape[0] for piece in pieces]
    total = sum(pieces_in)
    packed = pieces[0].shape[1]
    resident = pl.BlockSpec(memory_space=pltpu.VMEM)
    kernel = functools.partial(
        expert_kernel, pieces_in, pieces_out, local_experts, shard_units, model_width, top
    )
    out_rows = [sum(count for _, count in segments) for segments in pieces_out]
    return pl.pallas_call(
        kernel,
        out_shape=[jax.ShapeDtypeStruct((count, model_width), jnp.bfloat16) for count in out_rows],
        in_specs=[pl.BlockSpec(memory_space=pltpu.SMEM)] + [resident] * (len(pieces) + 3),
        out_specs=[resident] * len(out_rows),
        scratch_shapes=[
            pltpu.VMEM((total, packed), jnp.bfloat16),
            pltpu.VMEM((total, units), jnp.bfloat16),
        ],
        compiler_params=pltpu.CompilerParams(vmem_limit_bytes=12 * 1024 * 1024),
        cost_estimate=pl.CostEstimate(
            flops=6 * total * units * model_width,
            bytes_accessed=4 * total * model_width,
            transcendentals=total * units,
        ),
        name="experts",
    )(own, *pieces, gates, ups, downs)


def pack_kernel(
    tokens_ref, experts_ref, weights_ref, packed_ref, experts, weights, sems
):
    model_width = tokens_ref.shape[1]
    copies = [
        pltpu.make_async_copy(experts_ref, experts, sems.at[0]),
        pltpu.make_async_copy(weights_ref, weights, sems.at[1]),
        pltpu.make_async_copy(tokens_ref, packed_ref.at[:, pl.ds(0, model_width)], sems.at[2]),
    ]
    for copy in copies:
        copy.start()
    copies[0].wait()
    copies[1].wait()
    values = weights[...]
    high = values.astype(jnp.bfloat16).astype(jnp.float32)
    listed = jnp.concatenate([experts[...].astype(jnp.float32), high, values - high], axis=0)
    width = packed_ref.shape[1] - model_width
    place = lax.broadcasted_iota(jnp.int32, (listed.shape[0], width), 0)
    lane = lax.broadcasted_iota(jnp.int32, (listed.shape[0], width), 1)
    chosen = jnp.where(place == lane, 1.0, 0.0).astype(jnp.bfloat16)
    extra = lax.dot_general(
        listed.astype(jnp.bfloat16),
        chosen,
        (((0,), (0,)), ((), ())),
        preferred_element_type=jnp.float32,
    )
    packed_ref[:, model_width:] = extra.astype(jnp.bfloat16)
    copies[2].wait()


def with_routing(tokens, routed_experts, route_weights):
    rows, width = tokens.shape
    top = routed_experts.shape[1]
    return pl.pallas_call(
        pack_kernel,
        out_shape=jax.ShapeDtypeStruct((rows, width + 128), jnp.bfloat16),
        in_specs=[pl.BlockSpec(memory_space=pl.ANY)] * 3,
        out_specs=pl.BlockSpec(memory_space=pltpu.VMEM),
        scratch_shapes=[
            pltpu.VMEM((top, rows), jnp.int32),
            pltpu.VMEM((top, rows), jnp.float32),
            pltpu.SemaphoreType.DMA((3,)),
        ],
        compiler_params=pltpu.CompilerParams(vmem_limit_bytes=2 * 1024 * 1024),
        name="pack",
    )(tokens, routed_experts.T, route_weights.T)


def begin_kernel(own_ref, gate_ref, up_ref, down_ref, index_ref):
    index_ref[0] = own_ref[0]


def begun(own, *weights):
    scalar = pl.BlockSpec(memory_space=pltpu.SMEM)
    return pl.pallas_call(
        begin_kernel,
        out_shape=jax.ShapeDtypeStruct((1,), jnp.int32),
        in_specs=[scalar] + [pl.BlockSpec(memory_space=pl.ANY)] * 3,
        out_specs=scalar,
        compiler_params=pltpu.CompilerParams(
            vmem_limit_bytes=50 * 1024 * 1024, has_side_effects=True
        ),
        name="begin",
    )(own, *weights)


def swap_exp(value, bits):
    owners = lax.axis_size("exp")
    return lax.ppermute(value, "exp", [(i, i ^ bits) for i in range(owners)])


def swap_rep(value, bits):
    replicas = lax.axis_size("rep")
    return lax.ppermute(value, "rep", [(i, i ^ bits) for i in range(replicas)])


def added(*terms):
    total = terms[0].astype(jnp.float32)
    for term in terms[1:]:
        total = total + term.astype(jnp.float32)
    return total


def rounded(*terms):
    return added(*terms).astype(jnp.bfloat16)


def ordered(*values):
    return lax.optimization_barrier(values)


def row_groups(places, rows):
    return [[(place * rows, rows) for place in group] for group in places]


def on_device_dense(tokens, routed_experts, route_weights, gate_weight, up_weight, down_weight):
    local_experts, shard_units, model_width = gate_weight.shape
    units = local_experts * shard_units
    top = routed_experts.shape[1]
    rows = tokens.shape[0]
    gate_weight = gate_weight.reshape(units, model_width)
    up_weight = up_weight.reshape(units, model_width)
    down_weight = down_weight.reshape(units, model_width)
    own = jnp.full((1,), lax.axis_index("exp") * local_experts, jnp.int32)
    begin = begun(own, gate_weight, up_weight, down_weight)
    tokens, own, begin = ordered(tokens, own, begin)
    packed = with_routing(tokens, routed_experts, route_weights)

    two = swap_rep(packed, 2)
    x_own, y_own, far_own = [swap_exp(packed, bits) for bits in (2, 4, 6)]
    gates, ups = fetched(gate_weight, True), fetched(up_weight, True)
    one = swap_rep(packed, 1)
    x_own, y_own, far_own, one, two, gates, ups = ordered(
        x_own, y_own, far_own, one, two, gates, ups
    )
    three = swap_rep(two, 1)
    x_two, y_two, far_two = [swap_exp(two, bits) for bits in (2, 4, 6)]
    first = gathered(packed, x_own, y_own, far_own)
    first_other = swap_exp(first, 1)
    second = gathered(two, x_two, y_two, far_two)
    downs = fetched(down_weight, False)
    second, downs, three = ordered(second, downs, three)
    pair = gathered(one, three)
    pair, far_own = ordered(pair, far_own)
    x_pair, y_pair = swap_exp(pair, 2), swap_exp(pair, 4)
    far_one, far_three = swap_rep(far_own, 1), swap_rep(far_two, 1)

    near = [first, second, first_other, swap_exp(second, 1)]
    groups = row_groups([[5, 1], [6, 2], [7], [13, 9, 14, 10, 15], [4, 0, 3], [12, 8, 11]], rows)
    parts = experts_of(own, near, groups, gates, ups, downs, shard_units, top)
    *parts, x_pair, y_pair, far_one, far_three = ordered(
        *parts, x_pair, y_pair, far_one, far_three
    )
    to_x, to_y, to_far, other, near_kept, near_other = parts
    back = swap_exp(other, 1)
    to_x = rounded(to_x, back[: 2 * rows])
    to_y = rounded(to_y, back[2 * rows : 4 * rows])
    to_far = rounded(to_far, back[4 * rows :])
    to_x, to_y, to_far, near_other = ordered(to_x, to_y, to_far, near_other)
    near_x, near_y, near_far = swap_exp(to_x, 2), swap_exp(to_y, 4), swap_rep(to_far, 2)
    near_back = swap_exp(near_other, 1)

    far = [pair, x_pair, y_pair, far_one, far_three]
    far = far + [swap_exp(piece, 1) for piece in far]
    to_x, to_y, to_far, *far = ordered(to_x, to_y, to_far, *far)
    groups = row_groups([[6], [7], [2, 3], [4, 5], [10, 11, 12, 13, 8, 9], [14, 15], [0, 1]], rows)
    parts = experts_of(own, far, groups, gates, ups, downs, shard_units, top)
    to_one, to_three, to_x, to_y, other, other_far, far_kept = parts
    far_kept, near_far, near_y, near_x = ordered(far_kept, near_far, near_y, near_x)
    back = swap_exp(other, 1)
    kept = added(near_kept, near_back)
    to_two = rounded(kept[:rows], near_x[:rows], near_y[:rows])
    back, to_two = ordered(back, to_two)
    from_two = swap_rep(to_two, 2)
    to_x, to_y = rounded(to_x, back[: 2 * rows]), rounded(to_y, back[2 * rows : 4 * rows])
    to_x, to_y, other_far = ordered(to_x, to_y, other_far)
    far_x, far_y = swap_exp(to_x, 2), swap_exp(to_y, 4)
    back_far = swap_exp(other_far, 1)
    to_one, to_three = rounded(to_one, back_far[:rows]), rounded(to_three, back_far[rows:])
    from_three, from_one = swap_rep(to_three, 3), swap_rep(to_one, 1)

    own_sum = kept[rows : 2 * rows] + added(near_x[rows:], near_y[rows:])
    from_one, from_three, from_two = ordered(from_one, from_three, from_two)
    to_far = rounded(kept[2 * rows :], from_one, from_three, near_far)
    from_far = swap_exp(to_far, 6)
    to_one = rounded(far_kept[:rows], back[4 * rows : 5 * rows], far_x[:rows], far_y[:rows])
    to_three = rounded(far_kept[rows:], back[5 * rows :], far_x[rows:], far_y[rows:])
    arrived = [swap_rep(to_three, 3), swap_rep(to_one, 1)]
    return rounded(own_sum, from_two, from_far, *arrived)


def solution(mesh):
    placed = (
        P(("rep", "exp"), None),
        P(("rep", "exp"), None),
        P(("rep", "exp"), None),
        P("exp", "rep", None),
        P("exp", "rep", None),
        P("exp", "rep", None),
    )
    plane = mesh.shape["exp"] == 8 and mesh.shape["rep"] == 4
    return jax.shard_map(
        on_device_dense if plane else on_device_slots,
        mesh=mesh,
        in_specs=placed,
        out_specs=P(("rep", "exp"), None),
        check_vma=False,
    )
```
